256 devices in a mesh: row: 32 (over z, x), pair: 8 (over y, core).
Axes of the slice: x: 4, y: 4, z: 8, core: 2. Of those that a mesh axis runs over, the one named last changes fastest.
Arguments:
- matrix: float32 [6144, 4096], P('row', 'pair'), may hold values from -50 to 50
- seating: int32 [16], replicated, may hold values from 0 to 15, each once
Outputs:
- rotated: float32 [6144, 4096], P('row', 'pair')
The draws below stay inside these ranges and needn't reach their ends.
All inputs are finite; a program needn't handle non-finite values.
Results may differ from the reference program's by a relative error of at most 0.0003.
Values sent between devices are 32-bit elements; how exact they have to be, the bound alone decides.
No kernel may reach another device: no remote copies, remote signals or barrier semaphores. Data moves between devices by JAX's collectives and lax.ppermute only.
A program may use at most 64 MiB of HBM per device.

```python
import jax
import jax.numpy as jnp
from jax import lax

B = 256
STEPS = 4
INNER = 4
NBLK = 16
COLS = 4096
ROWS = 6144


def draw_matrix(key, part):
    key = jax.random.fold_in(key, 11)
    first, second, third = jax.random.split(key, 3)
    base = jnp.clip(jax.random.normal(first, (ROWS, COLS), jnp.float32), -5.0, 5.0)
    row_scales = jnp.exp(jax.random.uniform(second, (ROWS, 1), jnp.float32) * jnp.log(10.0))
    column_scales = jnp.exp(jax.random.uniform(third, (1, COLS), jnp.float32) * jnp.log(10.0))
    return base * row_scales * column_scales / 10.0


def setup_inputs(seed: int = 0) -> dict:
    streams_of = jax.random.split(jax.random.key(seed), 3)
    return {
        "matrix": draw_matrix(jax.random.fold_in(streams_of[2], 71), 0),
        "seating": jax.random.permutation(streams_of[1], NBLK).astype(jnp.int32),
    }


def columns_turn(block, cosines, sines):
    left = block[:, :B]
    right = block[:, B:]
    return jnp.concatenate([cosines * left - sines * right, sines * left + cosines * right], axis=1)

def rows_turn(block, cosines, sines):
    left = block[:B]
    right = block[B:]
    return jnp.concatenate([cosines[:, None] * left - sines[:, None] * right, sines[:, None] * left + cosines[:, None] * right], axis=0)

def roll_lower(block, axis_number):
    if axis_number == 1:
        return jnp.concatenate([block[:, :B], jnp.roll(block[:, B:], -1, axis=1)], axis=1)
    return jnp.concatenate([block[:B], jnp.roll(block[B:], -1, axis=0)], axis=0)

def solve_pair(gram):
    rotation = jnp.eye(2 * B, dtype=jnp.float32)
    for sweep in range(INNER):
        whole_diag = jnp.diagonal(gram)
        upper_diag = whole_diag[:B]
        lower_diag = whole_diag[B:]
        coupling = jnp.diagonal(gram[:B, B:])
        differ = lower_diag - upper_diag
        signs = jnp.where(differ >= 0.0, 1.0, -1.0).astype(jnp.float32)
        denom = jnp.abs(differ) + jnp.sqrt(differ * differ + 4.0 * coupling * coupling + 1e-12 * (upper_diag + lower_diag) ** 2)
        tangent = 2.0 * signs * coupling / denom
        cosines = 1.0 / jnp.sqrt(1.0 + tangent * tangent)
        sines = tangent * cosines
        gram = rows_turn(columns_turn(gram, cosines, sines), cosines, sines)
        rotation = columns_turn(rotation, cosines, sines)
        gram = roll_lower(roll_lower(gram, 1), 0)
        rotation = roll_lower(rotation, 1)
    rotation = jnp.concatenate([rotation[:, :B], jnp.roll(rotation[:, B:], INNER, axis=1)], axis=1)
    return (rotation, gram)

def rotate_pair(blocks):
    joined = jnp.concatenate([blocks[0], blocks[1]], axis=1)
    gram = jnp.dot(joined.T, joined, precision=lax.Precision.HIGHEST, preferred_element_type=jnp.float32)
    rotation, turned = solve_pair(gram)
    result = jnp.dot(joined, rotation, precision=lax.Precision.HIGHEST, preferred_element_type=jnp.float32)
    return (result[:, :B], result[:, B:])

def reference(matrix, seating):
    tables = NBLK // 2
    blocks = matrix.reshape(ROWS, NBLK, B)
    seated = jnp.transpose(blocks[:, seating.astype(jnp.int32), :], (1, 0, 2))
    upper = seated[0::2]
    lower = seated[1::2]
    for step in range(STEPS):
        upper, lower = lax.map(rotate_pair, (upper, lower))
        new_upper = jnp.concatenate([upper[0:1], lower[0:1], upper[1:tables - 1]], axis=0)
        new_lower = jnp.concatenate([lower[1:], upper[tables - 1:]], axis=0)
        upper, lower = (new_upper, new_lower)
    stacked = jnp.stack([upper, lower], axis=1)
    return jnp.transpose(stacked, (2, 0, 1, 3)).reshape(ROWS, COLS)
```

```python
import jax
import jax.numpy as jnp
from jax import lax
from jax.experimental import pallas as pl
from jax.experimental.pallas import tpu as pltpu
from jax.sharding import PartitionSpec as P

B = 256
STEPS = 4
INNER = 4
BANDS = 16
TILE = 8


def ahead(block, distance):
    return pltpu.roll(block, (B - distance) % B, axis=1)


def fold(total):
    return jnp.sum(total, axis=0, keepdims=True)


def band_sums(read, height):
    names = [("uu", d) for d in range(4)] + [("ll", d) for d in range(4)]
    names += [("ul", d) for d in range(4)] + [("lu", d) for d in range(1, 4)]
    totals = {}
    for tile in range(height // TILE):
        upper, lower = read(tile)
        shifted = {"u": [upper], "l": [lower]}
        for d in range(1, 4):
            shifted["u"].append(ahead(upper, d))
            shifted["l"].append(ahead(lower, d))
        for name in names:
            kind, d = name
            term = shifted[kind[0]][0] * shifted[kind[1]][d]
            totals[name] = term if tile == 0 else totals[name] + term
    rows = [fold(totals[name]) for name in names]
    return jnp.concatenate(rows + [jnp.zeros_like(rows[0])], axis=0)


def angle(upper_diag, lower_diag, coupling):
    differ = lower_diag - upper_diag
    signs = jnp.where(differ >= 0.0, 1.0, -1.0)
    whole = upper_diag + lower_diag
    denom = jnp.abs(differ) + jnp.sqrt(
        differ * differ + 4.0 * coupling * coupling + 1e-12 * (whole * whole)
    )
    tangent = 2.0 * signs * coupling / denom
    cosines = 1.0 / jnp.sqrt(1.0 + tangent * tangent)
    return cosines, tangent * cosines


def solve_bands(gram):
    rows = [jnp.broadcast_to(gram[r : r + 1], (TILE, B)) for r in range(15)]
    uu, ll, ul, lu = rows[0:4], rows[4:8], rows[8:12], [None] + rows[12:15]
    turns = []
    for sweep in range(INNER):
        c, s = angle(uu[0], ll[0], ul[0])
        turns.append((c, s))
        reach = INNER - 1 - sweep
        if reach == 0:
            break
        new_uu, new_ll, new_ul, new_lu = [], [], [], []
        for d in range(reach + 1):
            cd = c if d == 0 else ahead(c, d)
            sd = s if d == 0 else ahead(s, d)
            cross = ul[0] if d == 0 else lu[d]
            top_u = c * uu[d] - s * cross
            top_l = c * ul[d] - s * ll[d]
            low_u = s * uu[d] + c * cross
            low_l = s * ul[d] + c * ll[d]
            new_uu.append(cd * top_u - sd * top_l)
            new_ul.append(sd * top_u + cd * top_l)
            new_lu.append(cd * low_u - sd * low_l)
            new_ll.append(sd * low_u + cd * low_l)
        uu = new_uu[:reach]
        ll = [ahead(v, 1) for v in new_ll[:reach]]
        lu = [None] + [ahead(v, 1) for v in ([new_ul[0]] + new_lu[1:])[: reach - 1]]
        ul = new_ul[1 : reach + 1]
    return turns


def turn_tile(upper, lower, turns):
    for sweep, (c, s) in enumerate(turns):
        upper, lower = c * upper - s * lower, s * upper + c * lower
        if sweep < INNER - 1:
            lower = ahead(lower, 1)
    return upper, pltpu.roll(lower, INNER - 1, axis=1)


def read_pair(upper_ref, lower_ref):
    def read(tile):
        rows = pl.ds(tile * TILE, TILE)
        return upper_ref[rows, :], lower_ref[rows, :]

    return read


def read_moved(flags_ref, keep_ref, up_ref, down_ref):
    first = flags_ref[0] == 1
    last = flags_ref[1] == 1

    def read(tile):
        rows = pl.ds(tile * TILE, TILE)
        keep = keep_ref[rows, :]
        return jnp.where(first, keep, up_ref[rows, :]), jnp.where(last, keep, down_ref[rows, :])

    return read


def spread(out_ref, sums):
    for peer in range(out_ref.shape[0]):
        out_ref[peer] = sums


def first_bands_kernel(upper_ref, lower_ref, out_ref):
    spread(out_ref, band_sums(read_pair(upper_ref, lower_ref), upper_ref.shape[0]))


def moved_bands_kernel(flags_ref, keep_ref, up_ref, down_ref, out_ref):
    spread(out_ref, band_sums(read_moved(flags_ref, keep_ref, up_ref, down_ref), keep_ref.shape[0]))


def rotate(read, flags_ref, parts_ref, keep_out, up_out, down_out):
    gram = parts_ref[0]
    for peer in range(1, parts_ref.shape[0]):
        gram = gram + parts_ref[peer]
    turns = solve_bands(gram)
    first = flags_ref[0] == 1
    for tile in range(keep_out.shape[0] // TILE):
        rows = pl.ds(tile * TILE, TILE)
        upper, lower = turn_tile(*read(tile), turns)
        keep_out[rows, :] = upper
        up_out[rows, :] = jnp.where(first, lower, upper)
        down_out[rows, :] = lower


def first_rotate_kernel(flags_ref, parts_ref, upper_ref, lower_ref, keep_out, up_out, down_out):
    rotate(read_pair(upper_ref, lower_ref), flags_ref, parts_ref, keep_out, up_out, down_out)


def moved_rotate_kernel(flags_ref, parts_ref, keep_ref, up_ref, down_ref, keep_out, up_out, down_out):
    read = read_moved(flags_ref, keep_ref, up_ref, down_ref)
    rotate(read, flags_ref, parts_ref, keep_out, up_out, down_out)


def finish_kernel(flags_ref, keep_ref, up_ref, down_ref, out_ref):
    read = read_moved(flags_ref, keep_ref, up_ref, down_ref)
    for tile in range(keep_ref.shape[0] // TILE):
        rows = pl.ds(tile * TILE, TILE)
        upper, lower = read(tile)
        out_ref[rows, :B] = upper
        out_ref[rows, B:] = lower


def seat_kernel(seating_ref, blocks_ref, out_ref):
    tables = blocks_ref.shape[0]
    for seat in range(2 * tables):
        block = seating_ref[seat]
        columns = pl.ds(pl.multiple_of((block % 2) * B, B), B)
        half = (seat % 2) * B
        out_ref[seat // 2, :, half : half + B] = blocks_ref[block // 2, :, columns]


VMEM = pl.BlockSpec(memory_space=pltpu.VMEM)
SMEM = pl.BlockSpec(memory_space=pltpu.SMEM)
PARAMS = pltpu.CompilerParams(vmem_limit_bytes=32 * 1024 * 1024)


def call(kernel, out_shape, *args, specs=None):
    if specs is None:
        specs = [VMEM] * len(args)
    outs = [VMEM] * len(out_shape) if isinstance(out_shape, list) else VMEM
    return pl.pallas_call(
        kernel, out_shape=out_shape, in_specs=specs, out_specs=outs, compiler_params=PARAMS
    )(*args)


def shape_of(*sizes):
    return jax.ShapeDtypeStruct(sizes, jnp.float32)


def local(matrix, seating):
    height = matrix.shape[0]
    peers = lax.axis_size("row")
    tables = lax.axis_size("pair")
    place = lax.axis_index("pair")
    flags = jnp.stack([place == 0, place == tables - 1]).astype(jnp.int32)
    pieces = matrix.reshape(tables, height // tables, 2 * B)
    pieces = lax.all_to_all(pieces, "pair", 0, 0, tiled=True)
    pieces = call(seat_kernel, shape_of(*pieces.shape), seating, pieces, specs=[SMEM, VMEM])
    pieces = lax.all_to_all(pieces, "pair", 0, 0, tiled=True)
    seated = pieces.reshape(height, 2 * B)
    upper, lower = seated[:, :B], seated[:, B:]
    blocks = [shape_of(height, B)] * 3
    spread_shape = shape_of(peers, BANDS, B)
    forward = [(j, j + 1) for j in range(tables - 1)]
    backward = [(j + 1, j) for j in range(tables - 1)]
    for step in range(STEPS):
        if step == 0:
            sums = call(first_bands_kernel, spread_shape, upper, lower)
        else:
            sums = call(
                moved_bands_kernel, spread_shape, flags, keep, up, down, specs=[SMEM] + [VMEM] * 3
            )
        parts = lax.all_to_all(sums, "row", 0, 0, tiled=True)
        if step == 0:
            keep, up, down = call(
                first_rotate_kernel, blocks, flags, parts, upper, lower, specs=[SMEM] + [VMEM] * 3
            )
        else:
            keep, up, down = call(
                moved_rotate_kernel, blocks, flags, parts, keep, up, down, specs=[SMEM] + [VMEM] * 4
            )
        up = lax.ppermute(up, "pair", forward)
        down = lax.ppermute(down, "pair", backward)
    return call(
        finish_kernel, shape_of(height, 2 * B), flags, keep, up, down, specs=[SMEM] + [VMEM] * 3
    )


def solution(mesh):
    in_specs = (P("row", "pair"), P())
    out_specs = P("row", "pair")
    return jax.shard_map(local, mesh=mesh, in_specs=in_specs, out_specs=out_specs, check_vma=False)
```

```python
import functools

import jax
import jax.numpy as jnp
from jax import lax
from jax.experimental import pallas as pl
from jax.experimental.pallas import tpu as pltpu
from jax.sharding import PartitionSpec as P

B = 256
STEPS = 4
INNER = 4
BANDS = 16
TILE = 8


def ahead(block, distance):
    return pltpu.roll(block, (B - distance) % B, axis=1)


def table_of(device, step):
    return device if step % 2 == 0 else device ^ 1


def ring_route(tables, step):
    ring = [0] + list(range(1, tables, 2)) + list(range(tables - 2, 0, -2))
    hosts = [table_of(table, step) for table in ring]
    return list(zip(hosts, hosts[1:] + hosts[:1]))


def sends_upper(facts_ref, step):
    table = table_of(facts_ref[0], step)
    return (table == 0) | (table % 2 == 1)


def receives_upper(facts_ref, step):
    return table_of(facts_ref[0], step) % 2 == 0


def fold(total):
    return jnp.sum(total, axis=0, keepdims=True)


def band_sums(read, height):
    names = [("uu", d) for d in range(4)] + [("ll", d) for d in range(4)]
    names += [("ul", d) for d in range(4)] + [("lu", d) for d in range(1, 4)]
    totals = {}
    for tile in range(height // TILE):
        upper, lower = read(tile)
        shifted = {"u": [upper], "l": [lower]}
        for d in range(1, 4):
            shifted["u"].append(ahead(upper, d))
            shifted["l"].append(ahead(lower, d))
        for name in names:
            kind, d = name
            term = shifted[kind[0]][0] * shifted[kind[1]][d]
            totals[name] = term if tile == 0 else totals[name] + term
    rows = [fold(totals[name]) for name in names]
    return jnp.concatenate(rows + [jnp.zeros_like(rows[0])], axis=0)


def angle(upper_diag, lower_diag, coupling):
    differ = lower_diag - upper_diag
    signs = jnp.where(differ >= 0.0, 1.0, -1.0)
    whole = upper_diag + lower_diag
    denom = jnp.abs(differ) + jnp.sqrt(
        differ * differ + 4.0 * coupling * coupling + 1e-12 * (whole * whole)
    )
    tangent = 2.0 * signs * coupling / denom
    cosines = 1.0 / jnp.sqrt(1.0 + tangent * tangent)
    return cosines, tangent * cosines


def solve_bands(gram):
    rows = [jnp.broadcast_to(gram[r : r + 1], (TILE, B)) for r in range(15)]
    uu, ll, ul, lu = rows[0:4], rows[4:8], rows[8:12], [None] + rows[12:15]
    turns = []
    for sweep in range(INNER):
        c, s = angle(uu[0], ll[0], ul[0])
        turns.append((c, s))
        reach = INNER - 1 - sweep
        if reach == 0:
            break
        new_uu, new_ll, new_ul, new_lu = [], [], [], []
        for d in range(reach + 1):
            cd = c if d == 0 else ahead(c, d)
            sd = s if d == 0 else ahead(s, d)
            cross = ul[0] if d == 0 else lu[d]
            top_u = c * uu[d] - s * cross
            top_l = c * ul[d] - s * ll[d]
            low_u = s * uu[d] + c * cross
            low_l = s * ul[d] + c * ll[d]
            new_uu.append(cd * top_u - sd * top_l)
            new_ul.append(sd * top_u + cd * top_l)
            new_lu.append(cd * low_u - sd * low_l)
            new_ll.append(sd * low_u + cd * low_l)
        uu = new_uu[:reach]
        ll = [ahead(v, 1) for v in new_ll[:reach]]
        lu = [None] + [ahead(v, 1) for v in ([new_ul[0]] + new_lu[1:])[: reach - 1]]
        ul = new_ul[1 : reach + 1]
    return turns


def turn_tile(upper, lower, turns):
    for sweep, (c, s) in enumerate(turns):
        upper, lower = c * upper - s * lower, s * upper + c * lower
        if sweep < INNER - 1:
            lower = ahead(lower, 1)
    return upper, pltpu.roll(lower, INNER - 1, axis=1)


def read_pair(upper_ref, lower_ref):
    def read(tile):
        rows = pl.ds(tile * TILE, TILE)
        return upper_ref[rows, :], lower_ref[rows, :]

    return read


def read_moved(receives_upper, keep_ref, come_ref):
    def read(tile):
        rows = pl.ds(tile * TILE, TILE)
        keep, come = keep_ref[rows, :], come_ref[rows, :]
        return jnp.where(receives_upper, come, keep), jnp.where(receives_upper, keep, come)

    return read


def spread(out_ref, sums):
    for peer in range(out_ref.shape[0]):
        out_ref[peer] = sums


def first_bands_kernel(upper_ref, lower_ref, out_ref):
    spread(out_ref, band_sums(read_pair(upper_ref, lower_ref), upper_ref.shape[0]))


def moved_bands_kernel(step, facts_ref, keep_ref, come_ref, out_ref):
    read = read_moved(receives_upper(facts_ref, step), keep_ref, come_ref)
    spread(out_ref, band_sums(read, keep_ref.shape[0]))


def rotate(read, sends_upper, parts_ref, keep_out, send_out):
    gram = parts_ref[0]
    for peer in range(1, parts_ref.shape[0]):
        gram = gram + parts_ref[peer]
    turns = solve_bands(gram)
    for tile in range(keep_out.shape[0] // TILE):
        rows = pl.ds(tile * TILE, TILE)
        upper, lower = turn_tile(*read(tile), turns)
        keep_out[rows, :] = jnp.where(sends_upper, lower, upper)
        send_out[rows, :] = jnp.where(sends_upper, upper, lower)


def first_rotate_kernel(facts_ref, parts_ref, upper_ref, lower_ref, keep_out, send_out):
    read = read_pair(upper_ref, lower_ref)
    rotate(read, sends_upper(facts_ref, 0), parts_ref, keep_out, send_out)


def moved_rotate_kernel(step, facts_ref, parts_ref, keep_ref, come_ref, keep_out, send_out):
    read = read_moved(receives_upper(facts_ref, step), keep_ref, come_ref)
    rotate(read, sends_upper(facts_ref, step), parts_ref, keep_out, send_out)


def finish_kernel(facts_ref, keep_ref, come_ref, out_ref):
    read = read_moved(receives_upper(facts_ref, STEPS), keep_ref, come_ref)
    for tile in range(keep_ref.shape[0] // TILE):
        rows = pl.ds(tile * TILE, TILE)
        upper, lower = read(tile)
        out_ref[rows, :B] = upper
        out_ref[rows, B:] = lower


def seat_kernel(facts_ref, blocks_ref, out_ref):
    tables = blocks_ref.shape[0]
    for seat in range(2 * tables):
        block = facts_ref[1 + seat]
        columns = pl.ds(pl.multiple_of((block % 2) * B, B), B)
        half = (seat % 2) * B
        out_ref[seat // 2, :, half : half + B] = blocks_ref[block // 2, :, columns]


VMEM = pl.BlockSpec(memory_space=pltpu.VMEM)
SMEM = pl.BlockSpec(memory_space=pltpu.SMEM)
PARAMS = pltpu.CompilerParams(vmem_limit_bytes=32 * 1024 * 1024)


def call(kernel, out_shape, *args, specs=None):
    if specs is None:
        specs = [VMEM] * len(args)
    outs = [VMEM] * len(out_shape) if isinstance(out_shape, list) else VMEM
    return pl.pallas_call(
        kernel, out_shape=out_shape, in_specs=specs, out_specs=outs, compiler_params=PARAMS
    )(*args)


def shape_of(*sizes):
    return jax.ShapeDtypeStruct(sizes, jnp.float32)


def local(matrix, seating):
    height = matrix.shape[0]
    peers = lax.axis_size("row")
    tables = lax.axis_size("pair")
    place = lax.axis_index("pair")
    facts = jnp.concatenate([place[None].astype(jnp.int32), seating])
    pieces = matrix.reshape(tables, height // tables, 2 * B)
    pieces = lax.all_to_all(pieces, "pair", 0, 0, tiled=True)
    pieces = call(seat_kernel, shape_of(*pieces.shape), facts, pieces, specs=[SMEM, VMEM])
    pieces = lax.all_to_all(pieces, "pair", 0, 0, tiled=True)
    seated = pieces.reshape(height, 2 * B)
    upper, lower = seated[:, :B], seated[:, B:]
    blocks = [shape_of(height, B)] * 2
    spread_shape = shape_of(peers, BANDS, B)
    for step in range(STEPS):
        if step == 0:
            sums = call(first_bands_kernel, spread_shape, upper, lower)
        else:
            kernel = functools.partial(moved_bands_kernel, step)
            sums = call(kernel, spread_shape, facts, keep, come, specs=[SMEM] + [VMEM] * 2)
        parts = lax.all_to_all(sums, "row", 0, 0, tiled=True)
        if step == 0:
            kernel, pair = first_rotate_kernel, (upper, lower)
        else:
            kernel, pair = functools.partial(moved_rotate_kernel, step), (keep, come)
        keep, send = call(kernel, blocks, facts, parts, *pair, specs=[SMEM] + [VMEM] * 3)
        come = lax.ppermute(send, "pair", ring_route(tables, step))
    return call(
        finish_kernel, shape_of(height, 2 * B), facts, keep, come, specs=[SMEM] + [VMEM] * 2
    )


def solution(mesh):
    in_specs = (P("row", "pair"), P())
    out_specs = P("row", "pair")
    return jax.shard_map(local, mesh=mesh, in_specs=in_specs, out_specs=out_specs, check_vma=False)
```

```python
import jax
import jax.numpy as jnp
from jax import lax
from jax.experimental import pallas as pl
from jax.experimental.pallas import tpu as pltpu
from jax.sharding import PartitionSpec as P

B = 256
STEPS = 4
INNER = 4
TILE = 8
REACH = 2 * (INNER - 1)
LAG = INNER - 1
GROUP = 4
CHUNK = 4
GROUPS = 32


def ahead(block, distance):
    distance = distance % B
    return block if distance == 0 else pltpu.roll(block, B - distance, axis=1)


def ring_of(tables):
    return [0] + list(range(1, tables, 2)) + list(range(tables - 2, 0, -2))


def sends_upper(table):
    return (table == 0) | (table % 2 == 1)


def ring_before(place, tables):
    last = tables - 1
    odd = jnp.where(place == 1, 0, place - 2)
    even = jnp.where(place == last - 1, last, place + 2)
    return jnp.where(place % 2 == 1, odd, even)


def angle(upper_diag, lower_diag, coupling):
    differ = lower_diag - upper_diag
    signs = jnp.where(differ >= 0.0, 1.0, -1.0)
    whole = upper_diag + lower_diag
    denom = jnp.abs(differ) + jnp.sqrt(
        differ * differ + 4.0 * coupling * coupling + 1e-12 * (whole * whole)
    )
    tangent = 2.0 * signs * coupling / denom
    cosines = 1.0 / jnp.sqrt(1.0 + tangent * tangent)
    return cosines, tangent * cosines


def turn_both(uu, ul, lu, ll, left, right):
    (c, s), (cd, sd) = left, right
    top_u = c * uu - s * lu
    top_l = c * ul - s * ll
    low_u = s * uu + c * lu
    low_l = s * ul + c * ll
    return (
        cd * top_u - sd * top_l,
        sd * top_u + cd * top_l,
        cd * low_u - sd * low_l,
        sd * low_u + cd * low_l,
    )


def solve_bands(uu, ll, ul, lu, reach):
    turns = []
    for sweep in range(INNER):
        c, s = angle(uu[0], ll[0], ul[0])
        turns.append((c, s))
        if reach == 0:
            break
        new_uu, new_ll, new_ul, new_lu = [], [], [], []
        for d in range(reach + 1):
            cross = ul[0] if d == 0 else lu[d]
            done = turn_both(uu[d], ul[d], cross, ll[d], (c, s), (ahead(c, d), ahead(s, d)))
            for total, value in zip((new_uu, new_ul, new_lu, new_ll), done):
                total.append(value)
        if sweep == INNER - 1:
            uu, ll = new_uu, new_ll
            break
        uu = new_uu[:reach]
        ll = [ahead(v, 1) for v in new_ll[:reach]]
        lu = [None] + [ahead(v, 1) for v in ([new_ul[0]] + new_lu[1:])[: reach - 1]]
        ul = new_ul[1 : reach + 1]
        reach = reach - 1
    return turns, uu, ll


def cross_bands(uu, ul, lu, ll, left_turns, right_turns, left_lower, right_upper):
    reach = REACH
    for sweep in range(INNER - 1):
        c, s = right_turns[sweep]
        done = {}
        for e in range(-reach, reach + 1):
            right = (ahead(c, e), ahead(s, e))
            done[e] = turn_both(uu[e], ul[e], lu[e], ll[e], left_turns[sweep], right)
        reach = reach - 1
        inner = range(-reach, reach + 1)
        uu = {e: done[e][0] for e in inner}
        ul = {e: done[e + 1][1] for e in inner}
        lu = {e: ahead(done[e - 1][2], 1) for e in inner}
        ll = {e: ahead(done[e][3], 1) for e in inner}
    c, s = left_turns[-1]
    from_u, from_l = jnp.where(left_lower, s, c), jnp.where(left_lower, c, -s)
    c, s = right_turns[-1]
    to_u, to_l = jnp.where(right_upper, c, s), jnp.where(right_upper, -s, c)
    out = {}
    for e in range(-reach, reach + 1):
        half_u = from_u * uu[e] + from_l * lu[e]
        half_l = from_u * ul[e] + from_l * ll[e]
        out[e] = ahead(to_u, e) * half_u + ahead(to_l, e) * half_l
    return out


def turn_tile(upper, lower, turns):
    for sweep, (c, s) in enumerate(turns):
        upper, lower = c * upper - s * lower, s * upper + c * lower
        if sweep < INNER - 1:
            lower = ahead(lower, 1)
    return upper, lower


def sides(place, tables):
    return place == 0, place == tables - 2


def line_up(own, before, place, tables):
    own_right = place % 2 == 1
    left_lower, right_upper = sides(place, tables)
    left = [jnp.where(own_right, b, a) for a, b in zip(own, before)]
    right = [jnp.where(own_right, a, b) for a, b in zip(own, before)]
    left = [jnp.where(left_lower, ahead(v, -LAG), v) for v in left]
    right = [jnp.where(right_upper, v, ahead(v, -LAG)) for v in right]
    return left + right


def band_terms(now, then, d):
    lu, ll, ru, rl = now
    lu_d, ll_d, ru_d, rl_d = then
    same = [lu * lu_d, ru * ru_d, ll * ll_d, rl * rl_d, lu * ll_d, ru * rl_d]
    turned = [ll * lu_d, rl * ru_d]
    over = [lu * ru_d, lu * rl_d, ll * ru_d, ll * rl_d]
    back = [ru * lu_d, ru * ll_d, rl * lu_d, rl * ll_d]
    return same + over if d == 0 else same + turned + over + back


def band_rows(d):
    return list(range(6)) + list(range(8, 12)) if d == 0 else list(range(16))


def band_sums(lined_ref, out_ref):
    height = lined_ref.shape[1]
    out_ref[...] = jnp.zeros_like(out_ref)
    step_rows = GROUP * TILE
    for d in range(REACH + 1):
        slots = band_rows(d)

        def body(index, totals):
            start = pl.multiple_of(index * step_rows, step_rows)
            for part in range(GROUP):
                rows = pl.ds(start + part * TILE, TILE)
                now = [lined_ref[block, rows, :] for block in range(4)]
                terms = band_terms(now, [ahead(v, d) for v in now], d)
                totals = [total + term for total, term in zip(totals, terms)]
            return totals

        start = [jnp.zeros((TILE, B), jnp.float32)] * len(slots)
        totals = lax.fori_loop(0, height // step_rows, body, start)
        for slot, total in zip(slots, totals):
            row = jnp.sum(total, axis=0, keepdims=True)
            peer, place = d * (16 // CHUNK) + slot // CHUNK, slot % CHUNK
            out_ref[peer, place : place + 1, :] = row[:, : B // 2]
            out_ref[peer, CHUNK + place : CHUNK + place + 1, :] = row[:, B // 2 :]


def seated_bands_kernel(tables, facts_ref, blocks_ref, lined_ref, out_ref):
    place = facts_ref[0]
    for tile in range(blocks_ref.shape[0] // TILE):
        rows = pl.ds(tile * TILE, TILE)
        blocks = [blocks_ref[rows, n * B : (n + 1) * B] for n in range(4)]
        for n, value in enumerate(line_up(blocks[:2], blocks[2:], place, tables)):
            lined_ref[n, rows, :] = value
    band_sums(lined_ref, out_ref)


def moved_bands_kernel(tables, facts_ref, keep_ref, send_ref, come_ref, next_ref, lined_ref, out_ref):
    place, before = facts_ref[0], facts_ref[1]
    upper_comes = place % 2 == 0
    upper_sent = before % 2 == 0
    for tile in range(keep_ref.shape[0] // TILE):
        rows = pl.ds(tile * TILE, TILE)
        keep, send, come, near = (r[rows, :] for r in (keep_ref, send_ref, come_ref, next_ref))
        own = [jnp.where(upper_comes, come, keep), jnp.where(upper_comes, keep, come)]
        other = [jnp.where(upper_sent, send, near), jnp.where(upper_sent, near, send)]
        for n, value in enumerate(line_up(own, other, place, tables)):
            lined_ref[n, rows, :] = value
    band_sums(lined_ref, out_ref)


def total_kernel(peers, parts_ref, out_ref):
    share = parts_ref.shape[0] // peers
    for part in range(share):
        total = parts_ref[part]
        for peer in range(1, peers):
            total = total + parts_ref[peer * share + part]
        for peer in range(peers):
            out_ref[peer * share + part] = total


def rotate_kernel(tables, facts_ref, sums_ref, lined_ref, keep_out, send_out):
    place = facts_ref[0]
    left_lower, right_upper = sides(place, tables)

    def row(d, slot):
        peer, at = d * (16 // CHUNK) + slot // CHUNK, slot % CHUNK
        tile = sums_ref[peer]
        return jnp.concatenate([tile[at : at + 1], tile[CHUNK + at : CHUNK + at + 1]], axis=1)

    def wide(d, slot):
        return jnp.broadcast_to(row(d, slot), (TILE, B))

    is_left = lax.broadcasted_iota(jnp.int32, (TILE, B), 0) < TILE // 2

    def both(d, slot):
        return jnp.where(is_left, wide(d, slot), wide(d, slot + 1))

    span = range(REACH + 1)
    uu, ll, ul = ([both(d, slot) for d in span] for slot in (0, 2, 4))
    lu = [None] + [both(d, 6) for d in span if d > 0]
    turns, uu, ll = solve_bands(uu, ll, ul, lu, REACH)

    def spread(value, at):
        return jnp.broadcast_to(value[at : at + 1], (TILE, B))

    left_turns = [(spread(c, 0), spread(s, 0)) for c, s in turns]
    right_turns = [(spread(c, TILE // 2), spread(s, TILE // 2)) for c, s in turns]
    cross = []
    for slot, back in ((8, 12), (9, 14), (10, 13), (11, 15)):
        bands = {d: wide(d, slot) for d in span}
        bands.update({-d: ahead(wide(d, back), -d) for d in span if d > 0})
        cross.append(bands)
    cross = cross_bands(*cross, left_turns, right_turns, left_lower, right_upper)
    span = range(INNER)
    new_uu = [jnp.where(left_lower, spread(ll[d], 0), spread(uu[d], 0)) for d in span]
    half = TILE // 2
    new_ll = [jnp.where(right_upper, spread(uu[d], half), spread(ll[d], half)) for d in span]
    new_ul = [cross[d] for d in span]
    new_lu = [None] + [ahead(cross[-d], d) for d in span if d > 0]
    last_turns, _, _ = solve_bands(new_uu, new_ll, new_ul, new_lu, INNER - 1)
    upper_sent = sends_upper(place ^ 1)
    for tile in range(keep_out.shape[0] // TILE):
        rows = pl.ds(tile * TILE, TILE)
        left = turn_tile(lined_ref[0, rows, :], lined_ref[1, rows, :], left_turns)
        right = turn_tile(lined_ref[2, rows, :], lined_ref[3, rows, :], right_turns)
        upper = jnp.where(left_lower, left[1], left[0])
        lower = jnp.where(right_upper, right[0], right[1])
        upper, lower = turn_tile(upper, lower, last_turns)
        lower = ahead(lower, -LAG)
        keep_out[rows, :] = jnp.where(upper_sent, lower, upper)
        send_out[rows, :] = jnp.where(upper_sent, upper, lower)


def finish_kernel(facts_ref, keep_ref, come_ref, out_ref):
    upper_comes = facts_ref[0] % 2 == 0
    for tile in range(keep_ref.shape[0] // TILE):
        rows = pl.ds(tile * TILE, TILE)
        keep, come = keep_ref[rows, :], come_ref[rows, :]
        out_ref[rows, :B] = jnp.where(upper_comes, come, keep)
        out_ref[rows, B:] = jnp.where(upper_comes, keep, come)


def seat_kernel(facts_ref, blocks_ref, out_ref):
    tables = blocks_ref.shape[0]
    ring = ring_of(tables)
    for table in range(tables):
        before = ring[ring.index(table) - 1]
        for n, seat in enumerate((2 * table, 2 * table + 1, 2 * before, 2 * before + 1)):
            block = facts_ref[2 + seat]
            columns = pl.ds(pl.multiple_of((block % 2) * B, B), B)
            out_ref[table, :, n * B : (n + 1) * B] = blocks_ref[block // 2, :, columns]


VMEM = pl.BlockSpec(memory_space=pltpu.VMEM)
SMEM = pl.BlockSpec(memory_space=pltpu.SMEM)
PARAMS = pltpu.CompilerParams(vmem_limit_bytes=32 * 1024 * 1024)


def call(kernel, out_shape, *args):
    specs = [SMEM if a.dtype == jnp.int32 else VMEM for a in args]
    outs = [VMEM] * len(out_shape) if isinstance(out_shape, list) else VMEM
    return pl.pallas_call(
        kernel, out_shape=out_shape, in_specs=specs, out_specs=outs, compiler_params=PARAMS
    )(*args)


def shape_of(*sizes):
    return jax.ShapeDtypeStruct(sizes, jnp.float32)


def bind(kernel, size):
    def bound(*refs):
        return kernel(size, *refs)

    return bound


def local(matrix, seating):
    height = matrix.shape[0]
    peers = lax.axis_size("row")
    tables = lax.axis_size("pair")
    place = lax.axis_index("pair").astype(jnp.int32)
    before = ring_before(place, tables).astype(jnp.int32)
    facts = jnp.concatenate([place[None], before[None], seating])
    ring = ring_of(tables)
    hosts = [table ^ 1 for table in ring]
    forward = list(zip(hosts, hosts[1:] + hosts[:1]))
    backward = [(b, a) for a, b in forward]
    pieces = matrix.reshape(tables, height // tables, 2 * B)
    pieces = lax.all_to_all(pieces, "pair", 0, 0, tiled=True)
    pieces = call(seat_kernel, shape_of(tables, height // tables, 4 * B), facts, pieces)
    pieces = lax.all_to_all(pieces, "pair", 0, 0, tiled=True)
    held = [pieces.reshape(height, 4 * B)]
    lined_shape = shape_of(4, height, B)
    spread_shape = shape_of(GROUPS, TILE, B // 2)
    block_shape = shape_of(height, B)
    for pair_of_steps in range(STEPS // 2):
        kernel = bind(moved_bands_kernel if pair_of_steps else seated_bands_kernel, tables)
        lined, sums = call(kernel, [lined_shape, spread_shape], facts, *held)
        sums = lax.all_to_all(sums, "row", 0, 0, tiled=True)
        sums = call(bind(total_kernel, peers), spread_shape, sums)
        sums = lax.all_to_all(sums, "row", 0, 0, tiled=True)
        kernel = bind(rotate_kernel, tables)
        keep, send = call(kernel, [block_shape, block_shape], facts, sums, lined)
        come = lax.ppermute(send, "pair", forward)
        if pair_of_steps < STEPS // 2 - 1:
            held = [keep, send, come, lax.ppermute(keep, "pair", backward)]
    return call(finish_kernel, shape_of(height, 2 * B), facts, keep, come)


def solution(mesh):
    in_specs = (P("row", "pair"), P())
    out_specs = P("row", "pair")
    return jax.shard_map(local, mesh=mesh, in_specs=in_specs, out_specs=out_specs, check_vma=False)
```

```python
import jax
import jax.numpy as jnp
from jax import lax
from jax.experimental import pallas as pl
from jax.experimental.pallas import tpu as pltpu
from jax.sharding import PartitionSpec as P

B = 256
STEPS = 4
INNER = 4
TILE = 8
REACH = 2 * (INNER - 1)
LAG = INNER - 1
GROUP = 24
GROUPS = 32


def ahead(block, distance):
    distance = distance % B
    return block if distance == 0 else pltpu.roll(block, B - distance, axis=1)


def ring_of(tables):
    return [0] + list(range(1, tables, 2)) + list(range(tables - 2, 0, -2))


def sends_upper(table):
    return (table == 0) | (table % 2 == 1)


def ring_before(place, tables):
    last = tables - 1
    odd = jnp.where(place == 1, 0, place - 2)
    even = jnp.where(place == last - 1, last, place + 2)
    return jnp.where(place % 2 == 1, odd, even)


def angle(upper_diag, lower_diag, coupling):
    differ = lower_diag - upper_diag
    signs = jnp.where(differ >= 0.0, 1.0, -1.0)
    whole = upper_diag + lower_diag
    denom = jnp.abs(differ) + jnp.sqrt(
        differ * differ + 4.0 * coupling * coupling + 1e-12 * (whole * whole)
    )
    tangent = 2.0 * signs * coupling / denom
    square = 1.0 + tangent * tangent
    guess = lax.rsqrt(square)
    cosines = guess * (1.5 - 0.5 * square * (guess * guess))
    return cosines, tangent * cosines


def turn_both(bands, left, right):
    (c, s), (cd, sd) = left, right
    uu, ul, lu, ll = bands
    top_u = c * uu - s * lu
    top_l = c * ul - s * ll
    low_u = s * uu + c * lu
    low_l = s * ul + c * ll
    return [
        cd * top_u - sd * top_l,
        sd * top_u + cd * top_l,
        cd * low_u - sd * low_l,
        sd * low_u + cd * low_l,
    ]


def spread(value):
    return jnp.broadcast_to(value[:1], (TILE, B))


def behind(value):
    return pltpu.roll(value, 0, axis=1, stride=1, stride_axis=0)


def solve(pairs):
    count = 1 if len(pairs) == 1 else 2
    reach_rows = lax.broadcasted_iota(jnp.int32, (TILE, B), 0) == 0
    turns = [[] for _ in range(count)]
    for sweep in range(INNER):
        wide = []
        for table in range(count):
            uu, ul, _, ll = pairs[table, table]
            c, s = (spread(v) for v in angle(uu, ll, ul))
            turns[table].append((c, s))
            wide.append((behind(c), behind(s)))
        if sweep == INNER - 1 and count == 1:
            break
        pairs = {
            (a, b): turn_both(bands, turns[a][-1], wide[b]) for (a, b), bands in pairs.items()
        }
        if sweep == INNER - 1:
            break
        for key, (uu, ul, lu, ll) in pairs.items():
            ul = pltpu.roll(ul, 1, axis=0)
            lu = ahead(pltpu.roll(lu, TILE - 1, axis=0), 1)
            pairs[key] = [uu, ul, lu, ahead(ll, 1)]
        for a, b in pairs:
            pairs[a, b][1] = jnp.where(reach_rows, pairs[b, a][2], pairs[a, b][1])
    return turns, pairs


def turn_tiles(uppers, lowers, turns):
    for sweep, (c, s) in enumerate(turns):
        pairs = list(zip(uppers, lowers))
        uppers = [c * u - s * v for u, v in pairs]
        lowers = [s * u + c * v for u, v in pairs]
        if sweep < INNER - 1:
            lowers = [ahead(v, 1) for v in lowers]
    return uppers, lowers


def mix_tiles(uppers, lowers, turns, lower_wanted):
    uppers, lowers = turn_tiles(uppers, lowers, turns[:-1])
    c, s = turns[-1]
    from_u, from_l = jnp.where(lower_wanted, s, c), jnp.where(lower_wanted, c, -s)
    return [from_u * u + from_l * v for u, v in zip(uppers, lowers)]


def sides(place, tables):
    return place == 0, place == tables - 2


def line_up(own, before, place, tables):
    own_right = place % 2 == 1
    left_lower, right_upper = sides(place, tables)
    left = [jnp.where(own_right, b, a) for a, b in zip(own, before)]
    right = [jnp.where(own_right, a, b) for a, b in zip(own, before)]
    left = [jnp.where(left_lower, ahead(v, -LAG), v) for v in left]
    right = [jnp.where(right_upper, v, ahead(v, -LAG)) for v in right]
    return left + right


def band_sums(lined_ref, out_ref):
    height = lined_ref.shape[0]
    out_ref[...] = jnp.zeros_like(out_ref)
    slots = [(x, y) for x in range(4) for y in range(4)]
    for d in range(REACH + 1):
        kept = [(x, y) for x, y in slots if d or x <= y]

        totals = None
        for tile in range(height // TILE):
            now = [lined_ref[tile * TILE : (tile + 1) * TILE, n * B : (n + 1) * B] for n in range(4)]
            then = [ahead(v, -d) for v in now]
            terms = [now[x] * then[y] for x, y in kept]
            totals = terms if totals is None else [a + b for a, b in zip(totals, terms)]
        for (x, y), total in zip(kept, totals):
            row = jnp.sum(total, axis=0, keepdims=True)
            for slot in {4 * x + y, 4 * y + x} if d == 0 else {4 * x + y}:
                out_ref[2 * slot, d : d + 1, :] = row[:, : B // 2]
                out_ref[2 * slot + 1, d : d + 1, :] = row[:, B // 2 :]


def moved_bands_kernel(tables, facts_ref, keep_ref, send_ref, come_ref, next_ref, lined_ref, out_ref):
    place, before = facts_ref[0], facts_ref[1]
    upper_comes = place % 2 == 0
    upper_sent = before % 2 == 0
    for tile in range(keep_ref.shape[0] // TILE):
        rows = pl.ds(tile * TILE, TILE)
        keep, send, come, near = (r[rows, :] for r in (keep_ref, send_ref, come_ref, next_ref))
        own = [jnp.where(upper_comes, come, keep), jnp.where(upper_comes, keep, come)]
        other = [jnp.where(upper_sent, send, near), jnp.where(upper_sent, near, send)]
        for n, value in enumerate(line_up(own, other, place, tables)):
            lined_ref[rows, n * B : (n + 1) * B] = value
    band_sums(lined_ref, out_ref)


def total_kernel(peers, parts_ref, out_ref):
    share = parts_ref.shape[0] // peers
    for part in range(share):
        total = parts_ref[part]
        for peer in range(1, peers):
            total = total + parts_ref[peer * share + part]
        for peer in range(peers):
            out_ref[peer * share + part] = total


def rotate_kernel(tables, facts_ref, sums_ref, lined_ref, keep_out, send_out):
    place = facts_ref[0]
    left_lower, right_upper = sides(place, tables)

    def bands(x, y):
        slot = 4 * x + y
        return jnp.concatenate([sums_ref[2 * slot], sums_ref[2 * slot + 1]], axis=1)

    pairs = {
        (a, b): [bands(2 * a + x, 2 * b + y) for x in range(2) for y in range(2)]
        for a in range(2)
        for b in range(2)
    }
    (left_turns, right_turns), pairs = solve(pairs)
    uu, _, _, ll = pairs[0, 0]
    new_uu = jnp.where(left_lower, ll, uu)
    uu, _, _, ll = pairs[1, 1]
    new_ll = jnp.where(right_upper, uu, ll)
    uu, ul, lu, ll = pairs[0, 1]
    new_ul = jnp.where(
        left_lower, jnp.where(right_upper, lu, ll), jnp.where(right_upper, uu, ul)
    )
    uu, ul, lu, ll = pairs[1, 0]
    new_lu = jnp.where(
        left_lower, jnp.where(right_upper, ul, ll), jnp.where(right_upper, uu, lu)
    )
    (last_turns,), _ = solve({(0, 0): [new_uu, new_ul, new_lu, new_ll]})
    upper_sent = sends_upper(place ^ 1)
    height = keep_out.shape[0]
    groups = [
        [slice(r, r + TILE) for r in range(start, min(start + GROUP * TILE, height), TILE)]
        for start in range(0, height, GROUP * TILE)
    ]
    for n, out_ref, turns, lower_wanted in (
        (0, keep_out, left_turns, left_lower),
        (2, send_out, right_turns, jnp.logical_not(right_upper)),
    ):
        for group in groups:
            uppers = [lined_ref[rows, n * B : (n + 1) * B] for rows in group]
            lowers = [lined_ref[rows, (n + 1) * B : (n + 2) * B] for rows in group]
            for rows, value in zip(group, mix_tiles(uppers, lowers, turns, lower_wanted)):
                out_ref[rows, :] = value
    for group in groups:
        uppers = [keep_out[rows, :] for rows in group]
        lowers = [send_out[rows, :] for rows in group]
        uppers, lowers = turn_tiles(uppers, lowers, last_turns)
        for rows, upper, lower in zip(group, uppers, lowers):
            lower = ahead(lower, -LAG)
            keep_out[rows, :] = jnp.where(upper_sent, lower, upper)
            send_out[rows, :] = jnp.where(upper_sent, upper, lower)


def finish_kernel(facts_ref, keep_ref, come_ref, out_ref):
    upper_comes = facts_ref[0] % 2 == 0
    for tile in range(keep_ref.shape[0] // TILE):
        rows = pl.ds(tile * TILE, TILE)
        keep, come = keep_ref[rows, :], come_ref[rows, :]
        out_ref[rows, :B] = jnp.where(upper_comes, come, keep)
        out_ref[rows, B:] = jnp.where(upper_comes, keep, come)


def seat_kernel(facts_ref, blocks_ref, out_ref):
    tables = blocks_ref.shape[0]
    ring = ring_of(tables)
    for table in range(tables):
        before = ring[ring.index(table) - 1]
        left, right = (before, table) if table % 2 else (table, before)
        left_lower, right_upper = sides(table, tables)
        for n, seat in enumerate((2 * left, 2 * left + 1, 2 * right, 2 * right + 1)):
            block = facts_ref[2 + seat]
            columns = pl.ds(pl.multiple_of((block % 2) * B, B), B)
            late = left_lower if n < 2 else not right_upper
            for tile in range(blocks_ref.shape[1] // TILE):
                rows = slice(tile * TILE, (tile + 1) * TILE)
                value = blocks_ref[block // 2, rows, columns]
                out_ref[table, rows, n * B : (n + 1) * B] = ahead(value, -LAG) if late else value


VMEM = pl.BlockSpec(memory_space=pltpu.VMEM)
SMEM = pl.BlockSpec(memory_space=pltpu.SMEM)
PARAMS = pltpu.CompilerParams(vmem_limit_bytes=32 * 1024 * 1024)


def call(kernel, out_shape, *args):
    specs = [SMEM if a.dtype == jnp.int32 else VMEM for a in args]
    outs = [VMEM] * len(out_shape) if isinstance(out_shape, list) else VMEM
    return pl.pallas_call(
        kernel, out_shape=out_shape, in_specs=specs, out_specs=outs, compiler_params=PARAMS
    )(*args)


def shape_of(*sizes):
    return jax.ShapeDtypeStruct(sizes, jnp.float32)


def bind(kernel, size):
    def bound(*refs):
        return kernel(size, *refs)

    return bound


def local(matrix, seating):
    height = matrix.shape[0]
    peers = lax.axis_size("row")
    tables = lax.axis_size("pair")
    place = lax.axis_index("pair").astype(jnp.int32)
    before = ring_before(place, tables).astype(jnp.int32)
    facts = jnp.concatenate([place[None], before[None], seating])
    ring = ring_of(tables)
    hosts = [table ^ 1 for table in ring]
    forward = list(zip(hosts, hosts[1:] + hosts[:1]))
    backward = [(b, a) for a, b in forward]
    pieces = matrix.reshape(tables, height // tables, 2 * B)
    pieces = lax.all_to_all(pieces, "pair", 0, 0, tiled=True)
    pieces = call(seat_kernel, shape_of(tables, height // tables, 4 * B), facts, pieces)
    pieces = lax.all_to_all(pieces, "pair", 0, 0, tiled=True)
    lined = pieces.reshape(height, 4 * B)
    lined_shape = shape_of(height, 4 * B)
    spread_shape = shape_of(GROUPS, TILE, B // 2)
    block_shape = shape_of(height, B)
    for pair_of_steps in range(STEPS // 2):
        if pair_of_steps == 0:
            sums = call(band_sums, spread_shape, lined)
        else:
            kernel = bind(moved_bands_kernel, tables)
            lined, sums = call(kernel, [lined_shape, spread_shape], facts, *held)
        sums = lax.all_to_all(sums, "row", 0, 0, tiled=True)
        sums = call(bind(total_kernel, peers), spread_shape, sums)
        sums = lax.all_to_all(sums, "row", 0, 0, tiled=True)
        kernel = bind(rotate_kernel, tables)
        keep, send = call(kernel, [block_shape, block_shape], facts, sums, lined)
        come = lax.ppermute(send, "pair", forward)
        if pair_of_steps < STEPS // 2 - 1:
            held = [keep, send, come, lax.ppermute(keep, "pair", backward)]
    return call(finish_kernel, shape_of(height, 2 * B), facts, keep, come)


def solution(mesh):
    in_specs = (P("row", "pair"), P())
    out_specs = P("row", "pair")
    return jax.shard_map(local, mesh=mesh, in_specs=in_specs, out_specs=out_specs, check_vma=False)
```

```python
import jax
import jax.numpy as jnp
from jax import lax
from jax.experimental import pallas as pl
from jax.experimental.pallas import tpu as pltpu
from jax.sharding import PartitionSpec as P

B = 256
STEPS = 4
INNER = 4
TILE = 8
REACH = 2 * (INNER - 1)
LAG = INNER - 1
GROUP = 24
GROUPS = 32


def ahead(block, distance):
    distance = distance % B
    return block if distance == 0 else pltpu.roll(block, B - distance, axis=1)


def ring_of(tables):
    return [0] + list(range(1, tables, 2)) + list(range(tables - 2, 0, -2))


def sends_upper(table):
    return (table == 0) | (table % 2 == 1)


def ring_before(place, tables):
    last = tables - 1
    odd = jnp.where(place == 1, 0, place - 2)
    even = jnp.where(place == last - 1, last, place + 2)
    return jnp.where(place % 2 == 1, odd, even)


def angle(upper_diag, lower_diag, coupling):
    differ = lower_diag - upper_diag
    signs = jnp.where(differ >= 0.0, 1.0, -1.0)
    whole = upper_diag + lower_diag
    denom = jnp.abs(differ) + jnp.sqrt(
        differ * differ + 4.0 * coupling * coupling + 1e-12 * (whole * whole)
    )
    tangent = 2.0 * signs * coupling / denom
    square = 1.0 + tangent * tangent
    guess = lax.rsqrt(square)
    cosines = guess * (1.5 - 0.5 * square * (guess * guess))
    return cosines, tangent * cosines


def turn_both(bands, left, right):
    (c, s), (cd, sd) = left, right
    uu, ul, lu, ll = bands
    top_u = c * uu - s * lu
    top_l = c * ul - s * ll
    low_u = s * uu + c * lu
    low_l = s * ul + c * ll
    return [
        cd * top_u - sd * top_l,
        sd * top_u + cd * top_l,
        cd * low_u - sd * low_l,
        sd * low_u + cd * low_l,
    ]


def spread(value):
    return jnp.broadcast_to(value[:1], (TILE, B))


def behind(value):
    return pltpu.roll(value, 0, axis=1, stride=1, stride_axis=0)


def solve(pairs):
    count = 1 if len(pairs) == 1 else 2
    reach_rows = lax.broadcasted_iota(jnp.int32, (TILE, B), 0) == 0
    turns = [[] for _ in range(count)]
    for sweep in range(INNER):
        wide = []
        for table in range(count):
            uu, ul, _, ll = pairs[table, table]
            c, s = (spread(v) for v in angle(uu, ll, ul))
            turns[table].append((c, s))
            wide.append((behind(c), behind(s)))
        if sweep == INNER - 1 and count == 1:
            break
        pairs = {
            (a, b): turn_both(bands, turns[a][-1], wide[b]) for (a, b), bands in pairs.items()
        }
        if sweep == INNER - 1:
            break
        for key, (uu, ul, lu, ll) in pairs.items():
            ul = pltpu.roll(ul, 1, axis=0)
            lu = ahead(pltpu.roll(lu, TILE - 1, axis=0), 1)
            pairs[key] = [uu, ul, lu, ahead(ll, 1)]
        for a, b in pairs:
            pairs[a, b][1] = jnp.where(reach_rows, pairs[b, a][2], pairs[a, b][1])
    return turns, pairs


def turn_tiles(uppers, lowers, turns):
    for sweep, (c, s) in enumerate(turns):
        pairs = list(zip(uppers, lowers))
        uppers = [c * u - s * v for u, v in pairs]
        lowers = [s * u + c * v for u, v in pairs]
        if sweep < INNER - 1:
            lowers = [ahead(v, 1) for v in lowers]
    return uppers, lowers


def mix_tiles(uppers, lowers, turns, lower_wanted):
    uppers, lowers = turn_tiles(uppers, lowers, turns[:-1])
    c, s = turns[-1]
    from_u, from_l = jnp.where(lower_wanted, s, c), jnp.where(lower_wanted, c, -s)
    return [from_u * u + from_l * v for u, v in zip(uppers, lowers)]


def sides(place, tables):
    return place == 0, place == tables - 2


def line_up(own, before, place, tables):
    own_right = place % 2 == 1
    left_lower, right_upper = sides(place, tables)
    left = [jnp.where(own_right, b, a) for a, b in zip(own, before)]
    right = [jnp.where(own_right, a, b) for a, b in zip(own, before)]
    left = [jnp.where(left_lower, ahead(v, -LAG), v) for v in left]
    right = [jnp.where(right_upper, v, ahead(v, -LAG)) for v in right]
    return left + right


def band_sums(lined_ref, out_ref):
    height = lined_ref.shape[0]
    out_ref[...] = jnp.zeros_like(out_ref)
    slots = [(x, y) for x in range(4) for y in range(4)]
    for d in range(REACH + 1):
        kept = [(x, y) for x, y in slots if d or x <= y]

        totals = None
        for tile in range(height // TILE):
            now = [lined_ref[tile * TILE : (tile + 1) * TILE, n * B : (n + 1) * B] for n in range(4)]
            then = [ahead(v, -d) for v in now]
            terms = [now[x] * then[y] for x, y in kept]
            totals = terms if totals is None else [a + b for a, b in zip(totals, terms)]
        for (x, y), total in zip(kept, totals):
            row = jnp.sum(total, axis=0, keepdims=True)
            for slot in {4 * x + y, 4 * y + x} if d == 0 else {4 * x + y}:
                out_ref[2 * slot, d : d + 1, :] = row[:, : B // 2]
                out_ref[2 * slot + 1, d : d + 1, :] = row[:, B // 2 :]


def moved_bands_kernel(tables, keep_ref, send_ref, come_ref, next_ref, lined_ref, out_ref):
    place = lax.axis_index("pair")
    before = ring_before(place, tables)
    upper_comes = place % 2 == 0
    upper_sent = before % 2 == 0
    for tile in range(keep_ref.shape[0] // TILE):
        rows = pl.ds(tile * TILE, TILE)
        keep, send, come, near = (r[rows, :] for r in (keep_ref, send_ref, come_ref, next_ref))
        own = [jnp.where(upper_comes, come, keep), jnp.where(upper_comes, keep, come)]
        other = [jnp.where(upper_sent, send, near), jnp.where(upper_sent, near, send)]
        for n, value in enumerate(line_up(own, other, place, tables)):
            lined_ref[rows, n * B : (n + 1) * B] = value
    band_sums(lined_ref, out_ref)


def total_kernel(peers, parts_ref, out_ref):
    share = parts_ref.shape[0] // peers
    for part in range(share):
        total = parts_ref[part]
        for peer in range(1, peers):
            total = total + parts_ref[peer * share + part]
        for peer in range(peers):
            out_ref[peer * share + part] = total


def rotate_kernel(tables, sums_ref, lined_ref, keep_out, send_out):
    place = lax.axis_index("pair")
    left_lower, right_upper = sides(place, tables)

    def bands(x, y):
        slot = 4 * x + y
        return jnp.concatenate([sums_ref[2 * slot], sums_ref[2 * slot + 1]], axis=1)

    pairs = {
        (a, b): [bands(2 * a + x, 2 * b + y) for x in range(2) for y in range(2)]
        for a in range(2)
        for b in range(2)
    }
    (left_turns, right_turns), pairs = solve(pairs)
    uu, _, _, ll = pairs[0, 0]
    new_uu = jnp.where(left_lower, ll, uu)
    uu, _, _, ll = pairs[1, 1]
    new_ll = jnp.where(right_upper, uu, ll)
    uu, ul, lu, ll = pairs[0, 1]
    new_ul = jnp.where(
        left_lower, jnp.where(right_upper, lu, ll), jnp.where(right_upper, uu, ul)
    )
    uu, ul, lu, ll = pairs[1, 0]
    new_lu = jnp.where(
        left_lower, jnp.where(right_upper, ul, ll), jnp.where(right_upper, uu, lu)
    )
    (last_turns,), _ = solve({(0, 0): [new_uu, new_ul, new_lu, new_ll]})
    upper_sent = sends_upper(place ^ 1)
    height = keep_out.shape[0]
    groups = [
        [slice(r, r + TILE) for r in range(start, min(start + GROUP * TILE, height), TILE)]
        for start in range(0, height, GROUP * TILE)
    ]
    for n, out_ref, turns, lower_wanted in (
        (0, keep_out, left_turns, left_lower),
        (2, send_out, right_turns, jnp.logical_not(right_upper)),
    ):
        for group in groups:
            uppers = [lined_ref[rows, n * B : (n + 1) * B] for rows in group]
            lowers = [lined_ref[rows, (n + 1) * B : (n + 2) * B] for rows in group]
            for rows, value in zip(group, mix_tiles(uppers, lowers, turns, lower_wanted)):
                out_ref[rows, :] = value
    for group in groups:
        uppers = [keep_out[rows, :] for rows in group]
        lowers = [send_out[rows, :] for rows in group]
        uppers, lowers = turn_tiles(uppers, lowers, last_turns)
        for rows, upper, lower in zip(group, uppers, lowers):
            lower = ahead(lower, -LAG)
            keep_out[rows, :] = jnp.where(upper_sent, lower, upper)
            send_out[rows, :] = jnp.where(upper_sent, upper, lower)


def finish_kernel(keep_ref, come_ref, out_ref, sems):
    keep_at = jnp.where(lax.axis_index("pair") % 2 == 0, B, 0)
    copies = []
    for n, (block_ref, start) in enumerate(((keep_ref, keep_at), (come_ref, B - keep_at))):
        columns = pl.ds(pl.multiple_of(start, B), B)
        copies.append(pltpu.make_async_copy(block_ref, out_ref.at[:, columns], sems.at[n]))
    for copy in copies:
        copy.start()
    for copy in copies:
        copy.wait()


def seat_kernel(seating_ref, blocks_ref, out_ref):
    tables = blocks_ref.shape[0]
    ring = ring_of(tables)
    for table in range(tables):
        before = ring[ring.index(table) - 1]
        left, right = (before, table) if table % 2 else (table, before)
        left_lower, right_upper = sides(table, tables)
        for n, seat in enumerate((2 * left, 2 * left + 1, 2 * right, 2 * right + 1)):
            block = seating_ref[seat]
            columns = pl.ds(pl.multiple_of((block % 2) * B, B), B)
            late = left_lower if n < 2 else not right_upper
            for tile in range(blocks_ref.shape[1] // TILE):
                rows = slice(tile * TILE, (tile + 1) * TILE)
                value = blocks_ref[block // 2, rows, columns]
                out_ref[table, rows, n * B : (n + 1) * B] = ahead(value, -LAG) if late else value


VMEM = pl.BlockSpec(memory_space=pltpu.VMEM)
SMEM = pl.BlockSpec(memory_space=pltpu.SMEM)
PARAMS = pltpu.CompilerParams(vmem_limit_bytes=32 * 1024 * 1024)


def call(kernel, out_shape, *args):
    specs = [SMEM if a.dtype == jnp.int32 else VMEM for a in args]
    outs = [VMEM] * len(out_shape) if isinstance(out_shape, list) else VMEM
    return pl.pallas_call(
        kernel, out_shape=out_shape, in_specs=specs, out_specs=outs, compiler_params=PARAMS
    )(*args)


def shape_of(*sizes):
    return jax.ShapeDtypeStruct(sizes, jnp.float32)


def bind(kernel, size):
    def bound(*refs):
        return kernel(size, *refs)

    return bound


def local(matrix, seating):
    height = matrix.shape[0]
    peers = lax.axis_size("row")
    tables = lax.axis_size("pair")
    ring = ring_of(tables)
    hosts = [table ^ 1 for table in ring]
    forward = list(zip(hosts, hosts[1:] + hosts[:1]))
    backward = [(b, a) for a, b in forward]
    pieces = matrix.reshape(tables, height // tables, 2 * B)
    pieces = lax.all_to_all(pieces, "pair", 0, 0, tiled=True)
    pieces = call(seat_kernel, shape_of(tables, height // tables, 4 * B), seating, pieces)
    pieces = lax.all_to_all(pieces, "pair", 0, 0, tiled=True)
    lined = pieces.reshape(height, 4 * B)
    lined_shape = shape_of(height, 4 * B)
    spread_shape = shape_of(GROUPS, TILE, B // 2)
    block_shape = shape_of(height, B)
    for pair_of_steps in range(STEPS // 2):
        if pair_of_steps == 0:
            sums = call(band_sums, spread_shape, lined)
        else:
            kernel = bind(moved_bands_kernel, tables)
            lined, sums = call(kernel, [lined_shape, spread_shape], *held)
        sums = lax.all_to_all(sums, "row", 0, 0, tiled=True)
        sums = call(bind(total_kernel, peers), spread_shape, sums)
        sums = lax.all_to_all(sums, "row", 0, 0, tiled=True)
        kernel = bind(rotate_kernel, tables)
        keep, send = call(kernel, [block_shape, block_shape], sums, lined)
        come = lax.ppermute(send, "pair", forward)
        if pair_of_steps < STEPS // 2 - 1:
            held = [keep, send, come, lax.ppermute(keep, "pair", backward)]
    return pl.pallas_call(
        finish_kernel,
        out_shape=shape_of(height, 2 * B),
        in_specs=[VMEM] * 2,
        out_specs=pl.BlockSpec(memory_space=pl.ANY),
        scratch_shapes=[pltpu.SemaphoreType.DMA((2,))],
        compiler_params=PARAMS,
    )(keep, come)


def solution(mesh):
    in_specs = (P("row", "pair"), P())
    out_specs = P("row", "pair")
    return jax.shard_map(local, mesh=mesh, in_specs=in_specs, out_specs=out_specs, check_vma=False)
```

```python
import jax
import jax.numpy as jnp
from jax import lax
from jax.experimental import pallas as pl
from jax.experimental.pallas import tpu as pltpu
from jax.sharding import PartitionSpec as P

B = 256
STEPS = 4
INNER = 4
TILE = 8
REACH = 2 * (INNER - 1)
LAG = INNER - 1
GROUP = 24
GROUPS = 32


def ahead(block, distance):
    distance = distance % B
    return block if distance == 0 else pltpu.roll(block, B - distance, axis=1)


def ring_of(tables):
    return [0] + list(range(1, tables, 2)) + list(range(tables - 2, 0, -2))


def sends_upper(table):
    return (table == 0) | (table % 2 == 1)


def ring_before(place, tables):
    last = tables - 1
    odd = jnp.where(place == 1, 0, place - 2)
    even = jnp.where(place == last - 1, last, place + 2)
    return jnp.where(place % 2 == 1, odd, even)


def angle(upper_diag, lower_diag, coupling):
    differ = lower_diag - upper_diag
    signs = jnp.where(differ >= 0.0, 1.0, -1.0)
    whole = upper_diag + lower_diag
    denom = jnp.abs(differ) + jnp.sqrt(
        differ * differ + 4.0 * coupling * coupling + 1e-12 * (whole * whole)
    )
    tangent = 2.0 * signs * coupling / denom
    square = 1.0 + tangent * tangent
    guess = lax.rsqrt(square)
    cosines = guess * (1.5 - 0.5 * square * (guess * guess))
    return cosines, tangent * cosines


def turn_both(bands, left, right):
    (c, s), (cd, sd) = left, right
    uu, ul, lu, ll = bands
    top_u = c * uu - s * lu
    top_l = c * ul - s * ll
    low_u = s * uu + c * lu
    low_l = s * ul + c * ll
    return [
        cd * top_u - sd * top_l,
        sd * top_u + cd * top_l,
        cd * low_u - sd * low_l,
        sd * low_u + cd * low_l,
    ]


def spread(value):
    return jnp.broadcast_to(value[:1], (TILE, B))


def behind(value):
    return pltpu.roll(value, 0, axis=1, stride=1, stride_axis=0)


def next_heads(bands, c, s):
    uu, ul, lu, ll = bands
    uu_z, ul_z, lu_z, ll_z = (ahead(v, 1) for v in bands)
    uu_y, ul_y, lu_y, ll_y = (pltpu.roll(v, TILE - 1, axis=0) for v in (uu_z, ul_z, lu_z, ll_z))
    cz, sz = ahead(c, 1), ahead(s, 1)
    head_uu = c * (c * uu - s * lu) - s * (c * ul - s * ll)
    head_ul = c * (sz * uu_y + cz * lu_y) - s * (sz * ul_y + cz * ll_y)
    head_ll = sz * (sz * uu_z + cz * lu_z) + cz * (sz * ul_z + cz * ll_z)
    return head_uu, head_ul, head_ll


def solve(pairs):
    tables = sorted({a for a, _ in pairs})
    first_row = lax.broadcasted_iota(jnp.int32, (TILE, B), 0) == 0
    turns = [[] for _ in tables]
    heads = [(pairs[t, t][0], pairs[t, t][1], pairs[t, t][3]) for t in tables]
    for sweep in range(INNER):
        wide = []
        for t in tables:
            uu, ul, ll = heads[t]
            c, s = angle(uu, ll, ul)
            if sweep < INNER - 1:
                heads[t] = next_heads(pairs[t, t], c, s)
            c, s = spread(c), spread(s)
            turns[t].append((c, s))
            wide.append((behind(c), behind(s)))
        if sweep == INNER - 1 and len(tables) == 1:
            break
        pairs = {
            (a, b): turn_both(bands, turns[a][-1], wide[b]) for (a, b), bands in pairs.items()
        }
        if sweep == INNER - 1:
            break
        for key, (uu, ul, lu, ll) in pairs.items():
            ul = pltpu.roll(ul, 1, axis=0)
            lu = ahead(pltpu.roll(lu, TILE - 1, axis=0), 1)
            pairs[key] = [uu, ul, lu, ahead(ll, 1)]
        for a, b in pairs:
            pairs[a, b][1] = jnp.where(first_row, pairs[b, a][2], pairs[a, b][1])
    return turns, pairs


def turn_tiles(uppers, lowers, turns):
    for sweep, (c, s) in enumerate(turns):
        pairs = list(zip(uppers, lowers))
        uppers = [c * u - s * v for u, v in pairs]
        lowers = [s * u + c * v for u, v in pairs]
        if sweep < INNER - 1:
            lowers = [ahead(v, 1) for v in lowers]
    return uppers, lowers


def mix_tiles(uppers, lowers, turns, lower_wanted):
    uppers, lowers = turn_tiles(uppers, lowers, turns[:-1])
    c, s = turns[-1]
    from_u, from_l = jnp.where(lower_wanted, s, c), jnp.where(lower_wanted, c, -s)
    return [from_u * u + from_l * v for u, v in zip(uppers, lowers)]


def sides(place, tables):
    return place == 0, place == tables - 2


def line_up(own, before, place, tables):
    own_right = place % 2 == 1
    left_lower, right_upper = sides(place, tables)
    left = [jnp.where(own_right, b, a) for a, b in zip(own, before)]
    right = [jnp.where(own_right, a, b) for a, b in zip(own, before)]
    left = [jnp.where(left_lower, ahead(v, -LAG), v) for v in left]
    right = [jnp.where(right_upper, v, ahead(v, -LAG)) for v in right]
    return left + right


def band_sums(lined_ref, out_ref):
    height = lined_ref.shape[0]
    out_ref[...] = jnp.zeros_like(out_ref)
    slots = [(x, y) for x in range(4) for y in range(4)]
    for d in range(REACH + 1):
        kept = [(x, y) for x, y in slots if d or x <= y]

        totals = None
        for tile in range(height // TILE):
            now = [lined_ref[tile * TILE : (tile + 1) * TILE, n * B : (n + 1) * B] for n in range(4)]
            then = [ahead(v, -d) for v in now]
            terms = [now[x] * then[y] for x, y in kept]
            totals = terms if totals is None else [a + b for a, b in zip(totals, terms)]
        for (x, y), total in zip(kept, totals):
            row = jnp.sum(total, axis=0, keepdims=True)
            for slot in {4 * x + y, 4 * y + x} if d == 0 else {4 * x + y}:
                out_ref[2 * slot, d : d + 1, :] = row[:, : B // 2]
                out_ref[2 * slot + 1, d : d + 1, :] = row[:, B // 2 :]


def moved_bands_kernel(tables, keep_ref, send_ref, come_ref, next_ref, lined_ref, out_ref):
    place = lax.axis_index("pair")
    before = ring_before(place, tables)
    upper_comes = place % 2 == 0
    upper_sent = before % 2 == 0
    for tile in range(keep_ref.shape[0] // TILE):
        rows = pl.ds(tile * TILE, TILE)
        keep, send, come, near = (r[rows, :] for r in (keep_ref, send_ref, come_ref, next_ref))
        own = [jnp.where(upper_comes, come, keep), jnp.where(upper_comes, keep, come)]
        other = [jnp.where(upper_sent, send, near), jnp.where(upper_sent, near, send)]
        for n, value in enumerate(line_up(own, other, place, tables)):
            lined_ref[rows, n * B : (n + 1) * B] = value
    band_sums(lined_ref, out_ref)


def total_kernel(peers, parts_ref, out_ref):
    share = parts_ref.shape[0] // peers
    for part in range(share):
        total = parts_ref[part]
        for peer in range(1, peers):
            total = total + parts_ref[peer * share + part]
        for peer in range(peers):
            out_ref[peer * share + part] = total


def rotate_kernel(tables, sums_ref, lined_ref, keep_out, send_out):
    place = lax.axis_index("pair")
    left_lower, right_upper = sides(place, tables)

    def bands(x, y):
        slot = 4 * x + y
        return jnp.concatenate([sums_ref[2 * slot], sums_ref[2 * slot + 1]], axis=1)

    pairs = {
        (a, b): [bands(2 * a + x, 2 * b + y) for x in range(2) for y in range(2)]
        for a in range(2)
        for b in range(2)
    }
    (left_turns, right_turns), pairs = solve(pairs)
    uu, _, _, ll = pairs[0, 0]
    new_uu = jnp.where(left_lower, ll, uu)
    uu, _, _, ll = pairs[1, 1]
    new_ll = jnp.where(right_upper, uu, ll)
    uu, ul, lu, ll = pairs[0, 1]
    new_ul = jnp.where(
        left_lower, jnp.where(right_upper, lu, ll), jnp.where(right_upper, uu, ul)
    )
    uu, ul, lu, ll = pairs[1, 0]
    new_lu = jnp.where(
        left_lower, jnp.where(right_upper, ul, ll), jnp.where(right_upper, uu, lu)
    )
    (last_turns,), _ = solve({(0, 0): [new_uu, new_ul, new_lu, new_ll]})
    upper_sent = sends_upper(place ^ 1)
    height = keep_out.shape[0]
    groups = [
        [slice(r, r + TILE) for r in range(start, min(start + GROUP * TILE, height), TILE)]
        for start in range(0, height, GROUP * TILE)
    ]
    for n, out_ref, turns, lower_wanted in (
        (0, keep_out, left_turns, left_lower),
        (2, send_out, right_turns, jnp.logical_not(right_upper)),
    ):
        for group in groups:
            uppers = [lined_ref[rows, n * B : (n + 1) * B] for rows in group]
            lowers = [lined_ref[rows, (n + 1) * B : (n + 2) * B] for rows in group]
            for rows, value in zip(group, mix_tiles(uppers, lowers, turns, lower_wanted)):
                out_ref[rows, :] = value
    for group in groups:
        uppers = [keep_out[rows, :] for rows in group]
        lowers = [send_out[rows, :] for rows in group]
        uppers, lowers = turn_tiles(uppers, lowers, last_turns)
        for rows, upper, lower in zip(group, uppers, lowers):
            lower = ahead(lower, -LAG)
            keep_out[rows, :] = jnp.where(upper_sent, lower, upper)
            send_out[rows, :] = jnp.where(upper_sent, upper, lower)


def finish_kernel(keep_ref, come_ref, out_ref, sems):
    keep_at = jnp.where(lax.axis_index("pair") % 2 == 0, B, 0)
    copies = []
    for n, (block_ref, start) in enumerate(((keep_ref, keep_at), (come_ref, B - keep_at))):
        columns = pl.ds(pl.multiple_of(start, B), B)
        copies.append(pltpu.make_async_copy(block_ref, out_ref.at[:, columns], sems.at[n]))
    for copy in copies:
        copy.start()
    for copy in copies:
        copy.wait()


def seat_kernel(seating_ref, blocks_ref, out_ref):
    tables = blocks_ref.shape[0]
    ring = ring_of(tables)
    order = seating_ref[...]
    for table in range(tables):
        before = ring[ring.index(table) - 1]
        left, right = (before, table) if table % 2 else (table, before)
        left_lower, right_upper = sides(table, tables)
        for n, seat in enumerate((2 * left, 2 * left + 1, 2 * right, 2 * right + 1)):
            block = order[0, seat]
            columns = pl.ds(pl.multiple_of((block % 2) * B, B), B)
            late = left_lower if n < 2 else not right_upper
            for tile in range(blocks_ref.shape[1] // TILE):
                rows = slice(tile * TILE, (tile + 1) * TILE)
                value = blocks_ref[block // 2, rows, columns]
                out_ref[table, rows, n * B : (n + 1) * B] = ahead(value, -LAG) if late else value


VMEM = pl.BlockSpec(memory_space=pltpu.VMEM)
PARAMS = pltpu.CompilerParams(vmem_limit_bytes=32 * 1024 * 1024)


def call(kernel, out_shape, *args):
    outs = [VMEM] * len(out_shape) if isinstance(out_shape, list) else VMEM
    return pl.pallas_call(
        kernel,
        out_shape=out_shape,
        in_specs=[VMEM] * len(args),
        out_specs=outs,
        compiler_params=PARAMS,
    )(*args)


def shape_of(*sizes):
    return jax.ShapeDtypeStruct(sizes, jnp.float32)


def bind(kernel, size):
    def bound(*refs):
        return kernel(size, *refs)

    return bound


def local(matrix, seating):
    height = matrix.shape[0]
    peers = lax.axis_size("row")
    tables = lax.axis_size("pair")
    ring = ring_of(tables)
    hosts = [table ^ 1 for table in ring]
    forward = list(zip(hosts, hosts[1:] + hosts[:1]))
    backward = [(b, a) for a, b in forward]
    pieces = matrix.reshape(tables, height // tables, 2 * B)
    pieces = lax.all_to_all(pieces, "pair", 0, 0, tiled=True)
    pieces = call(seat_kernel, shape_of(tables, height // tables, 4 * B), seating[None], pieces)
    pieces = lax.all_to_all(pieces, "pair", 0, 0, tiled=True)
    lined = pieces.reshape(height, 4 * B)
    lined_shape = shape_of(height, 4 * B)
    spread_shape = shape_of(GROUPS, TILE, B // 2)
    block_shape = shape_of(height, B)
    for pair_of_steps in range(STEPS // 2):
        if pair_of_steps == 0:
            sums = call(band_sums, spread_shape, lined)
        else:
            kernel = bind(moved_bands_kernel, tables)
            lined, sums = call(kernel, [lined_shape, spread_shape], *held)
        sums = lax.all_to_all(sums, "row", 0, 0, tiled=True)
        sums = call(bind(total_kernel, peers), spread_shape, sums)
        sums = lax.all_to_all(sums, "row", 0, 0, tiled=True)
        kernel = bind(rotate_kernel, tables)
        keep, send = call(kernel, [block_shape, block_shape], sums, lined)
        come = lax.ppermute(send, "pair", forward)
        if pair_of_steps < STEPS // 2 - 1:
            held = [keep, send, come, lax.ppermute(keep, "pair", backward)]
    return pl.pallas_call(
        finish_kernel,
        out_shape=shape_of(height, 2 * B),
        in_specs=[VMEM] * 2,
        out_specs=pl.BlockSpec(memory_space=pl.ANY),
        scratch_shapes=[pltpu.SemaphoreType.DMA((2,))],
        compiler_params=PARAMS,
    )(keep, come)


def solution(mesh):
    in_specs = (P("row", "pair"), P())
    out_specs = P("row", "pair")
    return jax.shard_map(local, mesh=mesh, in_specs=in_specs, out_specs=out_specs, check_vma=False)
```

```python
import jax
import jax.numpy as jnp
from jax import lax
from jax.experimental import pallas as pl
from jax.experimental.pallas import tpu as pltpu
from jax.sharding import PartitionSpec as P

B = 256
STEPS = 4
INNER = 4
TILE = 8
REACH = 2 * (INNER - 1)
ALL_PAIRS = [(x, y) for x in range(4) for y in range(4)]
LAG = INNER - 1
GROUP = 24
GROUPS = 32


def ahead(block, distance):
    distance = distance % B
    return block if distance == 0 else pltpu.roll(block, B - distance, axis=1)


def ring_of(tables):
    return [0] + list(range(1, tables, 2)) + list(range(tables - 2, 0, -2))


def sends_upper(table):
    return (table == 0) | (table % 2 == 1)


def ring_before(place, tables):
    last = tables - 1
    odd = jnp.where(place == 1, 0, place - 2)
    even = jnp.where(place == last - 1, last, place + 2)
    return jnp.where(place % 2 == 1, odd, even)


def angle(upper_diag, lower_diag, coupling):
    differ = lower_diag - upper_diag
    signs = jnp.where(differ >= 0.0, 1.0, -1.0)
    whole = upper_diag + lower_diag
    denom = jnp.abs(differ) + jnp.sqrt(
        differ * differ + 4.0 * coupling * coupling + 1e-12 * (whole * whole)
    )
    tangent = 2.0 * signs * coupling / denom
    square = 1.0 + tangent * tangent
    guess = lax.rsqrt(square)
    cosines = guess * (1.5 - 0.5 * square * (guess * guess))
    return cosines, tangent * cosines


def turn_both(bands, left, right):
    (c, s), (cd, sd) = left, right
    uu, ul, lu, ll = bands
    top_u = c * uu - s * lu
    top_l = c * ul - s * ll
    low_u = s * uu + c * lu
    low_l = s * ul + c * ll
    return [
        cd * top_u - sd * top_l,
        sd * top_u + cd * top_l,
        cd * low_u - sd * low_l,
        sd * low_u + cd * low_l,
    ]


def spread(value):
    return jnp.broadcast_to(value[:1], (TILE, B))


def behind(value):
    return pltpu.roll(value, 0, axis=1, stride=1, stride_axis=0)


def next_heads(bands, c, s):
    uu, ul, lu, ll = bands
    uu_z, ul_z, lu_z, ll_z = (ahead(v, 1) for v in bands)
    uu_y, ul_y, lu_y, ll_y = (pltpu.roll(v, TILE - 1, axis=0) for v in (uu_z, ul_z, lu_z, ll_z))
    cz, sz = ahead(c, 1), ahead(s, 1)
    head_uu = c * (c * uu - s * lu) - s * (c * ul - s * ll)
    head_ul = c * (sz * uu_y + cz * lu_y) - s * (sz * ul_y + cz * ll_y)
    head_ll = sz * (sz * uu_z + cz * lu_z) + cz * (sz * ul_z + cz * ll_z)
    return head_uu, head_ul, head_ll


def solve(pairs):
    tables = sorted({a for a, _ in pairs})
    first_row = lax.broadcasted_iota(jnp.int32, (TILE, B), 0) == 0
    turns = [[] for _ in tables]
    heads = [(pairs[t, t][0], pairs[t, t][1], pairs[t, t][3]) for t in tables]
    for sweep in range(INNER):
        wide = []
        for t in tables:
            uu, ul, ll = heads[t]
            c, s = angle(uu, ll, ul)
            if sweep < INNER - 1:
                heads[t] = next_heads(pairs[t, t], c, s)
            c, s = spread(c), spread(s)
            turns[t].append((c, s))
            wide.append((behind(c), behind(s)))
        if sweep == INNER - 1 and len(tables) == 1:
            break
        pairs = {
            (a, b): turn_both(bands, turns[a][-1], wide[b]) for (a, b), bands in pairs.items()
        }
        if sweep == INNER - 1:
            break
        for key, (uu, ul, lu, ll) in pairs.items():
            ul = pltpu.roll(ul, 1, axis=0)
            lu = ahead(pltpu.roll(lu, TILE - 1, axis=0), 1)
            pairs[key] = [uu, ul, lu, ahead(ll, 1)]
        for a, b in pairs:
            pairs[a, b][1] = jnp.where(first_row, pairs[b, a][2], pairs[a, b][1])
    return turns, pairs


def turn_tiles(uppers, lowers, turns):
    for sweep, (c, s) in enumerate(turns):
        pairs = list(zip(uppers, lowers))
        uppers = [c * u - s * v for u, v in pairs]
        lowers = [s * u + c * v for u, v in pairs]
        if sweep < INNER - 1:
            lowers = [ahead(v, 1) for v in lowers]
    return uppers, lowers


def mix_tiles(uppers, lowers, turns, lower_wanted):
    uppers, lowers = turn_tiles(uppers, lowers, turns[:-1])
    c, s = turns[-1]
    from_u, from_l = jnp.where(lower_wanted, s, c), jnp.where(lower_wanted, c, -s)
    return [from_u * u + from_l * v for u, v in zip(uppers, lowers)]


def sides(place, tables):
    return place == 0, place == tables - 2


def product_sums(load, height, pairs):
    used = sorted({n for pair in pairs for n in pair})
    totals = {}
    for d in range(REACH + 1):
        kept = [(x, y) for x, y in pairs if d or x <= y or (y, x) not in pairs]
        for start in range(0, height, TILE):
            now = {n: load(n, slice(start, start + TILE)) for n in used}
            then = {n: ahead(v, -d) for n, v in now.items()}
            for x, y in kept:
                term = now[x] * then[y]
                totals[x, y, d] = term if start == 0 else totals[x, y, d] + term
    for x, y in pairs:
        if (x, y, 0) not in totals:
            totals[x, y, 0] = totals[y, x, 0]
    return {key: jnp.sum(total, axis=0, keepdims=True) for key, total in totals.items()}


def put_sums(out_ref, sums, pairs, slot_of):
    for x, y in pairs:
        slot = slot_of(x, y)
        for half in range(2):
            columns = slice(half * (B // 2), (half + 1) * (B // 2))
            for d in range(REACH + 1):
                out_ref[2 * slot + half, d : d + 1, :] = sums[x, y, d][:, columns]


def seated_bands_kernel(lined_ref, out_ref):
    def load(n, rows):
        return lined_ref[rows, n * B : (n + 1) * B]

    out_ref[...] = jnp.zeros_like(out_ref)
    sums = product_sums(load, lined_ref.shape[0], ALL_PAIRS)
    put_sums(out_ref, sums, ALL_PAIRS, lambda x, y: 4 * x + y)


def lags(place, tables):
    odd = place % 2 == 1
    return odd | (place == 0), jnp.logical_not(odd | (place == tables - 2))


def held_bands_kernel(tables, keep_ref, send_ref, late_ref, out_ref):
    lag = lags(lax.axis_index("pair"), tables)
    out_ref[...] = jnp.zeros_like(out_ref)
    height = keep_ref.shape[0]
    for start in range(0, height, TILE):
        rows = slice(start, start + TILE)
        for n, ref in enumerate((keep_ref, send_ref)):
            value = ref[rows, :]
            late_ref[rows, n * B : (n + 1) * B] = jnp.where(lag[n], ahead(value, -LAG), value)

    def load(n, rows):
        return late_ref[rows, n * B : (n + 1) * B]

    pairs = [(x, y) for x in range(2) for y in range(2)]
    put_sums(out_ref, product_sums(load, height, pairs), pairs, lambda x, y: 2 * x + y)


def moved_bands_kernel(tables, late_ref, held_ref, come_ref, next_ref, lined_ref, out_ref):
    place = lax.axis_index("pair")
    odd = place % 2
    lower_sent = ring_before(place, tables) % 2
    own, other = 2 * odd, 2 - 2 * odd
    at = [own + 1 - odd, other + lower_sent, own + odd, other + 1 - lower_sent]
    lag = lags(place, tables)
    out_ref[...] = jnp.zeros_like(out_ref)
    height = come_ref.shape[0]
    columns = [pl.ds(pl.multiple_of(n * B, B), B) for n in at]
    for start in range(0, height, TILE):
        rows = slice(start, start + TILE)
        for n in range(2):
            lined_ref[rows, columns[n]] = late_ref[rows, n * B : (n + 1) * B]
        for n, ref in enumerate((come_ref, next_ref)):
            value = ref[rows, :]
            lined_ref[rows, columns[2 + n]] = jnp.where(lag[n], ahead(value, -LAG), value)

    def load(n, rows):
        return lined_ref[rows, columns[n]]

    def slot_of(x, y):
        return 4 * at[x] + at[y]

    pairs = [(x, y) for x, y in ALL_PAIRS if x > 1 or y > 1]
    put_sums(out_ref, product_sums(load, height, pairs), pairs, slot_of)
    for x in range(2):
        for y in range(2):
            for half in range(2):
                out_ref[2 * slot_of(x, y) + half] = held_ref[2 * (2 * x + y) + half]


def total_kernel(peers, parts_ref, out_ref):
    share = parts_ref.shape[0] // peers
    for part in range(share):
        total = parts_ref[part]
        for peer in range(1, peers):
            total = total + parts_ref[peer * share + part]
        for peer in range(peers):
            out_ref[peer * share + part] = total


def rotate_kernel(tables, sums_ref, lined_ref, keep_out, send_out):
    place = lax.axis_index("pair")
    left_lower, right_upper = sides(place, tables)

    def bands(x, y):
        slot = 4 * x + y
        return jnp.concatenate([sums_ref[2 * slot], sums_ref[2 * slot + 1]], axis=1)

    pairs = {
        (a, b): [bands(2 * a + x, 2 * b + y) for x in range(2) for y in range(2)]
        for a in range(2)
        for b in range(2)
    }
    (left_turns, right_turns), pairs = solve(pairs)
    uu, _, _, ll = pairs[0, 0]
    new_uu = jnp.where(left_lower, ll, uu)
    uu, _, _, ll = pairs[1, 1]
    new_ll = jnp.where(right_upper, uu, ll)
    uu, ul, lu, ll = pairs[0, 1]
    new_ul = jnp.where(
        left_lower, jnp.where(right_upper, lu, ll), jnp.where(right_upper, uu, ul)
    )
    uu, ul, lu, ll = pairs[1, 0]
    new_lu = jnp.where(
        left_lower, jnp.where(right_upper, ul, ll), jnp.where(right_upper, uu, lu)
    )
    (last_turns,), _ = solve({(0, 0): [new_uu, new_ul, new_lu, new_ll]})
    upper_sent = sends_upper(place ^ 1)
    height = keep_out.shape[0]
    groups = [
        [slice(r, r + TILE) for r in range(start, min(start + GROUP * TILE, height), TILE)]
        for start in range(0, height, GROUP * TILE)
    ]
    for n, out_ref, turns, lower_wanted in (
        (0, keep_out, left_turns, left_lower),
        (2, send_out, right_turns, jnp.logical_not(right_upper)),
    ):
        for group in groups:
            uppers = [lined_ref[rows, n * B : (n + 1) * B] for rows in group]
            lowers = [lined_ref[rows, (n + 1) * B : (n + 2) * B] for rows in group]
            for rows, value in zip(group, mix_tiles(uppers, lowers, turns, lower_wanted)):
                out_ref[rows, :] = value
    for group in groups:
        uppers = [keep_out[rows, :] for rows in group]
        lowers = [send_out[rows, :] for rows in group]
        uppers, lowers = turn_tiles(uppers, lowers, last_turns)
        for rows, upper, lower in zip(group, uppers, lowers):
            lower = ahead(lower, -LAG)
            keep_out[rows, :] = jnp.where(upper_sent, lower, upper)
            send_out[rows, :] = jnp.where(upper_sent, upper, lower)


def finish_kernel(keep_ref, come_ref, out_ref, sems):
    keep_at = jnp.where(lax.axis_index("pair") % 2 == 0, B, 0)
    copies = []
    for n, (block_ref, start) in enumerate(((keep_ref, keep_at), (come_ref, B - keep_at))):
        columns = pl.ds(pl.multiple_of(start, B), B)
        copies.append(pltpu.make_async_copy(block_ref, out_ref.at[:, columns], sems.at[n]))
    for copy in copies:
        copy.start()
    for copy in copies:
        copy.wait()


def seat_kernel(seating_ref, blocks_ref, out_ref):
    tables = blocks_ref.shape[0]
    ring = ring_of(tables)
    for table in range(tables):
        before = ring[ring.index(table) - 1]
        left, right = (before, table) if table % 2 else (table, before)
        left_lower, right_upper = sides(table, tables)
        for n, seat in enumerate((2 * left, 2 * left + 1, 2 * right, 2 * right + 1)):
            block = seating_ref[seat]
            columns = pl.ds(pl.multiple_of((block % 2) * B, B), B)
            late = left_lower if n < 2 else not right_upper
            for tile in range(blocks_ref.shape[1] // TILE):
                rows = slice(tile * TILE, (tile + 1) * TILE)
                value = blocks_ref[block // 2, rows, columns]
                out_ref[table, rows, n * B : (n + 1) * B] = ahead(value, -LAG) if late else value


VMEM = pl.BlockSpec(memory_space=pltpu.VMEM)
SMEM = pl.BlockSpec(memory_space=pltpu.SMEM)
PARAMS = pltpu.CompilerParams(vmem_limit_bytes=32 * 1024 * 1024)


def call(kernel, out_shape, *args):
    outs = [VMEM] * len(out_shape) if isinstance(out_shape, list) else VMEM
    return pl.pallas_call(
        kernel,
        out_shape=out_shape,
        in_specs=[SMEM if a.dtype == jnp.int32 else VMEM for a in args],
        out_specs=outs,
        compiler_params=PARAMS,
    )(*args)


def shape_of(*sizes):
    return jax.ShapeDtypeStruct(sizes, jnp.float32)


def bind(kernel, size):
    def bound(*refs):
        return kernel(size, *refs)

    return bound


def local(matrix, seating):
    height = matrix.shape[0]
    peers = lax.axis_size("row")
    tables = lax.axis_size("pair")
    ring = ring_of(tables)
    hosts = [table ^ 1 for table in ring]
    forward = list(zip(hosts, hosts[1:] + hosts[:1]))
    backward = [(b, a) for a, b in forward]
    pieces = matrix.reshape(tables, height // tables, 2 * B)
    pieces = lax.all_to_all(pieces, "pair", 0, 0, tiled=True)
    pieces = call(seat_kernel, shape_of(tables, height // tables, 4 * B), seating, pieces)
    pieces = lax.all_to_all(pieces, "pair", 0, 0, tiled=True)
    lined = pieces.reshape(height, 4 * B)
    lined_shape = shape_of(height, 4 * B)
    spread_shape = shape_of(GROUPS, TILE, B // 2)
    block_shape = shape_of(height, B)
    for pair_of_steps in range(STEPS // 2):
        if pair_of_steps == 0:
            sums = call(seated_bands_kernel, spread_shape, lined)
        else:
            kernel = bind(moved_bands_kernel, tables)
            lined, sums = call(kernel, [lined_shape, spread_shape], *held)
        sums = lax.all_to_all(sums, "row", 0, 0, tiled=True)
        sums = call(bind(total_kernel, peers), spread_shape, sums)
        sums = lax.all_to_all(sums, "row", 0, 0, tiled=True)
        kernel = bind(rotate_kernel, tables)
        keep, send = call(kernel, [block_shape, block_shape], sums, lined)
        come = lax.ppermute(send, "pair", forward)
        if pair_of_steps < STEPS // 2 - 1:
            near = lax.ppermute(keep, "pair", backward)
            shapes = [shape_of(height, 2 * B), shape_of(TILE, TILE, B // 2)]
            late, local_sums = call(bind(held_bands_kernel, tables), shapes, keep, send)
            held = [late, local_sums, come, near]
    return pl.pallas_call(
        finish_kernel,
        out_shape=shape_of(height, 2 * B),
        in_specs=[VMEM] * 2,
        out_specs=pl.BlockSpec(memory_space=pl.ANY),
        scratch_shapes=[pltpu.SemaphoreType.DMA((2,))],
        compiler_params=PARAMS,
    )(keep, come)


def solution(mesh):
    in_specs = (P("row", "pair"), P())
    out_specs = P("row", "pair")
    return jax.shard_map(local, mesh=mesh, in_specs=in_specs, out_specs=out_specs, check_vma=False)
```

```python
import jax
import jax.numpy as jnp
from jax import lax
from jax.experimental import pallas as pl
from jax.experimental.pallas import tpu as pltpu
from jax.sharding import PartitionSpec as P

B = 256
STEPS = 4
INNER = 4
TILE = 8
REACH = 2 * (INNER - 1)
ALL_PAIRS = [(x, y) for x in range(4) for y in range(4)]
LAG = INNER - 1
GROUP = 24
GROUPS = 32


def ahead(block, distance):
    distance = distance % B
    return block if distance == 0 else pltpu.roll(block, B - distance, axis=1)


def ring_of(tables):
    return [0] + list(range(1, tables, 2)) + list(range(tables - 2, 0, -2))


def sends_upper(table):
    return (table == 0) | (table % 2 == 1)


def ring_before(place, tables):
    last = tables - 1
    odd = jnp.where(place == 1, 0, place - 2)
    even = jnp.where(place == last - 1, last, place + 2)
    return jnp.where(place % 2 == 1, odd, even)


def angle(upper_diag, lower_diag, coupling):
    differ = lower_diag - upper_diag
    signs = jnp.where(differ >= 0.0, 1.0, -1.0)
    whole = upper_diag + lower_diag
    denom = jnp.abs(differ) + jnp.sqrt(
        differ * differ + 4.0 * coupling * coupling + 1e-12 * (whole * whole)
    )
    tangent = 2.0 * signs * coupling / denom
    square = 1.0 + tangent * tangent
    guess = lax.rsqrt(square)
    cosines = guess * (1.5 - 0.5 * square * (guess * guess))
    return cosines, tangent * cosines


def turn_both(bands, left, right):
    (c, s), (cd, sd) = left, right
    uu, ul, lu, ll = bands
    top_u = c * uu - s * lu
    top_l = c * ul - s * ll
    low_u = s * uu + c * lu
    low_l = s * ul + c * ll
    return [
        cd * top_u - sd * top_l,
        sd * top_u + cd * top_l,
        cd * low_u - sd * low_l,
        sd * low_u + cd * low_l,
    ]


def spread(value):
    return jnp.broadcast_to(value[:1], (TILE, B))


def behind(value):
    return pltpu.roll(value, 0, axis=1, stride=1, stride_axis=0)


def next_heads(bands, c, s):
    uu, ul, lu, ll = bands
    uu_z, ul_z, lu_z, ll_z = (ahead(v, 1) for v in bands)
    uu_y, ul_y, lu_y, ll_y = (pltpu.roll(v, TILE - 1, axis=0) for v in (uu_z, ul_z, lu_z, ll_z))
    cz, sz = ahead(c, 1), ahead(s, 1)
    head_uu = c * (c * uu - s * lu) - s * (c * ul - s * ll)
    head_ul = c * (sz * uu_y + cz * lu_y) - s * (sz * ul_y + cz * ll_y)
    head_ll = sz * (sz * uu_z + cz * lu_z) + cz * (sz * ul_z + cz * ll_z)
    return head_uu, head_ul, head_ll


def solve(pairs):
    tables = sorted({a for a, _ in pairs})
    first_row = lax.broadcasted_iota(jnp.int32, (TILE, B), 0) == 0
    turns = [[] for _ in tables]
    heads = [(pairs[t, t][0], pairs[t, t][1], pairs[t, t][3]) for t in tables]
    for sweep in range(INNER):
        wide = []
        for t in tables:
            uu, ul, ll = heads[t]
            c, s = angle(uu, ll, ul)
            if sweep < INNER - 1:
                heads[t] = next_heads(pairs[t, t], c, s)
            c, s = spread(c), spread(s)
            turns[t].append((c, s))
            wide.append((behind(c), behind(s)))
        if sweep == INNER - 1 and len(tables) == 1:
            break
        pairs = {
            (a, b): turn_both(bands, turns[a][-1], wide[b]) for (a, b), bands in pairs.items()
        }
        if sweep == INNER - 1:
            break
        for key, (uu, ul, lu, ll) in pairs.items():
            ul = pltpu.roll(ul, 1, axis=0)
            lu = ahead(pltpu.roll(lu, TILE - 1, axis=0), 1)
            pairs[key] = [uu, ul, lu, ahead(ll, 1)]
        for a, b in pairs:
            pairs[a, b][1] = jnp.where(first_row, pairs[b, a][2], pairs[a, b][1])
    return turns, pairs


def turn_tiles(uppers, lowers, turns):
    for sweep, (c, s) in enumerate(turns):
        pairs = list(zip(uppers, lowers))
        uppers = [c * u - s * v for u, v in pairs]
        lowers = [s * u + c * v for u, v in pairs]
        if sweep < INNER - 1:
            lowers = [ahead(v, 1) for v in lowers]
    return uppers, lowers


def mix_tiles(uppers, lowers, turns, lower_wanted):
    uppers, lowers = turn_tiles(uppers, lowers, turns[:-1])
    c, s = turns[-1]
    from_u, from_l = jnp.where(lower_wanted, s, c), jnp.where(lower_wanted, c, -s)
    return [from_u * u + from_l * v for u, v in zip(uppers, lowers)]


def sides(place, tables):
    return place == 0, place == tables - 2


def product_sums(load, height, pairs):
    used = sorted({n for pair in pairs for n in pair})
    totals = {}
    for d in range(REACH + 1):
        kept = [(x, y) for x, y in pairs if d or x <= y or (y, x) not in pairs]
        for start in range(0, height, TILE):
            now = {n: load(n, slice(start, start + TILE)) for n in used}
            then = {n: ahead(v, -d) for n, v in now.items()}
            for x, y in kept:
                term = now[x] * then[y]
                totals[x, y, d] = term if start == 0 else totals[x, y, d] + term
    for x, y in pairs:
        if (x, y, 0) not in totals:
            totals[x, y, 0] = totals[y, x, 0]
    return {key: jnp.sum(total, axis=0, keepdims=True) for key, total in totals.items()}


def put_sums(out_ref, sums, pairs, slot_of):
    for x, y in pairs:
        slot = slot_of(x, y)
        for half in range(2):
            columns = slice(half * (B // 2), (half + 1) * (B // 2))
            for d in range(REACH + 1):
                out_ref[2 * slot + half, d : d + 1, :] = sums[x, y, d][:, columns]


def seated_bands_kernel(lined_ref, out_ref):
    def load(n, rows):
        return lined_ref[rows, n * B : (n + 1) * B]

    out_ref[...] = jnp.zeros_like(out_ref)
    sums = product_sums(load, lined_ref.shape[0], ALL_PAIRS)
    put_sums(out_ref, sums, ALL_PAIRS, lambda x, y: 4 * x + y)


def lags(place, tables):
    odd = place % 2 == 1
    return odd | (place == 0), jnp.logical_not(odd | (place == tables - 2))


def held_bands_kernel(tables, keep_ref, send_ref, late_ref, out_ref):
    lag = lags(lax.axis_index("pair"), tables)
    out_ref[...] = jnp.zeros_like(out_ref)
    height = keep_ref.shape[0]
    for start in range(0, height, TILE):
        rows = slice(start, start + TILE)
        for n, ref in enumerate((keep_ref, send_ref)):
            value = ref[rows, :]
            late_ref[rows, n * B : (n + 1) * B] = jnp.where(lag[n], ahead(value, -LAG), value)

    def load(n, rows):
        return late_ref[rows, n * B : (n + 1) * B]

    pairs = [(x, y) for x in range(2) for y in range(2)]
    put_sums(out_ref, product_sums(load, height, pairs), pairs, lambda x, y: 2 * x + y)


def moved_bands_kernel(tables, late_ref, held_ref, come_ref, next_ref, lined_ref, out_ref):
    place = lax.axis_index("pair")
    odd = place % 2
    lower_sent = ring_before(place, tables) % 2
    own, other = 2 * odd, 2 - 2 * odd
    at = [own + 1 - odd, other + lower_sent, own + odd, other + 1 - lower_sent]
    lag = lags(place, tables)
    out_ref[...] = jnp.zeros_like(out_ref)
    height = come_ref.shape[0]
    columns = [pl.ds(pl.multiple_of(n * B, B), B) for n in at]
    for start in range(0, height, TILE):
        rows = slice(start, start + TILE)
        for n in range(2):
            lined_ref[rows, columns[n]] = late_ref[rows, n * B : (n + 1) * B]
        for n, ref in enumerate((come_ref, next_ref)):
            value = ref[rows, :]
            lined_ref[rows, columns[2 + n]] = jnp.where(lag[n], ahead(value, -LAG), value)

    def load(n, rows):
        return lined_ref[rows, columns[n]]

    def slot_of(x, y):
        return 4 * at[x] + at[y]

    pairs = [(x, y) for x, y in ALL_PAIRS if x > 1 or y > 1]
    put_sums(out_ref, product_sums(load, height, pairs), pairs, slot_of)
    for x in range(2):
        for y in range(2):
            for half in range(2):
                out_ref[2 * slot_of(x, y) + half] = held_ref[2 * (2 * x + y) + half]


def total_kernel(peers, parts_ref, out_ref):
    share = parts_ref.shape[0] // peers
    for part in range(share):
        total = parts_ref[part]
        for peer in range(1, peers):
            total = total + parts_ref[peer * share + part]
        for peer in range(peers):
            out_ref[peer * share + part] = total


def rotate_kernel(tables, sums_ref, lined_ref, keep_out, send_out):
    place = lax.axis_index("pair")
    left_lower, right_upper = sides(place, tables)

    def bands(x, y):
        slot = 4 * x + y
        return jnp.concatenate([sums_ref[2 * slot], sums_ref[2 * slot + 1]], axis=1)

    pairs = {
        (a, b): [bands(2 * a + x, 2 * b + y) for x in range(2) for y in range(2)]
        for a in range(2)
        for b in range(2)
    }
    (left_turns, right_turns), pairs = solve(pairs)
    uu, _, _, ll = pairs[0, 0]
    new_uu = jnp.where(left_lower, ll, uu)
    uu, _, _, ll = pairs[1, 1]
    new_ll = jnp.where(right_upper, uu, ll)
    uu, ul, lu, ll = pairs[0, 1]
    new_ul = jnp.where(
        left_lower, jnp.where(right_upper, lu, ll), jnp.where(right_upper, uu, ul)
    )
    uu, ul, lu, ll = pairs[1, 0]
    new_lu = jnp.where(
        left_lower, jnp.where(right_upper, ul, ll), jnp.where(right_upper, uu, lu)
    )
    (last_turns,), _ = solve({(0, 0): [new_uu, new_ul, new_lu, new_ll]})
    upper_sent = sends_upper(place ^ 1)
    height = keep_out.shape[0]
    groups = [
        [slice(r, r + TILE) for r in range(start, min(start + GROUP * TILE, height), TILE)]
        for start in range(0, height, GROUP * TILE)
    ]
    for n, out_ref, turns, lower_wanted in (
        (0, keep_out, left_turns, left_lower),
        (2, send_out, right_turns, jnp.logical_not(right_upper)),
    ):
        for group in groups:
            uppers = [lined_ref[rows, n * B : (n + 1) * B] for rows in group]
            lowers = [lined_ref[rows, (n + 1) * B : (n + 2) * B] for rows in group]
            for rows, value in zip(group, mix_tiles(uppers, lowers, turns, lower_wanted)):
                out_ref[rows, :] = value
    for group in groups:
        uppers = [keep_out[rows, :] for rows in group]
        lowers = [send_out[rows, :] for rows in group]
        uppers, lowers = turn_tiles(uppers, lowers, last_turns)
        for rows, upper, lower in zip(group, uppers, lowers):
            lower = ahead(lower, -LAG)
            keep_out[rows, :] = jnp.where(upper_sent, lower, upper)
            send_out[rows, :] = jnp.where(upper_sent, upper, lower)


def finish_kernel(keep_ref, come_ref, out_ref, sems):
    keep_at = jnp.where(lax.axis_index("pair") % 2 == 0, B, 0)
    copies = []
    for n, (block_ref, start) in enumerate(((keep_ref, keep_at), (come_ref, B - keep_at))):
        columns = pl.ds(pl.multiple_of(start, B), B)
        copies.append(pltpu.make_async_copy(block_ref, out_ref.at[:, columns], sems.at[n]))
    for copy in copies:
        copy.start()
    for copy in copies:
        copy.wait()


def seat_kernel(seating_ref, blocks_ref, out_ref):
    tables = blocks_ref.shape[0]
    ring = ring_of(tables)
    order = seating_ref[...]
    for table in range(tables):
        before = ring[ring.index(table) - 1]
        left, right = (before, table) if table % 2 else (table, before)
        left_lower, right_upper = sides(table, tables)
        for n, seat in enumerate((2 * left, 2 * left + 1, 2 * right, 2 * right + 1)):
            block = order[seat]
            columns = pl.ds(pl.multiple_of((block % 2) * B, B), B)
            late = left_lower if n < 2 else not right_upper
            for tile in range(blocks_ref.shape[1] // TILE):
                rows = slice(tile * TILE, (tile + 1) * TILE)
                value = blocks_ref[block // 2, rows, columns]
                out_ref[table, rows, n * B : (n + 1) * B] = ahead(value, -LAG) if late else value


VMEM = pl.BlockSpec(memory_space=pltpu.VMEM)
PARAMS = pltpu.CompilerParams(vmem_limit_bytes=32 * 1024 * 1024)


def call(kernel, out_shape, *args):
    outs = [VMEM] * len(out_shape) if isinstance(out_shape, list) else VMEM
    return pl.pallas_call(
        kernel,
        out_shape=out_shape,
        in_specs=[VMEM] * len(args),
        out_specs=outs,
        compiler_params=PARAMS,
    )(*args)


def shape_of(*sizes):
    return jax.ShapeDtypeStruct(sizes, jnp.float32)


def bind(kernel, size):
    def bound(*refs):
        return kernel(size, *refs)

    return bound


def local(matrix, seating):
    height = matrix.shape[0]
    peers = lax.axis_size("row")
    tables = lax.axis_size("pair")
    ring = ring_of(tables)
    hosts = [table ^ 1 for table in ring]
    forward = list(zip(hosts, hosts[1:] + hosts[:1]))
    backward = [(b, a) for a, b in forward]
    pieces = matrix.reshape(tables, height // tables, 2 * B)
    pieces = lax.all_to_all(pieces, "pair", 0, 0, tiled=True)
    pieces = call(seat_kernel, shape_of(tables, height // tables, 4 * B), seating, pieces)
    pieces = lax.all_to_all(pieces, "pair", 0, 0, tiled=True)
    lined = pieces.reshape(height, 4 * B)
    lined_shape = shape_of(height, 4 * B)
    spread_shape = shape_of(GROUPS, TILE, B // 2)
    block_shape = shape_of(height, B)
    for pair_of_steps in range(STEPS // 2):
        if pair_of_steps == 0:
            sums = call(seated_bands_kernel, spread_shape, lined)
        else:
            kernel = bind(moved_bands_kernel, tables)
            lined, sums = call(kernel, [lined_shape, spread_shape], *held)
        sums = lax.all_to_all(sums, "row", 0, 0, tiled=True)
        sums = call(bind(total_kernel, peers), spread_shape, sums)
        sums = lax.all_to_all(sums, "row", 0, 0, tiled=True)
        kernel = bind(rotate_kernel, tables)
        keep, send = call(kernel, [block_shape, block_shape], sums, lined)
        come = lax.ppermute(send, "pair", forward)
        if pair_of_steps < STEPS // 2 - 1:
            near = lax.ppermute(keep, "pair", backward)
            shapes = [shape_of(height, 2 * B), shape_of(TILE, TILE, B // 2)]
            late, local_sums = call(bind(held_bands_kernel, tables), shapes, keep, send)
            held = [late, local_sums, come, near]
    return pl.pallas_call(
        finish_kernel,
        out_shape=shape_of(height, 2 * B),
        in_specs=[VMEM] * 2,
        out_specs=pl.BlockSpec(memory_space=pl.ANY),
        scratch_shapes=[pltpu.SemaphoreType.DMA((2,))],
        compiler_params=PARAMS,
    )(keep, come)


def solution(mesh):
    in_specs = (P("row", "pair"), P())
    out_specs = P("row", "pair")
    return jax.shard_map(local, mesh=mesh, in_specs=in_specs, out_specs=out_specs, check_vma=False)
```

```python
import jax
import jax.numpy as jnp
from jax import lax
from jax.experimental import pallas as pl
from jax.experimental.pallas import tpu as pltpu
from jax.sharding import PartitionSpec as P

B = 256
STEPS = 4
INNER = 4
TILE = 8
REACH = 2 * (INNER - 1)
ALL_PAIRS = [(x, y) for x in range(4) for y in range(4)]
LAG = INNER - 1
GROUP = 24
GROUPS = 32


def ahead(block, distance):
    distance = distance % B
    return block if distance == 0 else pltpu.roll(block, B - distance, axis=1)


def ring_of(tables):
    return [0] + list(range(1, tables, 2)) + list(range(tables - 2, 0, -2))


def sends_upper(table):
    return (table == 0) | (table % 2 == 1)


def ring_before(place, tables):
    last = tables - 1
    odd = jnp.where(place == 1, 0, place - 2)
    even = jnp.where(place == last - 1, last, place + 2)
    return jnp.where(place % 2 == 1, odd, even)


def angle(upper_diag, lower_diag, coupling):
    differ = lower_diag - upper_diag
    signs = jnp.where(differ >= 0.0, 1.0, -1.0)
    whole = upper_diag + lower_diag
    denom = jnp.abs(differ) + jnp.sqrt(
        differ * differ + 4.0 * coupling * coupling + 1e-12 * (whole * whole)
    )
    tangent = 2.0 * signs * coupling / denom
    square = 1.0 + tangent * tangent
    guess = lax.rsqrt(square)
    cosines = guess * (1.5 - 0.5 * square * (guess * guess))
    return cosines, tangent * cosines


def turn_both(bands, left, right):
    (c, s), (cd, sd) = left, right
    uu, ul, lu, ll = bands
    top_u = c * uu - s * lu
    top_l = c * ul - s * ll
    low_u = s * uu + c * lu
    low_l = s * ul + c * ll
    return [
        cd * top_u - sd * top_l,
        sd * top_u + cd * top_l,
        cd * low_u - sd * low_l,
        sd * low_u + cd * low_l,
    ]


def spread(value):
    return jnp.broadcast_to(value[:1], (TILE, B))


def behind(value):
    return pltpu.roll(value, 0, axis=1, stride=1, stride_axis=0)


def next_heads(bands, c, s):
    uu, ul, lu, ll = bands
    uu_z, ul_z, lu_z, ll_z = (ahead(v, 1) for v in bands)
    uu_y, ul_y, lu_y, ll_y = (pltpu.roll(v, TILE - 1, axis=0) for v in (uu_z, ul_z, lu_z, ll_z))
    cz, sz = ahead(c, 1), ahead(s, 1)
    head_uu = c * (c * uu - s * lu) - s * (c * ul - s * ll)
    head_ul = c * (sz * uu_y + cz * lu_y) - s * (sz * ul_y + cz * ll_y)
    head_ll = sz * (sz * uu_z + cz * lu_z) + cz * (sz * ul_z + cz * ll_z)
    return head_uu, head_ul, head_ll


def solve(pairs):
    tables = sorted({a for a, _ in pairs})
    first_row = lax.broadcasted_iota(jnp.int32, (TILE, B), 0) == 0
    turns = [[] for _ in tables]
    heads = [(pairs[t, t][0], pairs[t, t][1], pairs[t, t][3]) for t in tables]
    for sweep in range(INNER):
        wide = []
        for t in tables:
            uu, ul, ll = heads[t]
            c, s = angle(uu, ll, ul)
            if sweep < INNER - 1:
                heads[t] = next_heads(pairs[t, t], c, s)
            c, s = spread(c), spread(s)
            turns[t].append((c, s))
            wide.append((behind(c), behind(s)))
        if sweep == INNER - 1 and len(tables) == 1:
            break
        pairs = {
            (a, b): turn_both(bands, turns[a][-1], wide[b]) for (a, b), bands in pairs.items()
        }
        if sweep == INNER - 1:
            break
        for key, (uu, ul, lu, ll) in pairs.items():
            ul = pltpu.roll(ul, 1, axis=0)
            lu = ahead(pltpu.roll(lu, TILE - 1, axis=0), 1)
            pairs[key] = [uu, ul, lu, ahead(ll, 1)]
        for a, b in pairs:
            pairs[a, b][1] = jnp.where(first_row, pairs[b, a][2], pairs[a, b][1])
    return turns, pairs


def turn_tiles(uppers, lowers, turns):
    for sweep, (c, s) in enumerate(turns):
        pairs = list(zip(uppers, lowers))
        uppers = [c * u - s * v for u, v in pairs]
        lowers = [s * u + c * v for u, v in pairs]
        if sweep < INNER - 1:
            lowers = [ahead(v, 1) for v in lowers]
    return uppers, lowers


def mix_tiles(uppers, lowers, turns, lower_wanted):
    uppers, lowers = turn_tiles(uppers, lowers, turns[:-1])
    c, s = turns[-1]
    from_u, from_l = jnp.where(lower_wanted, s, c), jnp.where(lower_wanted, c, -s)
    return [from_u * u + from_l * v for u, v in zip(uppers, lowers)]


def sides(place, tables):
    return place == 0, place == tables - 2


def product_sums(load, height, pairs):
    used = sorted({n for pair in pairs for n in pair})
    totals = {}
    for d in range(REACH + 1):
        kept = [(x, y) for x, y in pairs if d or x <= y or (y, x) not in pairs]
        for start in range(0, height, TILE):
            now = {n: load(n, slice(start, start + TILE)) for n in used}
            then = {n: ahead(v, -d) for n, v in now.items()}
            for x, y in kept:
                term = now[x] * then[y]
                totals[x, y, d] = term if start == 0 else totals[x, y, d] + term
    for x, y in pairs:
        if (x, y, 0) not in totals:
            totals[x, y, 0] = totals[y, x, 0]
    return {key: jnp.sum(total, axis=0, keepdims=True) for key, total in totals.items()}


def put_sums(out_ref, sums, pairs, slot_of):
    for x, y in pairs:
        slot = slot_of(x, y)
        for half in range(2):
            columns = slice(half * (B // 2), (half + 1) * (B // 2))
            for d in range(REACH + 1):
                out_ref[2 * slot + half, d : d + 1, :] = sums[x, y, d][:, columns]


def lags(place, tables):
    odd = place % 2 == 1
    return odd | (place == 0), jnp.logical_not(odd | (place == tables - 2))


def held_bands_kernel(tables, keep_ref, send_ref, late_ref, out_ref):
    lag = lags(lax.axis_index("pair"), tables)
    out_ref[...] = jnp.zeros_like(out_ref)
    height = keep_ref.shape[0]
    for start in range(0, height, TILE):
        rows = slice(start, start + TILE)
        for n, ref in enumerate((keep_ref, send_ref)):
            value = ref[rows, :]
            late_ref[rows, n * B : (n + 1) * B] = jnp.where(lag[n], ahead(value, -LAG), value)

    def load(n, rows):
        return late_ref[rows, n * B : (n + 1) * B]

    pairs = [(x, y) for x in range(2) for y in range(2)]
    put_sums(out_ref, product_sums(load, height, pairs), pairs, lambda x, y: 2 * x + y)


def moved_bands_kernel(tables, late_ref, held_ref, come_ref, next_ref, lined_ref, out_ref):
    place = lax.axis_index("pair")
    odd = place % 2
    lower_sent = ring_before(place, tables) % 2
    own, other = 2 * odd, 2 - 2 * odd
    at = [own + 1 - odd, other + lower_sent, own + odd, other + 1 - lower_sent]
    lag = lags(place, tables)
    out_ref[...] = jnp.zeros_like(out_ref)
    height = come_ref.shape[0]
    columns = [pl.ds(pl.multiple_of(n * B, B), B) for n in at]
    for start in range(0, height, TILE):
        rows = slice(start, start + TILE)
        for n in range(2):
            lined_ref[rows, columns[n]] = late_ref[rows, n * B : (n + 1) * B]
        for n, ref in enumerate((come_ref, next_ref)):
            value = ref[rows, :]
            lined_ref[rows, columns[2 + n]] = jnp.where(lag[n], ahead(value, -LAG), value)

    def load(n, rows):
        return lined_ref[rows, columns[n]]

    def slot_of(x, y):
        return 4 * at[x] + at[y]

    pairs = [(x, y) for x, y in ALL_PAIRS if x > 1 or y > 1]
    put_sums(out_ref, product_sums(load, height, pairs), pairs, slot_of)
    for x in range(2):
        for y in range(2):
            for half in range(2):
                out_ref[2 * slot_of(x, y) + half] = held_ref[2 * (2 * x + y) + half]


def total_kernel(peers, parts_ref, out_ref):
    share = parts_ref.shape[0] // peers
    for part in range(share):
        total = parts_ref[part]
        for peer in range(1, peers):
            total = total + parts_ref[peer * share + part]
        for peer in range(peers):
            out_ref[peer * share + part] = total


def rotate_kernel(tables, sums_ref, lined_ref, keep_out, send_out):
    place = lax.axis_index("pair")
    left_lower, right_upper = sides(place, tables)

    def bands(x, y):
        slot = 4 * x + y
        return jnp.concatenate([sums_ref[2 * slot], sums_ref[2 * slot + 1]], axis=1)

    pairs = {
        (a, b): [bands(2 * a + x, 2 * b + y) for x in range(2) for y in range(2)]
        for a in range(2)
        for b in range(2)
    }
    (left_turns, right_turns), pairs = solve(pairs)
    uu, _, _, ll = pairs[0, 0]
    new_uu = jnp.where(left_lower, ll, uu)
    uu, _, _, ll = pairs[1, 1]
    new_ll = jnp.where(right_upper, uu, ll)
    uu, ul, lu, ll = pairs[0, 1]
    new_ul = jnp.where(
        left_lower, jnp.where(right_upper, lu, ll), jnp.where(right_upper, uu, ul)
    )
    uu, ul, lu, ll = pairs[1, 0]
    new_lu = jnp.where(
        left_lower, jnp.where(right_upper, ul, ll), jnp.where(right_upper, uu, lu)
    )
    (last_turns,), _ = solve({(0, 0): [new_uu, new_ul, new_lu, new_ll]})
    upper_sent = sends_upper(place ^ 1)
    height = keep_out.shape[0]
    groups = [
        [slice(r, r + TILE) for r in range(start, min(start + GROUP * TILE, height), TILE)]
        for start in range(0, height, GROUP * TILE)
    ]
    for n, out_ref, turns, lower_wanted in (
        (0, keep_out, left_turns, left_lower),
        (2, send_out, right_turns, jnp.logical_not(right_upper)),
    ):
        for group in groups:
            uppers = [lined_ref[rows, n * B : (n + 1) * B] for rows in group]
            lowers = [lined_ref[rows, (n + 1) * B : (n + 2) * B] for rows in group]
            for rows, value in zip(group, mix_tiles(uppers, lowers, turns, lower_wanted)):
                out_ref[rows, :] = value
    for group in groups:
        uppers = [keep_out[rows, :] for rows in group]
        lowers = [send_out[rows, :] for rows in group]
        uppers, lowers = turn_tiles(uppers, lowers, last_turns)
        for rows, upper, lower in zip(group, uppers, lowers):
            lower = ahead(lower, -LAG)
            keep_out[rows, :] = jnp.where(upper_sent, lower, upper)
            send_out[rows, :] = jnp.where(upper_sent, upper, lower)


def finish_kernel(keep_ref, come_ref, out_ref, sems):
    keep_at = jnp.where(lax.axis_index("pair") % 2 == 0, B, 0)
    copies = []
    for n, (block_ref, start) in enumerate(((keep_ref, keep_at), (come_ref, B - keep_at))):
        columns = pl.ds(pl.multiple_of(start, B), B)
        copies.append(pltpu.make_async_copy(block_ref, out_ref.at[:, columns], sems.at[n]))
    for copy in copies:
        copy.start()
    for copy in copies:
        copy.wait()


def line_seats(place, tables):
    odd = place % 2 == 1
    before = ring_before(place, tables)
    left, right = jnp.where(odd, before, place), jnp.where(odd, place, before)
    return 2 * left, 2 * left + 1, 2 * right, 2 * right + 1


def wanted_kernel(tables, seating_ref, out_ref):
    place = lax.axis_index("pair")
    lane = lax.broadcasted_iota(jnp.int32, out_ref.shape, 1)
    out = jnp.zeros(out_ref.shape, jnp.int32)
    for n, seat in enumerate(line_seats(place, tables) + line_seats(place ^ 1, tables)):
        out = jnp.where(lane == n, seating_ref[seat], out)
    out_ref[...] = out


def copy_block(tables, block, chosen, put, gathered):
    here_ref, left_ref, right_ref, far_refs = gathered
    chips = tables // 2
    away = (block // 4 - lax.axis_index("pair") // 2 + chips) % chips
    columns = pl.ds(pl.multiple_of((block % 2) * B, B), B)
    height = here_ref.shape[0]
    for distance in range(chips):

        @pl.when(chosen & (away == distance))
        def _():
            for start in range(0, height, TILE):
                rows = slice(start, start + TILE)
                if distance == 2:
                    half = height // 2
                    at = start % half
                    ref, rows_there = far_refs[start // half], slice(at, at + TILE)
                else:
                    ref, rows_there = {0: here_ref, 1: right_ref, 3: left_ref}[distance], rows
                put(rows, ref[rows_there, columns])


def pick_kernel(tables, wanted_ref, here_ref, left_ref, right_ref, *rest):
    far_refs, out_ref = rest[:2], rest[2]
    wanted = wanted_ref[...]
    for n in range(4):

        def put(rows, value, n=n):
            out_ref[rows, n * B : (n + 1) * B] = value

        gathered = (here_ref, left_ref, right_ref, far_refs)
        copy_block(tables, wanted[0, 4 + n], True, put, gathered)


def seated_bands_kernel(tables, wanted_ref, here_ref, left_ref, right_ref, *rest):
    far_refs, (swap_ref, lined_ref, out_ref) = rest[:2], rest[2:]
    place = lax.axis_index("pair")
    wanted = wanted_ref[...]
    height = here_ref.shape[0]
    left_lower, right_upper = sides(place, tables)
    for n in range(4):
        block = wanted[0, n]
        late = left_lower if n < 2 else jnp.logical_not(right_upper)

        def put(rows, value, n=n, late=late):
            lined_ref[rows, n * B : (n + 1) * B] = jnp.where(late, ahead(value, -LAG), value)

        mine = (block // 2) % 2 == place % 2
        copy_block(tables, block, mine, put, (here_ref, left_ref, right_ref, far_refs))

        @pl.when(jnp.logical_not(mine))
        def _():
            for start in range(0, height, TILE):
                rows = slice(start, start + TILE)
                put(rows, swap_ref[rows, n * B : (n + 1) * B])

    def load(n, rows):
        return lined_ref[rows, n * B : (n + 1) * B]

    out_ref[...] = jnp.zeros_like(out_ref)
    sums = product_sums(load, height, ALL_PAIRS)
    put_sums(out_ref, sums, ALL_PAIRS, lambda x, y: 4 * x + y)


VMEM = pl.BlockSpec(memory_space=pltpu.VMEM)
PARAMS = pltpu.CompilerParams(vmem_limit_bytes=32 * 1024 * 1024)


def call(kernel, out_shape, *args):
    outs = [VMEM] * len(out_shape) if isinstance(out_shape, list) else VMEM
    return pl.pallas_call(
        kernel,
        out_shape=out_shape,
        in_specs=[VMEM] * len(args),
        out_specs=outs,
        compiler_params=PARAMS,
    )(*args)


def shape_of(*sizes):
    return jax.ShapeDtypeStruct(sizes, jnp.float32)


def bind(kernel, size):
    def bound(*refs):
        return kernel(size, *refs)

    return bound


def local(matrix, seating):
    height = matrix.shape[0]
    peers = lax.axis_size("row")
    tables = lax.axis_size("pair")
    ring = ring_of(tables)
    hosts = [table ^ 1 for table in ring]
    forward = list(zip(hosts, hosts[1:] + hosts[:1]))
    backward = [(b, a) for a, b in forward]
    up = [(j, (j + 2) % tables) for j in range(tables)]
    down = [(b, a) for a, b in up]
    across = [(j, j ^ 1) for j in range(tables)]
    wanted = pl.pallas_call(
        bind(wanted_kernel, tables),
        out_shape=jax.ShapeDtypeStruct((1, B // 2), jnp.int32),
        in_specs=[pl.BlockSpec(memory_space=pltpu.SMEM)],
        out_specs=VMEM,
        compiler_params=PARAMS,
    )(seating)
    left, right = lax.ppermute(matrix, "pair", up), lax.ppermute(matrix, "pair", down)
    top = lax.ppermute(left[: height // 2], "pair", up)
    bottom = lax.ppermute(right[height // 2 :], "pair", down)
    gathered = [wanted, matrix, left, right, top, bottom]
    swap = call(bind(pick_kernel, tables), shape_of(height, 4 * B), *gathered)
    swap = lax.ppermute(swap, "pair", across)
    lined_shape = shape_of(height, 4 * B)
    spread_shape = shape_of(GROUPS, TILE, B // 2)
    block_shape = shape_of(height, B)
    for pair_of_steps in range(STEPS // 2):
        if pair_of_steps == 0:
            kernel = bind(seated_bands_kernel, tables)
            lined, sums = call(kernel, [lined_shape, spread_shape], *gathered, swap)
        else:
            kernel = bind(moved_bands_kernel, tables)
            lined, sums = call(kernel, [lined_shape, spread_shape], *held)
        sums = lax.all_to_all(sums, "row", 0, 0, tiled=True)
        sums = call(bind(total_kernel, peers), spread_shape, sums)
        sums = lax.all_to_all(sums, "row", 0, 0, tiled=True)
        kernel = bind(rotate_kernel, tables)
        keep, send = call(kernel, [block_shape, block_shape], sums, lined)
        come = lax.ppermute(send, "pair", forward)
        if pair_of_steps < STEPS // 2 - 1:
            near = lax.ppermute(keep, "pair", backward)
            shapes = [shape_of(height, 2 * B), shape_of(TILE, TILE, B // 2)]
            late, local_sums = call(bind(held_bands_kernel, tables), shapes, keep, send)
            held = [late, local_sums, come, near]
    return pl.pallas_call(
        finish_kernel,
        out_shape=shape_of(height, 2 * B),
        in_specs=[VMEM] * 2,
        out_specs=pl.BlockSpec(memory_space=pl.ANY),
        scratch_shapes=[pltpu.SemaphoreType.DMA((2,))],
        compiler_params=PARAMS,
    )(keep, come)


def solution(mesh):
    in_specs = (P("row", "pair"), P())
    out_specs = P("row", "pair")
    return jax.shard_map(local, mesh=mesh, in_specs=in_specs, out_specs=out_specs, check_vma=False)
```

```python
import jax
import jax.numpy as jnp
from jax import lax
from jax.experimental import pallas as pl
from jax.experimental.pallas import tpu as pltpu
from jax.sharding import PartitionSpec as P

B = 256
STEPS = 4
INNER = 4
TILE = 8
REACH = 2 * (INNER - 1)
ALL_PAIRS = [(x, y) for x in range(4) for y in range(4)]
LAG = INNER - 1
GROUP = 24
GROUPS = 32


def ahead(block, distance):
    distance = distance % B
    return block if distance == 0 else pltpu.roll(block, B - distance, axis=1)


def ring_of(tables):
    return [0] + list(range(1, tables, 2)) + list(range(tables - 2, 0, -2))


def sends_upper(table):
    return (table == 0) | (table % 2 == 1)


def ring_before(place, tables):
    last = tables - 1
    odd = jnp.where(place == 1, 0, place - 2)
    even = jnp.where(place == last - 1, last, place + 2)
    return jnp.where(place % 2 == 1, odd, even)


def angle(upper_diag, lower_diag, coupling):
    differ = lower_diag - upper_diag
    signs = jnp.where(differ >= 0.0, 1.0, -1.0)
    whole = upper_diag + lower_diag
    denom = jnp.abs(differ) + jnp.sqrt(
        differ * differ + 4.0 * coupling * coupling + 1e-12 * (whole * whole)
    )
    tangent = 2.0 * signs * coupling / denom
    square = 1.0 + tangent * tangent
    guess = lax.rsqrt(square)
    cosines = guess * (1.5 - 0.5 * square * (guess * guess))
    return cosines, tangent * cosines


def turn_both(bands, left, right):
    (c, s), (cd, sd) = left, right
    uu, ul, lu, ll = bands
    top_u = c * uu - s * lu
    top_l = c * ul - s * ll
    low_u = s * uu + c * lu
    low_l = s * ul + c * ll
    return [
        cd * top_u - sd * top_l,
        sd * top_u + cd * top_l,
        cd * low_u - sd * low_l,
        sd * low_u + cd * low_l,
    ]


def spread(value):
    return jnp.broadcast_to(value[:1], (TILE, B))


def behind(value):
    return pltpu.roll(value, 0, axis=1, stride=1, stride_axis=0)


def next_heads(bands, c, s):
    uu, ul, lu, ll = bands
    uu_z, ul_z, lu_z, ll_z = (ahead(v, 1) for v in bands)
    uu_y, ul_y, lu_y, ll_y = (pltpu.roll(v, TILE - 1, axis=0) for v in (uu_z, ul_z, lu_z, ll_z))
    cz, sz = ahead(c, 1), ahead(s, 1)
    head_uu = c * (c * uu - s * lu) - s * (c * ul - s * ll)
    head_ul = c * (sz * uu_y + cz * lu_y) - s * (sz * ul_y + cz * ll_y)
    head_ll = sz * (sz * uu_z + cz * lu_z) + cz * (sz * ul_z + cz * ll_z)
    return head_uu, head_ul, head_ll


def solve(pairs):
    tables = sorted({a for a, _ in pairs})
    first_row = lax.broadcasted_iota(jnp.int32, (TILE, B), 0) == 0
    turns = [[] for _ in tables]
    heads = [(pairs[t, t][0], pairs[t, t][1], pairs[t, t][3]) for t in tables]
    for sweep in range(INNER):
        wide = []
        for t in tables:
            uu, ul, ll = heads[t]
            c, s = angle(uu, ll, ul)
            if sweep < INNER - 1:
                heads[t] = next_heads(pairs[t, t], c, s)
            c, s = spread(c), spread(s)
            turns[t].append((c, s))
            wide.append((behind(c), behind(s)))
        if sweep == INNER - 1 and len(tables) == 1:
            break
        pairs = {
            (a, b): turn_both(bands, turns[a][-1], wide[b]) for (a, b), bands in pairs.items()
        }
        if sweep == INNER - 1:
            break
        for key, (uu, ul, lu, ll) in pairs.items():
            ul = pltpu.roll(ul, 1, axis=0)
            lu = ahead(pltpu.roll(lu, TILE - 1, axis=0), 1)
            pairs[key] = [uu, ul, lu, ahead(ll, 1)]
        for a, b in pairs:
            pairs[a, b][1] = jnp.where(first_row, pairs[b, a][2], pairs[a, b][1])
    return turns, pairs


def turn_tiles(uppers, lowers, turns):
    for sweep, (c, s) in enumerate(turns):
        pairs = list(zip(uppers, lowers))
        uppers = [c * u - s * v for u, v in pairs]
        lowers = [s * u + c * v for u, v in pairs]
        if sweep < INNER - 1:
            lowers = [ahead(v, 1) for v in lowers]
    return uppers, lowers


def mix_tiles(uppers, lowers, turns, lower_wanted):
    uppers, lowers = turn_tiles(uppers, lowers, turns[:-1])
    c, s = turns[-1]
    from_u, from_l = jnp.where(lower_wanted, s, c), jnp.where(lower_wanted, c, -s)
    return [from_u * u + from_l * v for u, v in zip(uppers, lowers)]


def sides(place, tables):
    return place == 0, place == tables - 2


def product_sums(load, height, pairs):
    used = sorted({n for pair in pairs for n in pair})
    totals = {}
    for d in range(REACH + 1):
        kept = [(x, y) for x, y in pairs if d or x <= y or (y, x) not in pairs]
        for start in range(0, height, TILE):
            now = {n: load(n, slice(start, start + TILE)) for n in used}
            then = {n: ahead(v, -d) for n, v in now.items()}
            for x, y in kept:
                term = now[x] * then[y]
                totals[x, y, d] = term if start == 0 else totals[x, y, d] + term
    for x, y in pairs:
        if (x, y, 0) not in totals:
            totals[x, y, 0] = totals[y, x, 0]
    return {key: jnp.sum(total, axis=0, keepdims=True) for key, total in totals.items()}


def put_sums(out_ref, sums, pairs, slot_of):
    for x, y in pairs:
        slot = slot_of(x, y)
        for half in range(2):
            columns = slice(half * (B // 2), (half + 1) * (B // 2))
            for d in range(REACH + 1):
                out_ref[2 * slot + half, d : d + 1, :] = sums[x, y, d][:, columns]


def lags(place, tables):
    odd = place % 2 == 1
    return odd | (place == 0), jnp.logical_not(odd | (place == tables - 2))


def held_bands_kernel(tables, keep_ref, send_ref, late_ref, out_ref):
    lag = lags(lax.axis_index("pair"), tables)
    out_ref[...] = jnp.zeros_like(out_ref)
    height = keep_ref.shape[0]
    for start in range(0, height, TILE):
        rows = slice(start, start + TILE)
        for n, ref in enumerate((keep_ref, send_ref)):
            value = ref[rows, :]
            late_ref[rows, n * B : (n + 1) * B] = jnp.where(lag[n], ahead(value, -LAG), value)

    def load(n, rows):
        return late_ref[rows, n * B : (n + 1) * B]

    pairs = [(x, y) for x in range(2) for y in range(2)]
    put_sums(out_ref, product_sums(load, height, pairs), pairs, lambda x, y: 2 * x + y)


def moved_bands_kernel(tables, late_ref, held_ref, come_ref, next_ref, lined_ref, out_ref):
    place = lax.axis_index("pair")
    odd = place % 2
    lower_sent = ring_before(place, tables) % 2
    own, other = 2 * odd, 2 - 2 * odd
    at = [own + 1 - odd, other + lower_sent, own + odd, other + 1 - lower_sent]
    lag = lags(place, tables)
    out_ref[...] = jnp.zeros_like(out_ref)
    height = come_ref.shape[0]
    columns = [pl.ds(pl.multiple_of(n * B, B), B) for n in at]
    for start in range(0, height, TILE):
        rows = slice(start, start + TILE)
        for n in range(2):
            lined_ref[rows, columns[n]] = late_ref[rows, n * B : (n + 1) * B]
        for n, ref in enumerate((come_ref, next_ref)):
            value = ref[rows, :]
            lined_ref[rows, columns[2 + n]] = jnp.where(lag[n], ahead(value, -LAG), value)

    def load(n, rows):
        return lined_ref[rows, columns[n]]

    def slot_of(x, y):
        return 4 * at[x] + at[y]

    pairs = [(x, y) for x, y in ALL_PAIRS if x > 1 or y > 1]
    put_sums(out_ref, product_sums(load, height, pairs), pairs, slot_of)
    for x in range(2):
        for y in range(2):
            for half in range(2):
                out_ref[2 * slot_of(x, y) + half] = held_ref[2 * (2 * x + y) + half]


def total_kernel(peers, parts_ref, out_ref):
    share = parts_ref.shape[0] // peers
    for part in range(share):
        total = parts_ref[part]
        for peer in range(1, peers):
            total = total + parts_ref[peer * share + part]
        for peer in range(peers):
            out_ref[peer * share + part] = total


def rotate_kernel(tables, sums_ref, lined_ref, keep_out, send_out):
    place = lax.axis_index("pair")
    left_lower, right_upper = sides(place, tables)

    def bands(x, y):
        slot = 4 * x + y
        return jnp.concatenate([sums_ref[2 * slot], sums_ref[2 * slot + 1]], axis=1)

    pairs = {
        (a, b): [bands(2 * a + x, 2 * b + y) for x in range(2) for y in range(2)]
        for a in range(2)
        for b in range(2)
    }
    (left_turns, right_turns), pairs = solve(pairs)
    uu, _, _, ll = pairs[0, 0]
    new_uu = jnp.where(left_lower, ll, uu)
    uu, _, _, ll = pairs[1, 1]
    new_ll = jnp.where(right_upper, uu, ll)
    uu, ul, lu, ll = pairs[0, 1]
    new_ul = jnp.where(
        left_lower, jnp.where(right_upper, lu, ll), jnp.where(right_upper, uu, ul)
    )
    uu, ul, lu, ll = pairs[1, 0]
    new_lu = jnp.where(
        left_lower, jnp.where(right_upper, ul, ll), jnp.where(right_upper, uu, lu)
    )
    (last_turns,), _ = solve({(0, 0): [new_uu, new_ul, new_lu, new_ll]})
    upper_sent = sends_upper(place ^ 1)
    height = keep_out.shape[0]
    groups = [
        [slice(r, r + TILE) for r in range(start, min(start + GROUP * TILE, height), TILE)]
        for start in range(0, height, GROUP * TILE)
    ]
    for n, out_ref, turns, lower_wanted in (
        (0, keep_out, left_turns, left_lower),
        (2, send_out, right_turns, jnp.logical_not(right_upper)),
    ):
        for group in groups:
            uppers = [lined_ref[rows, n * B : (n + 1) * B] for rows in group]
            lowers = [lined_ref[rows, (n + 1) * B : (n + 2) * B] for rows in group]
            for rows, value in zip(group, mix_tiles(uppers, lowers, turns, lower_wanted)):
                out_ref[rows, :] = value
    for group in groups:
        uppers = [keep_out[rows, :] for rows in group]
        lowers = [send_out[rows, :] for rows in group]
        uppers, lowers = turn_tiles(uppers, lowers, last_turns)
        for rows, upper, lower in zip(group, uppers, lowers):
            lower = ahead(lower, -LAG)
            keep_out[rows, :] = jnp.where(upper_sent, lower, upper)
            send_out[rows, :] = jnp.where(upper_sent, upper, lower)


def finish_kernel(keep_ref, come_ref, out_ref, sems):
    keep_at = jnp.where(lax.axis_index("pair") % 2 == 0, B, 0)
    copies = []
    for n, (block_ref, start) in enumerate(((keep_ref, keep_at), (come_ref, B - keep_at))):
        columns = pl.ds(pl.multiple_of(start, B), B)
        copies.append(pltpu.make_async_copy(block_ref, out_ref.at[:, columns], sems.at[n]))
    for copy in copies:
        copy.start()
    for copy in copies:
        copy.wait()


def line_seats(place, tables):
    odd = place % 2 == 1
    before = ring_before(place, tables)
    left, right = jnp.where(odd, before, place), jnp.where(odd, place, before)
    return 2 * left, 2 * left + 1, 2 * right, 2 * right + 1


def wanted_kernel(tables, seating_ref, out_ref):
    place = lax.axis_index("pair")
    lane = lax.broadcasted_iota(jnp.int32, out_ref.shape, 1)
    out = jnp.zeros(out_ref.shape, jnp.int32)
    for n, seat in enumerate(line_seats(place, tables) + line_seats(place ^ 1, tables)):
        out = jnp.where(lane == n, seating_ref[seat], out)
    out_ref[...] = out


def copy_block(tables, block, chosen, put, gathered):
    chips = tables // 2
    away = (block // 4 - lax.axis_index("pair") // 2 + chips) % chips
    columns = pl.ds(pl.multiple_of((block % 2) * B, B), B)
    half = gathered[0].shape[0]
    for distance in range(chips):

        @pl.when(chosen & (away == distance))
        def _():
            for part in range(2):
                ref = gathered[2 * distance + part]
                for start in range(0, half, TILE):
                    rows = slice(part * half + start, part * half + start + TILE)
                    put(rows, ref[start : start + TILE, columns])


def pick_kernel(tables, wanted_ref, *rest):
    gathered, out_ref = rest[:-1], rest[-1]
    wanted = wanted_ref[...]
    for n in range(4):

        def put(rows, value, n=n):
            out_ref[rows, n * B : (n + 1) * B] = value

        copy_block(tables, wanted[0, 4 + n], True, put, gathered)


def is_here(block):
    return (block // 2) % 2 == lax.axis_index("pair") % 2


def is_late(n, tables):
    left_lower, right_upper = sides(lax.axis_index("pair"), tables)
    return left_lower if n < 2 else jnp.logical_not(right_upper)


def here_kernel(tables, wanted_ref, *rest):
    gathered, out_ref = rest[:-1], rest[-1]
    wanted = wanted_ref[...]
    for n in range(4):
        late = is_late(n, tables)

        def put(rows, value, n=n, late=late):
            out_ref[rows, n * B : (n + 1) * B] = jnp.where(late, ahead(value, -LAG), value)

        copy_block(tables, wanted[0, n], is_here(wanted[0, n]), put, gathered)


def seated_bands_kernel(tables, wanted_ref, here_ref, swap_ref, lined_ref, out_ref):
    wanted = wanted_ref[...]
    height = here_ref.shape[0]
    for n in range(4):
        here, late = is_here(wanted[0, n]), is_late(n, tables)
        columns = slice(n * B, (n + 1) * B)
        for start in range(0, height, TILE):
            rows = slice(start, start + TILE)
            value = swap_ref[rows, columns]
            value = jnp.where(late, ahead(value, -LAG), value)
            lined_ref[rows, columns] = jnp.where(here, here_ref[rows, columns], value)

    def load(n, rows):
        return lined_ref[rows, n * B : (n + 1) * B]

    out_ref[...] = jnp.zeros_like(out_ref)
    sums = product_sums(load, height, ALL_PAIRS)
    put_sums(out_ref, sums, ALL_PAIRS, lambda x, y: 4 * x + y)


VMEM = pl.BlockSpec(memory_space=pltpu.VMEM)
PARAMS = pltpu.CompilerParams(vmem_limit_bytes=32 * 1024 * 1024)


def call(kernel, out_shape, *args):
    outs = [VMEM] * len(out_shape) if isinstance(out_shape, list) else VMEM
    return pl.pallas_call(
        kernel,
        out_shape=out_shape,
        in_specs=[VMEM] * len(args),
        out_specs=outs,
        compiler_params=PARAMS,
    )(*args)


def shape_of(*sizes):
    return jax.ShapeDtypeStruct(sizes, jnp.float32)


def bind(kernel, size):
    def bound(*refs):
        return kernel(size, *refs)

    return bound


def local(matrix, seating):
    height = matrix.shape[0]
    peers = lax.axis_size("row")
    tables = lax.axis_size("pair")
    ring = ring_of(tables)
    hosts = [table ^ 1 for table in ring]
    forward = list(zip(hosts, hosts[1:] + hosts[:1]))
    backward = [(b, a) for a, b in forward]
    up = [(j, (j + 2) % tables) for j in range(tables)]
    down = [(b, a) for a, b in up]
    across = [(j, j ^ 1) for j in range(tables)]
    wanted = pl.pallas_call(
        bind(wanted_kernel, tables),
        out_shape=jax.ShapeDtypeStruct((1, B // 2), jnp.int32),
        in_specs=[pl.BlockSpec(memory_space=pltpu.SMEM)],
        out_specs=VMEM,
        compiler_params=PARAMS,
    )(seating)
    top, bottom = matrix[: height // 2], matrix[height // 2 :]
    left_top = lax.ppermute(top, "pair", up)
    right_bottom = lax.ppermute(bottom, "pair", down)
    left_bottom = lax.ppermute(bottom, "pair", up)
    right_top = lax.ppermute(top, "pair", down)
    far_top = lax.ppermute(left_top, "pair", up)
    far_bottom = lax.ppermute(right_bottom, "pair", down)
    gathered = [wanted, top, bottom, right_top, right_bottom]
    gathered += [far_top, far_bottom, left_top, left_bottom]
    seated_shape = shape_of(height, 4 * B)
    swap = call(bind(pick_kernel, tables), seated_shape, *gathered)
    swap = lax.ppermute(swap, "pair", across)
    here = call(bind(here_kernel, tables), seated_shape, *gathered)
    lined_shape = shape_of(height, 4 * B)
    spread_shape = shape_of(GROUPS, TILE, B // 2)
    block_shape = shape_of(height, B)
    for pair_of_steps in range(STEPS // 2):
        if pair_of_steps == 0:
            kernel = bind(seated_bands_kernel, tables)
            lined, sums = call(kernel, [lined_shape, spread_shape], wanted, here, swap)
        else:
            kernel = bind(moved_bands_kernel, tables)
            lined, sums = call(kernel, [lined_shape, spread_shape], *held)
        sums = lax.all_to_all(sums, "row", 0, 0, tiled=True)
        sums = call(bind(total_kernel, peers), spread_shape, sums)
        sums = lax.all_to_all(sums, "row", 0, 0, tiled=True)
        kernel = bind(rotate_kernel, tables)
        keep, send = call(kernel, [block_shape, block_shape], sums, lined)
        come = lax.ppermute(send, "pair", forward)
        if pair_of_steps < STEPS // 2 - 1:
            near = lax.ppermute(keep, "pair", backward)
            shapes = [shape_of(height, 2 * B), shape_of(TILE, TILE, B // 2)]
            late, local_sums = call(bind(held_bands_kernel, tables), shapes, keep, send)
            held = [late, local_sums, come, near]
    return pl.pallas_call(
        finish_kernel,
        out_shape=shape_of(height, 2 * B),
        in_specs=[VMEM] * 2,
        out_specs=pl.BlockSpec(memory_space=pl.ANY),
        scratch_shapes=[pltpu.SemaphoreType.DMA((2,))],
        compiler_params=PARAMS,
    )(keep, come)


def solution(mesh):
    in_specs = (P("row", "pair"), P())
    out_specs = P("row", "pair")
    return jax.shard_map(local, mesh=mesh, in_specs=in_specs, out_specs=out_specs, check_vma=False)
```

```python
import jax
import jax.numpy as jnp
from jax import lax
from jax.experimental import pallas as pl
from jax.experimental.pallas import tpu as pltpu
from jax.sharding import PartitionSpec as P

B = 256
STEPS = 4
INNER = 4
TILE = 8
REACH = 2 * (INNER - 1)
ALL_PAIRS = [(x, y) for x in range(4) for y in range(4)]
LAG = INNER - 1
GROUP = 24
GROUPS = 32


def ahead(block, distance):
    distance = distance % B
    return block if distance == 0 else pltpu.roll(block, B - distance, axis=1)


def ring_of(tables):
    return [0] + list(range(1, tables, 2)) + list(range(tables - 2, 0, -2))


def sends_upper(table):
    return (table == 0) | (table % 2 == 1)


def ring_before(place, tables):
    last = tables - 1
    odd = jnp.where(place == 1, 0, place - 2)
    even = jnp.where(place == last - 1, last, place + 2)
    return jnp.where(place % 2 == 1, odd, even)


def angle(upper_diag, lower_diag, coupling):
    differ = lower_diag - upper_diag
    signs = jnp.where(differ >= 0.0, 1.0, -1.0)
    whole = upper_diag + lower_diag
    denom = jnp.abs(differ) + jnp.sqrt(
        differ * differ + 4.0 * coupling * coupling + 1e-12 * (whole * whole)
    )
    tangent = 2.0 * signs * coupling / denom
    square = 1.0 + tangent * tangent
    guess = lax.rsqrt(square)
    cosines = guess * (1.5 - 0.5 * square * (guess * guess))
    return cosines, tangent * cosines


def turn_both(bands, left, right):
    (c, s), (cd, sd) = left, right
    uu, ul, lu, ll = bands
    top_u = c * uu - s * lu
    top_l = c * ul - s * ll
    low_u = s * uu + c * lu
    low_l = s * ul + c * ll
    return [
        cd * top_u - sd * top_l,
        sd * top_u + cd * top_l,
        cd * low_u - sd * low_l,
        sd * low_u + cd * low_l,
    ]


def spread(value):
    return jnp.broadcast_to(value[:1], (TILE, B))


def behind(value):
    return pltpu.roll(value, 0, axis=1, stride=1, stride_axis=0)


def next_heads(bands, c, s):
    uu, ul, lu, ll = bands
    uu_z, ul_z, lu_z, ll_z = (ahead(v, 1) for v in bands)
    uu_y, ul_y, lu_y, ll_y = (pltpu.roll(v, TILE - 1, axis=0) for v in (uu_z, ul_z, lu_z, ll_z))
    cz, sz = ahead(c, 1), ahead(s, 1)
    head_uu = c * (c * uu - s * lu) - s * (c * ul - s * ll)
    head_ul = c * (sz * uu_y + cz * lu_y) - s * (sz * ul_y + cz * ll_y)
    head_ll = sz * (sz * uu_z + cz * lu_z) + cz * (sz * ul_z + cz * ll_z)
    return head_uu, head_ul, head_ll


def solve(pairs):
    tables = sorted({a for a, _ in pairs})
    first_row = lax.broadcasted_iota(jnp.int32, (TILE, B), 0) == 0
    turns = [[] for _ in tables]
    heads = [(pairs[t, t][0], pairs[t, t][1], pairs[t, t][3]) for t in tables]
    for sweep in range(INNER):
        wide = []
        for t in tables:
            uu, ul, ll = heads[t]
            c, s = angle(uu, ll, ul)
            if sweep < INNER - 1:
                heads[t] = next_heads(pairs[t, t], c, s)
            c, s = spread(c), spread(s)
            turns[t].append((c, s))
            wide.append((behind(c), behind(s)))
        if sweep == INNER - 1 and len(tables) == 1:
            break
        pairs = {
            (a, b): turn_both(bands, turns[a][-1], wide[b]) for (a, b), bands in pairs.items()
        }
        if sweep == INNER - 1:
            break
        for key, (uu, ul, lu, ll) in pairs.items():
            ul = pltpu.roll(ul, 1, axis=0)
            lu = ahead(pltpu.roll(lu, TILE - 1, axis=0), 1)
            pairs[key] = [uu, ul, lu, ahead(ll, 1)]
        for a, b in pairs:
            pairs[a, b][1] = jnp.where(first_row, pairs[b, a][2], pairs[a, b][1])
    return turns, pairs


def turn_tiles(uppers, lowers, turns):
    for sweep, (c, s) in enumerate(turns):
        pairs = list(zip(uppers, lowers))
        uppers = [c * u - s * v for u, v in pairs]
        lowers = [s * u + c * v for u, v in pairs]
        if sweep < INNER - 1:
            lowers = [ahead(v, 1) for v in lowers]
    return uppers, lowers


def mix_tiles(uppers, lowers, turns, lower_wanted):
    uppers, lowers = turn_tiles(uppers, lowers, turns[:-1])
    c, s = turns[-1]
    from_u, from_l = jnp.where(lower_wanted, s, c), jnp.where(lower_wanted, c, -s)
    return [from_u * u + from_l * v for u, v in zip(uppers, lowers)]


def sides(place, tables):
    return place == 0, place == tables - 2


def product_sums(load, height, pairs):
    used = sorted({n for pair in pairs for n in pair})
    totals = {}
    for d in range(REACH + 1):
        kept = [(x, y) for x, y in pairs if d or x <= y or (y, x) not in pairs]
        for start in range(0, height, TILE):
            now = {n: load(n, slice(start, start + TILE)) for n in used}
            then = {n: ahead(v, -d) for n, v in now.items()}
            for x, y in kept:
                term = now[x] * then[y]
                totals[x, y, d] = term if start == 0 else totals[x, y, d] + term
    for x, y in pairs:
        if (x, y, 0) not in totals:
            totals[x, y, 0] = totals[y, x, 0]
    return {key: jnp.sum(total, axis=0, keepdims=True) for key, total in totals.items()}


def put_sums(out_ref, sums, pairs, slot_of):
    for x, y in pairs:
        slot = slot_of(x, y)
        for half in range(2):
            columns = slice(half * (B // 2), (half + 1) * (B // 2))
            for d in range(REACH + 1):
                out_ref[2 * slot + half, d : d + 1, :] = sums[x, y, d][:, columns]


def lags(place, tables):
    odd = place % 2 == 1
    return odd | (place == 0), jnp.logical_not(odd | (place == tables - 2))


def held_bands_kernel(tables, keep_ref, send_ref, late_ref, out_ref):
    lag = lags(lax.axis_index("pair"), tables)
    out_ref[...] = jnp.zeros_like(out_ref)
    height = keep_ref.shape[0]
    for start in range(0, height, TILE):
        rows = slice(start, start + TILE)
        for n, ref in enumerate((keep_ref, send_ref)):
            value = ref[rows, :]
            late_ref[rows, n * B : (n + 1) * B] = jnp.where(lag[n], ahead(value, -LAG), value)

    def load(n, rows):
        return late_ref[rows, n * B : (n + 1) * B]

    pairs = [(x, y) for x in range(2) for y in range(2)]
    put_sums(out_ref, product_sums(load, height, pairs), pairs, lambda x, y: 2 * x + y)


def moved_bands_kernel(tables, late_ref, held_ref, come_ref, next_ref, lined_ref, out_ref):
    place = lax.axis_index("pair")
    odd = place % 2
    lower_sent = ring_before(place, tables) % 2
    own, other = 2 * odd, 2 - 2 * odd
    at = [own + 1 - odd, other + lower_sent, own + odd, other + 1 - lower_sent]
    lag = lags(place, tables)
    out_ref[...] = jnp.zeros_like(out_ref)
    height = come_ref.shape[0]
    columns = [pl.ds(pl.multiple_of(n * B, B), B) for n in at]
    for start in range(0, height, TILE):
        rows = slice(start, start + TILE)
        for n in range(2):
            lined_ref[rows, columns[n]] = late_ref[rows, n * B : (n + 1) * B]
        for n, ref in enumerate((come_ref, next_ref)):
            value = ref[rows, :]
            lined_ref[rows, columns[2 + n]] = jnp.where(lag[n], ahead(value, -LAG), value)

    def load(n, rows):
        return lined_ref[rows, columns[n]]

    def slot_of(x, y):
        return 4 * at[x] + at[y]

    pairs = [(x, y) for x, y in ALL_PAIRS if x > 1 or y > 1]
    put_sums(out_ref, product_sums(load, height, pairs), pairs, slot_of)
    for x in range(2):
        for y in range(2):
            for half in range(2):
                out_ref[2 * slot_of(x, y) + half] = held_ref[2 * (2 * x + y) + half]


def total_kernel(peers, parts_ref, out_ref):
    share = parts_ref.shape[0] // peers
    for part in range(share):
        total = parts_ref[part]
        for peer in range(1, peers):
            total = total + parts_ref[peer * share + part]
        for peer in range(peers):
            out_ref[peer * share + part] = total


def rotate_kernel(tables, sums_ref, lined_ref, keep_out, send_out):
    place = lax.axis_index("pair")
    left_lower, right_upper = sides(place, tables)

    def bands(x, y):
        slot = 4 * x + y
        return jnp.concatenate([sums_ref[2 * slot], sums_ref[2 * slot + 1]], axis=1)

    pairs = {
        (a, b): [bands(2 * a + x, 2 * b + y) for x in range(2) for y in range(2)]
        for a in range(2)
        for b in range(2)
    }
    (left_turns, right_turns), pairs = solve(pairs)
    uu, _, _, ll = pairs[0, 0]
    new_uu = jnp.where(left_lower, ll, uu)
    uu, _, _, ll = pairs[1, 1]
    new_ll = jnp.where(right_upper, uu, ll)
    uu, ul, lu, ll = pairs[0, 1]
    new_ul = jnp.where(
        left_lower, jnp.where(right_upper, lu, ll), jnp.where(right_upper, uu, ul)
    )
    uu, ul, lu, ll = pairs[1, 0]
    new_lu = jnp.where(
        left_lower, jnp.where(right_upper, ul, ll), jnp.where(right_upper, uu, lu)
    )
    (last_turns,), _ = solve({(0, 0): [new_uu, new_ul, new_lu, new_ll]})
    upper_sent = sends_upper(place ^ 1)
    height = keep_out.shape[0]
    groups = [
        [slice(r, r + TILE) for r in range(start, min(start + GROUP * TILE, height), TILE)]
        for start in range(0, height, GROUP * TILE)
    ]
    for n, out_ref, turns, lower_wanted in (
        (0, keep_out, left_turns, left_lower),
        (2, send_out, right_turns, jnp.logical_not(right_upper)),
    ):
        for group in groups:
            uppers = [lined_ref[rows, n * B : (n + 1) * B] for rows in group]
            lowers = [lined_ref[rows, (n + 1) * B : (n + 2) * B] for rows in group]
            for rows, value in zip(group, mix_tiles(uppers, lowers, turns, lower_wanted)):
                out_ref[rows, :] = value
    for group in groups:
        uppers = [keep_out[rows, :] for rows in group]
        lowers = [send_out[rows, :] for rows in group]
        uppers, lowers = turn_tiles(uppers, lowers, last_turns)
        for rows, upper, lower in zip(group, uppers, lowers):
            lower = ahead(lower, -LAG)
            keep_out[rows, :] = jnp.where(upper_sent, lower, upper)
            send_out[rows, :] = jnp.where(upper_sent, upper, lower)


def finish_kernel(keep_ref, come_ref, out_ref, sems):
    keep_at = jnp.where(lax.axis_index("pair") % 2 == 0, B, 0)
    copies = []
    for n, (block_ref, start) in enumerate(((keep_ref, keep_at), (come_ref, B - keep_at))):
        columns = pl.ds(pl.multiple_of(start, B), B)
        copies.append(pltpu.make_async_copy(block_ref, out_ref.at[:, columns], sems.at[n]))
    for copy in copies:
        copy.start()
    for copy in copies:
        copy.wait()


def line_seats(place, tables):
    odd = place % 2 == 1
    before = ring_before(place, tables)
    left, right = jnp.where(odd, before, place), jnp.where(odd, place, before)
    return 2 * left, 2 * left + 1, 2 * right, 2 * right + 1


def wanted_kernel(tables, seating_ref, out_ref):
    place = lax.axis_index("pair")
    lane = lax.broadcasted_iota(jnp.int32, out_ref.shape, 1)
    out = jnp.zeros(out_ref.shape, jnp.int32)
    for n, seat in enumerate(line_seats(place, tables) + line_seats(place ^ 1, tables)):
        out = jnp.where(lane == n, seating_ref[seat], out)
    out_ref[...] = out


def copy_block(tables, block, chosen, put, gathered):
    chips = tables // 2
    away = (block // 4 - lax.axis_index("pair") // 2 + chips) % chips
    columns = pl.ds(pl.multiple_of((block % 2) * B, B), B)
    half = gathered[0].shape[0]
    for distance in range(chips):

        @pl.when(chosen & (away == distance))
        def _():
            for part in range(2):
                ref = gathered[2 * distance + part]
                for start in range(0, half, TILE):
                    rows = slice(part * half + start, part * half + start + TILE)
                    put(rows, ref[start : start + TILE, columns])


def pick_kernel(tables, wanted_ref, *rest):
    gathered, out_ref = rest[:-1], rest[-1]
    wanted = wanted_ref[...]
    for n in range(4):

        def put(rows, value, n=n):
            out_ref[rows, n * B : (n + 1) * B] = value

        copy_block(tables, wanted[0, 4 + n], True, put, gathered)


def is_here(block):
    return (block // 2) % 2 == lax.axis_index("pair") % 2


def is_late(n, tables):
    left_lower, right_upper = sides(lax.axis_index("pair"), tables)
    return left_lower if n < 2 else jnp.logical_not(right_upper)


def here_kernel(tables, wanted_ref, *rest):
    gathered, out_ref = rest[:-1], rest[-1]
    wanted = wanted_ref[...]
    for n in range(4):
        late = is_late(n, tables)

        def put(rows, value, n=n, late=late):
            out_ref[rows, n * B : (n + 1) * B] = jnp.where(late, ahead(value, -LAG), value)

        copy_block(tables, wanted[0, n], is_here(wanted[0, n]), put, gathered)


def seated_bands_kernel(tables, wanted_ref, here_ref, swap_ref, lined_ref, out_ref):
    wanted = wanted_ref[...]
    height = here_ref.shape[0]
    for n in range(4):
        here, late = is_here(wanted[0, n]), is_late(n, tables)
        columns = slice(n * B, (n + 1) * B)
        for start in range(0, height, TILE):
            rows = slice(start, start + TILE)
            value = swap_ref[rows, columns]
            value = jnp.where(late, ahead(value, -LAG), value)
            lined_ref[rows, columns] = jnp.where(here, here_ref[rows, columns], value)

    def load(n, rows):
        return lined_ref[rows, n * B : (n + 1) * B]

    out_ref[...] = jnp.zeros_like(out_ref)
    sums = product_sums(load, height, ALL_PAIRS)
    put_sums(out_ref, sums, ALL_PAIRS, lambda x, y: 4 * x + y)


VMEM = pl.BlockSpec(memory_space=pltpu.VMEM)
PARAMS = pltpu.CompilerParams(vmem_limit_bytes=32 * 1024 * 1024)


def call(kernel, out_shape, *args):
    outs = [VMEM] * len(out_shape) if isinstance(out_shape, list) else VMEM
    return pl.pallas_call(
        kernel,
        out_shape=out_shape,
        in_specs=[VMEM] * len(args),
        out_specs=outs,
        compiler_params=PARAMS,
    )(*args)


def shape_of(*sizes):
    return jax.ShapeDtypeStruct(sizes, jnp.float32)


def bind(kernel, size):
    def bound(*refs):
        return kernel(size, *refs)

    return bound


def local(matrix, seating):
    height = matrix.shape[0]
    peers = lax.axis_size("row")
    tables = lax.axis_size("pair")
    ring = ring_of(tables)
    hosts = [table ^ 1 for table in ring]
    forward = list(zip(hosts, hosts[1:] + hosts[:1]))
    backward = [(b, a) for a, b in forward]
    up = [(j, (j + 2) % tables) for j in range(tables)]
    down = [(b, a) for a, b in up]
    across = [(j, j ^ 1) for j in range(tables)]
    wanted = pl.pallas_call(
        bind(wanted_kernel, tables),
        out_shape=jax.ShapeDtypeStruct((1, B // 2), jnp.int32),
        in_specs=[pl.BlockSpec(memory_space=pltpu.SMEM)],
        out_specs=VMEM,
        compiler_params=PARAMS,
    )(seating)
    top = matrix[: height // 2]
    bottom = lax.optimization_barrier(matrix)[height // 2 :]
    left_top = lax.ppermute(top, "pair", up)
    right_bottom = lax.ppermute(bottom, "pair", down)
    left_bottom = lax.ppermute(bottom, "pair", up)
    right_top = lax.ppermute(top, "pair", down)
    far_top = lax.ppermute(left_top, "pair", up)
    far_bottom = lax.ppermute(right_bottom, "pair", down)
    gathered = [wanted, top, bottom, right_top, right_bottom]
    gathered += [far_top, far_bottom, left_top, left_bottom]
    seated_shape = shape_of(height, 4 * B)
    swap = call(bind(pick_kernel, tables), seated_shape, *gathered)
    swap = lax.ppermute(swap, "pair", across)
    here = call(bind(here_kernel, tables), seated_shape, *gathered)
    lined_shape = shape_of(height, 4 * B)
    spread_shape = shape_of(GROUPS, TILE, B // 2)
    block_shape = shape_of(height, B)
    for pair_of_steps in range(STEPS // 2):
        if pair_of_steps == 0:
            kernel = bind(seated_bands_kernel, tables)
            lined, sums = call(kernel, [lined_shape, spread_shape], wanted, here, swap)
        else:
            kernel = bind(moved_bands_kernel, tables)
            lined, sums = call(kernel, [lined_shape, spread_shape], *held)
        sums = lax.all_to_all(sums, "row", 0, 0, tiled=True)
        sums = call(bind(total_kernel, peers), spread_shape, sums)
        sums = lax.all_to_all(sums, "row", 0, 0, tiled=True)
        kernel = bind(rotate_kernel, tables)
        keep, send = call(kernel, [block_shape, block_shape], sums, lined)
        come = lax.ppermute(send, "pair", forward)
        if pair_of_steps < STEPS // 2 - 1:
            near = lax.ppermute(keep, "pair", backward)
            shapes = [shape_of(height, 2 * B), shape_of(TILE, TILE, B // 2)]
            late, local_sums = call(bind(held_bands_kernel, tables), shapes, keep, send)
            held = [late, local_sums, come, near]
    return pl.pallas_call(
        finish_kernel,
        out_shape=shape_of(height, 2 * B),
        in_specs=[VMEM] * 2,
        out_specs=pl.BlockSpec(memory_space=pl.ANY),
        scratch_shapes=[pltpu.SemaphoreType.DMA((2,))],
        compiler_params=PARAMS,
    )(keep, come)


def solution(mesh):
    in_specs = (P("row", "pair"), P())
    out_specs = P("row", "pair")
    return jax.shard_map(local, mesh=mesh, in_specs=in_specs, out_specs=out_specs, check_vma=False)
```

```python
import jax
import jax.numpy as jnp
from jax import lax
from jax.experimental import pallas as pl
from jax.experimental.pallas import tpu as pltpu
from jax.sharding import PartitionSpec as P

B = 256
STEPS = 4
INNER = 4
TILE = 8
REACH = 2 * (INNER - 1)
ALL_PAIRS = [(x, y) for x in range(4) for y in range(4)]
LAG = INNER - 1
GROUP = 24
GROUPS = 32


def ahead(block, distance):
    distance = distance % B
    return block if distance == 0 else pltpu.roll(block, B - distance, axis=1)


def ring_of(tables):
    return [0] + list(range(1, tables, 2)) + list(range(tables - 2, 0, -2))


def sends_upper(table):
    return (table == 0) | (table % 2 == 1)


def ring_before(place, tables):
    last = tables - 1
    odd = jnp.where(place == 1, 0, place - 2)
    even = jnp.where(place == last - 1, last, place + 2)
    return jnp.where(place % 2 == 1, odd, even)


def angle(upper_diag, lower_diag, coupling):
    differ = lower_diag - upper_diag
    signs = jnp.where(differ >= 0.0, 1.0, -1.0)
    whole = upper_diag + lower_diag
    denom = jnp.abs(differ) + jnp.sqrt(
        differ * differ + 4.0 * coupling * coupling + 1e-12 * (whole * whole)
    )
    tangent = 2.0 * signs * coupling / denom
    square = 1.0 + tangent * tangent
    guess = lax.rsqrt(square)
    cosines = guess * (1.5 - 0.5 * square * (guess * guess))
    return cosines, tangent * cosines


def turn_both(bands, left, right):
    (c, s), (cd, sd) = left, right
    uu, ul, lu, ll = bands
    top_u = c * uu - s * lu
    top_l = c * ul - s * ll
    low_u = s * uu + c * lu
    low_l = s * ul + c * ll
    return [
        cd * top_u - sd * top_l,
        sd * top_u + cd * top_l,
        cd * low_u - sd * low_l,
        sd * low_u + cd * low_l,
    ]


def spread(value):
    return jnp.broadcast_to(value[:1], (TILE, B))


def behind(value):
    return pltpu.roll(value, 0, axis=1, stride=1, stride_axis=0)


def next_heads(bands, c, s):
    uu, ul, lu, ll = bands
    uu_z, ul_z, lu_z, ll_z = (ahead(v, 1) for v in bands)
    uu_y, ul_y, lu_y, ll_y = (pltpu.roll(v, TILE - 1, axis=0) for v in (uu_z, ul_z, lu_z, ll_z))
    cz, sz = ahead(c, 1), ahead(s, 1)
    head_uu = c * (c * uu - s * lu) - s * (c * ul - s * ll)
    head_ul = c * (sz * uu_y + cz * lu_y) - s * (sz * ul_y + cz * ll_y)
    head_ll = sz * (sz * uu_z + cz * lu_z) + cz * (sz * ul_z + cz * ll_z)
    return head_uu, head_ul, head_ll


def solve(pairs):
    tables = sorted({a for a, _ in pairs})
    first_row = lax.broadcasted_iota(jnp.int32, (TILE, B), 0) == 0
    turns = [[] for _ in tables]
    heads = [(pairs[t, t][0], pairs[t, t][1], pairs[t, t][3]) for t in tables]
    for sweep in range(INNER):
        wide = []
        for t in tables:
            uu, ul, ll = heads[t]
            c, s = angle(uu, ll, ul)
            if sweep < INNER - 1:
                heads[t] = next_heads(pairs[t, t], c, s)
            c, s = spread(c), spread(s)
            turns[t].append((c, s))
            wide.append((behind(c), behind(s)))
        if sweep == INNER - 1 and len(tables) == 1:
            break
        pairs = {
            (a, b): turn_both(bands, turns[a][-1], wide[b]) for (a, b), bands in pairs.items()
        }
        if sweep == INNER - 1:
            break
        for key, (uu, ul, lu, ll) in pairs.items():
            ul = pltpu.roll(ul, 1, axis=0)
            lu = ahead(pltpu.roll(lu, TILE - 1, axis=0), 1)
            pairs[key] = [uu, ul, lu, ahead(ll, 1)]
        for a, b in pairs:
            pairs[a, b][1] = jnp.where(first_row, pairs[b, a][2], pairs[a, b][1])
    return turns, pairs


def turn_tiles(uppers, lowers, turns):
    for sweep, (c, s) in enumerate(turns):
        pairs = list(zip(uppers, lowers))
        uppers = [c * u - s * v for u, v in pairs]
        lowers = [s * u + c * v for u, v in pairs]
        if sweep < INNER - 1:
            lowers = [ahead(v, 1) for v in lowers]
    return uppers, lowers


def mix_tiles(uppers, lowers, turns, lower_wanted):
    uppers, lowers = turn_tiles(uppers, lowers, turns[:-1])
    c, s = turns[-1]
    from_u, from_l = jnp.where(lower_wanted, s, c), jnp.where(lower_wanted, c, -s)
    return [from_u * u + from_l * v for u, v in zip(uppers, lowers)]


def sides(place, tables):
    return place == 0, place == tables - 2


def product_sums(load, height, pairs):
    used = sorted({n for pair in pairs for n in pair})
    totals = {}
    for d in range(REACH + 1):
        kept = [(x, y) for x, y in pairs if d or x <= y or (y, x) not in pairs]
        for start in range(0, height, TILE):
            now = {n: load(n, slice(start, start + TILE)) for n in used}
            then = {n: ahead(v, -d) for n, v in now.items()}
            for x, y in kept:
                term = now[x] * then[y]
                totals[x, y, d] = term if start == 0 else totals[x, y, d] + term
    for x, y in pairs:
        if (x, y, 0) not in totals:
            totals[x, y, 0] = totals[y, x, 0]
    return {key: jnp.sum(total, axis=0, keepdims=True) for key, total in totals.items()}


def put_sums(out_ref, sums, pairs, slot_of):
    for x, y in pairs:
        slot = slot_of(x, y)
        for half in range(2):
            columns = slice(half * (B // 2), (half + 1) * (B // 2))
            for d in range(REACH + 1):
                out_ref[2 * slot + half, d : d + 1, :] = sums[x, y, d][:, columns]


def lags(place, tables):
    odd = place % 2 == 1
    return odd | (place == 0), jnp.logical_not(odd | (place == tables - 2))


def held_bands_kernel(tables, keep_ref, send_ref, late_ref, out_ref):
    lag = lags(lax.axis_index("pair"), tables)
    out_ref[...] = jnp.zeros_like(out_ref)
    height = keep_ref.shape[0]
    for start in range(0, height, TILE):
        rows = slice(start, start + TILE)
        for n, ref in enumerate((keep_ref, send_ref)):
            value = ref[rows, :]
            late_ref[rows, n * B : (n + 1) * B] = jnp.where(lag[n], ahead(value, -LAG), value)

    def load(n, rows):
        return late_ref[rows, n * B : (n + 1) * B]

    pairs = [(x, y) for x in range(2) for y in range(2)]
    put_sums(out_ref, product_sums(load, height, pairs), pairs, lambda x, y: 2 * x + y)


def moved_bands_kernel(tables, late_ref, held_ref, come_ref, next_ref, lined_ref, out_ref):
    place = lax.axis_index("pair")
    odd = place % 2
    lower_sent = ring_before(place, tables) % 2
    own, other = 2 * odd, 2 - 2 * odd
    at = [own + 1 - odd, other + lower_sent, own + odd, other + 1 - lower_sent]
    lag = lags(place, tables)
    out_ref[...] = jnp.zeros_like(out_ref)
    height = come_ref.shape[0]
    columns = [pl.ds(pl.multiple_of(n * B, B), B) for n in at]
    for start in range(0, height, TILE):
        rows = slice(start, start + TILE)
        for n in range(2):
            lined_ref[rows, columns[n]] = late_ref[rows, n * B : (n + 1) * B]
        for n, ref in enumerate((come_ref, next_ref)):
            value = ref[rows, :]
            lined_ref[rows, columns[2 + n]] = jnp.where(lag[n], ahead(value, -LAG), value)

    def load(n, rows):
        return lined_ref[rows, columns[n]]

    def slot_of(x, y):
        return 4 * at[x] + at[y]

    pairs = [(x, y) for x, y in ALL_PAIRS if x > 1 or y > 1]
    put_sums(out_ref, product_sums(load, height, pairs), pairs, slot_of)
    for x in range(2):
        for y in range(2):
            for half in range(2):
                out_ref[2 * slot_of(x, y) + half] = held_ref[2 * (2 * x + y) + half]


def total_kernel(peers, parts_ref, out_ref):
    share = parts_ref.shape[0] // peers
    for part in range(share):
        total = parts_ref[part]
        for peer in range(1, peers):
            total = total + parts_ref[peer * share + part]
        for peer in range(peers):
            out_ref[peer * share + part] = total


def rotate_kernel(tables, sums_ref, lined_ref, keep_out, send_out):
    place = lax.axis_index("pair")
    left_lower, right_upper = sides(place, tables)

    def bands(x, y):
        slot = 4 * x + y
        return jnp.concatenate([sums_ref[2 * slot], sums_ref[2 * slot + 1]], axis=1)

    pairs = {
        (a, b): [bands(2 * a + x, 2 * b + y) for x in range(2) for y in range(2)]
        for a in range(2)
        for b in range(2)
    }
    (left_turns, right_turns), pairs = solve(pairs)
    uu, _, _, ll = pairs[0, 0]
    new_uu = jnp.where(left_lower, ll, uu)
    uu, _, _, ll = pairs[1, 1]
    new_ll = jnp.where(right_upper, uu, ll)
    uu, ul, lu, ll = pairs[0, 1]
    new_ul = jnp.where(
        left_lower, jnp.where(right_upper, lu, ll), jnp.where(right_upper, uu, ul)
    )
    uu, ul, lu, ll = pairs[1, 0]
    new_lu = jnp.where(
        left_lower, jnp.where(right_upper, ul, ll), jnp.where(right_upper, uu, lu)
    )
    (last_turns,), _ = solve({(0, 0): [new_uu, new_ul, new_lu, new_ll]})
    upper_sent = sends_upper(place ^ 1)
    height = keep_out.shape[0]
    groups = [
        [slice(r, r + TILE) for r in range(start, min(start + GROUP * TILE, height), TILE)]
        for start in range(0, height, GROUP * TILE)
    ]
    for n, out_ref, turns, lower_wanted in (
        (0, keep_out, left_turns, left_lower),
        (2, send_out, right_turns, jnp.logical_not(right_upper)),
    ):
        for group in groups:
            uppers = [lined_ref[rows, n * B : (n + 1) * B] for rows in group]
            lowers = [lined_ref[rows, (n + 1) * B : (n + 2) * B] for rows in group]
            for rows, value in zip(group, mix_tiles(uppers, lowers, turns, lower_wanted)):
                out_ref[rows, :] = value
    for group in groups:
        uppers = [keep_out[rows, :] for rows in group]
        lowers = [send_out[rows, :] for rows in group]
        uppers, lowers = turn_tiles(uppers, lowers, last_turns)
        for rows, upper, lower in zip(group, uppers, lowers):
            lower = ahead(lower, -LAG)
            keep_out[rows, :] = jnp.where(upper_sent, lower, upper)
            send_out[rows, :] = jnp.where(upper_sent, upper, lower)


def finish_kernel(keep_ref, come_ref, out_ref, sems):
    keep_at = jnp.where(lax.axis_index("pair") % 2 == 0, B, 0)
    copies = []
    for n, (block_ref, start) in enumerate(((keep_ref, keep_at), (come_ref, B - keep_at))):
        columns = pl.ds(pl.multiple_of(start, B), B)
        copies.append(pltpu.make_async_copy(block_ref, out_ref.at[:, columns], sems.at[n]))
    for copy in copies:
        copy.start()
    for copy in copies:
        copy.wait()


def line_seats(place, tables):
    odd = place % 2 == 1
    before = ring_before(place, tables)
    left, right = jnp.where(odd, before, place), jnp.where(odd, place, before)
    return 2 * left, 2 * left + 1, 2 * right, 2 * right + 1


def wanted_kernel(tables, seating_ref, out_ref):
    place = lax.axis_index("pair")
    lane = lax.broadcasted_iota(jnp.int32, out_ref.shape, 1)
    out = jnp.zeros(out_ref.shape, jnp.int32)
    for n, seat in enumerate(line_seats(place, tables) + line_seats(place ^ 1, tables)):
        out = jnp.where(lane == n, seating_ref[seat], out)
    out_ref[...] = out


def split_kernel(matrix_ref, top_ref, bottom_ref):
    half = top_ref.shape[0]
    top_ref[...] = matrix_ref[:half, :]
    bottom_ref[...] = matrix_ref[half:, :]


def chips_away(block, tables):
    chips = tables // 2
    return (block // 4 - lax.axis_index("pair") // 2 + chips) % chips


def block_columns(block):
    return pl.ds(pl.multiple_of((block % 2) * B, B), B)


def copy_block(tables, block, chosen, put, gathered):
    away = chips_away(block, tables)
    columns = block_columns(block)
    half = gathered[0].shape[0]
    for n in range(len(gathered) // 2):
        distance = (0, 1, 3, 2)[n]

        @pl.when(chosen & (away == distance))
        def _():
            for part in range(2):
                ref = gathered[2 * n + part]
                for start in range(0, half, TILE):
                    rows = slice(part * half + start, part * half + start + TILE)
                    put(rows, ref[start : start + TILE, columns])


def pick_near_kernel(tables, wanted_ref, *rest):
    gathered, out_ref = rest[:-1], rest[-1]
    wanted = wanted_ref[...]
    for n in range(4):

        def put(rows, value, n=n):
            out_ref[rows, n * B : (n + 1) * B] = value

        copy_block(tables, wanted[0, 4 + n], True, put, gathered)


def pick_far_kernel(tables, wanted_ref, near_ref, top_ref, bottom_ref, out_ref):
    wanted = wanted_ref[...]
    half = top_ref.shape[0]
    for n in range(4):
        block = wanted[0, 4 + n]
        far = chips_away(block, tables) == 2
        columns = block_columns(block)
        at = slice(n * B, (n + 1) * B)
        for part, ref in enumerate((top_ref, bottom_ref)):
            for start in range(0, half, TILE):
                rows = slice(part * half + start, part * half + start + TILE)
                value = ref[start : start + TILE, columns]
                out_ref[rows, at] = jnp.where(far, value, near_ref[rows, at])


def is_here(block):
    return (block // 2) % 2 == lax.axis_index("pair") % 2


def is_late(n, tables):
    left_lower, right_upper = sides(lax.axis_index("pair"), tables)
    return left_lower if n < 2 else jnp.logical_not(right_upper)


def here_kernel(tables, wanted_ref, *rest):
    gathered, out_ref = rest[:-1], rest[-1]
    wanted = wanted_ref[...]
    for n in range(4):
        late = is_late(n, tables)

        def put(rows, value, n=n, late=late):
            out_ref[rows, n * B : (n + 1) * B] = jnp.where(late, ahead(value, -LAG), value)

        copy_block(tables, wanted[0, n], is_here(wanted[0, n]), put, gathered)


def seated_bands_kernel(tables, wanted_ref, here_ref, swap_ref, lined_ref, out_ref):
    wanted = wanted_ref[...]
    height = here_ref.shape[0]
    for n in range(4):
        here, late = is_here(wanted[0, n]), is_late(n, tables)
        columns = slice(n * B, (n + 1) * B)
        for start in range(0, height, TILE):
            rows = slice(start, start + TILE)
            value = swap_ref[rows, columns]
            value = jnp.where(late, ahead(value, -LAG), value)
            lined_ref[rows, columns] = jnp.where(here, here_ref[rows, columns], value)

    def load(n, rows):
        return lined_ref[rows, n * B : (n + 1) * B]

    out_ref[...] = jnp.zeros_like(out_ref)
    sums = product_sums(load, height, ALL_PAIRS)
    put_sums(out_ref, sums, ALL_PAIRS, lambda x, y: 4 * x + y)


VMEM = pl.BlockSpec(memory_space=pltpu.VMEM)
PARAMS = pltpu.CompilerParams(vmem_limit_bytes=32 * 1024 * 1024)


def call(kernel, out_shape, *args):
    outs = [VMEM] * len(out_shape) if isinstance(out_shape, list) else VMEM
    return pl.pallas_call(
        kernel,
        out_shape=out_shape,
        in_specs=[VMEM] * len(args),
        out_specs=outs,
        compiler_params=PARAMS,
    )(*args)


def shape_of(*sizes):
    return jax.ShapeDtypeStruct(sizes, jnp.float32)


def bind(kernel, size):
    def bound(*refs):
        return kernel(size, *refs)

    return bound


def local(matrix, seating):
    height = matrix.shape[0]
    peers = lax.axis_size("row")
    tables = lax.axis_size("pair")
    ring = ring_of(tables)
    hosts = [table ^ 1 for table in ring]
    forward = list(zip(hosts, hosts[1:] + hosts[:1]))
    backward = [(b, a) for a, b in forward]
    up = [(j, (j + 2) % tables) for j in range(tables)]
    down = [(b, a) for a, b in up]
    across = [(j, j ^ 1) for j in range(tables)]
    wanted = pl.pallas_call(
        bind(wanted_kernel, tables),
        out_shape=jax.ShapeDtypeStruct((1, B // 2), jnp.int32),
        in_specs=[pl.BlockSpec(memory_space=pltpu.SMEM)],
        out_specs=VMEM,
        compiler_params=PARAMS,
    )(seating)
    top, bottom = call(split_kernel, [shape_of(height // 2, 2 * B)] * 2, matrix)
    left_top = lax.ppermute(top, "pair", up)
    right_bottom = lax.ppermute(bottom, "pair", down)
    left_bottom = lax.ppermute(bottom, "pair", up)
    right_top = lax.ppermute(top, "pair", down)
    far_top = lax.ppermute(left_top, "pair", up)
    far_bottom = lax.ppermute(right_bottom, "pair", down)
    near = [wanted, top, bottom, right_top, right_bottom, left_top, left_bottom]
    far = [far_top, far_bottom]
    seated_shape = shape_of(height, 4 * B)
    swap = call(bind(pick_near_kernel, tables), seated_shape, *near)
    swap = call(bind(pick_far_kernel, tables), seated_shape, wanted, swap, *far)
    swap = lax.ppermute(swap, "pair", across)
    here = call(bind(here_kernel, tables), seated_shape, *near, *far)
    lined_shape = shape_of(height, 4 * B)
    spread_shape = shape_of(GROUPS, TILE, B // 2)
    block_shape = shape_of(height, B)
    for pair_of_steps in range(STEPS // 2):
        if pair_of_steps == 0:
            kernel = bind(seated_bands_kernel, tables)
            lined, sums = call(kernel, [lined_shape, spread_shape], wanted, here, swap)
        else:
            kernel = bind(moved_bands_kernel, tables)
            lined, sums = call(kernel, [lined_shape, spread_shape], *held)
        sums = lax.all_to_all(sums, "row", 0, 0, tiled=True)
        sums = call(bind(total_kernel, peers), spread_shape, sums)
        sums = lax.all_to_all(sums, "row", 0, 0, tiled=True)
        kernel = bind(rotate_kernel, tables)
        keep, send = call(kernel, [block_shape, block_shape], sums, lined)
        come = lax.ppermute(send, "pair", forward)
        if pair_of_steps < STEPS // 2 - 1:
            near = lax.ppermute(keep, "pair", backward)
            shapes = [shape_of(height, 2 * B), shape_of(TILE, TILE, B // 2)]
            late, local_sums = call(bind(held_bands_kernel, tables), shapes, keep, send)
            held = [late, local_sums, come, near]
    return pl.pallas_call(
        finish_kernel,
        out_shape=shape_of(height, 2 * B),
        in_specs=[VMEM] * 2,
        out_specs=pl.BlockSpec(memory_space=pl.ANY),
        scratch_shapes=[pltpu.SemaphoreType.DMA((2,))],
        compiler_params=PARAMS,
    )(keep, come)


def solution(mesh):
    in_specs = (P("row", "pair"), P())
    out_specs = P("row", "pair")
    return jax.shard_map(local, mesh=mesh, in_specs=in_specs, out_specs=out_specs, check_vma=False)
```

```python
import jax
import jax.numpy as jnp
from jax import lax
from jax.experimental import pallas as pl
from jax.experimental.pallas import tpu as pltpu
from jax.sharding import PartitionSpec as P

B = 256
STEPS = 4
INNER = 4
TILE = 8
REACH = 2 * (INNER - 1)
ALL_PAIRS = [(x, y) for x in range(4) for y in range(4)]
LAG = INNER - 1
GROUP = 24
GROUPS = 32


def ahead(block, distance):
    distance = distance % B
    return block if distance == 0 else pltpu.roll(block, B - distance, axis=1)


def ring_of(tables):
    return [0] + list(range(1, tables, 2)) + list(range(tables - 2, 0, -2))


def sends_upper(table):
    return (table == 0) | (table % 2 == 1)


def ring_before(place, tables):
    last = tables - 1
    odd = jnp.where(place == 1, 0, place - 2)
    even = jnp.where(place == last - 1, last, place + 2)
    return jnp.where(place % 2 == 1, odd, even)


def angle(upper_diag, lower_diag, coupling):
    differ = lower_diag - upper_diag
    signs = jnp.where(differ >= 0.0, 1.0, -1.0)
    whole = upper_diag + lower_diag
    denom = jnp.abs(differ) + jnp.sqrt(
        differ * differ + 4.0 * coupling * coupling + 1e-12 * (whole * whole)
    )
    tangent = 2.0 * signs * coupling / denom
    square = 1.0 + tangent * tangent
    guess = lax.rsqrt(square)
    cosines = guess * (1.5 - 0.5 * square * (guess * guess))
    return cosines, tangent * cosines


def turn_both(bands, left, right):
    (c, s), (cd, sd) = left, right
    uu, ul, lu, ll = bands
    top_u = c * uu - s * lu
    top_l = c * ul - s * ll
    low_u = s * uu + c * lu
    low_l = s * ul + c * ll
    return [
        cd * top_u - sd * top_l,
        sd * top_u + cd * top_l,
        cd * low_u - sd * low_l,
        sd * low_u + cd * low_l,
    ]


def spread(value):
    return jnp.broadcast_to(value[:1], (TILE, B))


def behind(value):
    return pltpu.roll(value, 0, axis=1, stride=1, stride_axis=0)


def next_heads(bands, c, s):
    uu, ul, lu, ll = bands
    uu_z, ul_z, lu_z, ll_z = (ahead(v, 1) for v in bands)
    uu_y, ul_y, lu_y, ll_y = (pltpu.roll(v, TILE - 1, axis=0) for v in (uu_z, ul_z, lu_z, ll_z))
    cz, sz = ahead(c, 1), ahead(s, 1)
    head_uu = c * (c * uu - s * lu) - s * (c * ul - s * ll)
    head_ul = c * (sz * uu_y + cz * lu_y) - s * (sz * ul_y + cz * ll_y)
    head_ll = sz * (sz * uu_z + cz * lu_z) + cz * (sz * ul_z + cz * ll_z)
    return head_uu, head_ul, head_ll


def solve(pairs):
    tables = sorted({a for a, _ in pairs})
    first_row = lax.broadcasted_iota(jnp.int32, (TILE, B), 0) == 0
    turns = [[] for _ in tables]
    heads = [(pairs[t, t][0], pairs[t, t][1], pairs[t, t][3]) for t in tables]
    for sweep in range(INNER):
        wide = []
        for t in tables:
            uu, ul, ll = heads[t]
            c, s = angle(uu, ll, ul)
            if sweep < INNER - 1:
                heads[t] = next_heads(pairs[t, t], c, s)
            c, s = spread(c), spread(s)
            turns[t].append((c, s))
            wide.append((behind(c), behind(s)))
        if sweep == INNER - 1 and len(tables) == 1:
            break
        pairs = {
            (a, b): turn_both(bands, turns[a][-1], wide[b]) for (a, b), bands in pairs.items()
        }
        if sweep == INNER - 1:
            break
        for key, (uu, ul, lu, ll) in pairs.items():
            ul = pltpu.roll(ul, 1, axis=0)
            lu = ahead(pltpu.roll(lu, TILE - 1, axis=0), 1)
            pairs[key] = [uu, ul, lu, ahead(ll, 1)]
        for a, b in pairs:
            pairs[a, b][1] = jnp.where(first_row, pairs[b, a][2], pairs[a, b][1])
    return turns, pairs


def turn_tiles(uppers, lowers, turns):
    for sweep, (c, s) in enumerate(turns):
        pairs = list(zip(uppers, lowers))
        uppers = [c * u - s * v for u, v in pairs]
        lowers = [s * u + c * v for u, v in pairs]
        if sweep < INNER - 1:
            lowers = [ahead(v, 1) for v in lowers]
    return uppers, lowers


def mix_tiles(uppers, lowers, turns, lower_wanted):
    uppers, lowers = turn_tiles(uppers, lowers, turns[:-1])
    c, s = turns[-1]
    from_u, from_l = jnp.where(lower_wanted, s, c), jnp.where(lower_wanted, c, -s)
    return [from_u * u + from_l * v for u, v in zip(uppers, lowers)]


def sides(place, tables):
    return place == 0, place == tables - 2


def product_sums(load, height, pairs):
    used = sorted({n for pair in pairs for n in pair})
    totals = {}
    for d in range(REACH + 1):
        kept = [(x, y) for x, y in pairs if d or x <= y or (y, x) not in pairs]
        for start in range(0, height, TILE):
            now = {n: load(n, slice(start, start + TILE)) for n in used}
            then = {n: ahead(v, -d) for n, v in now.items()}
            for x, y in kept:
                term = now[x] * then[y]
                totals[x, y, d] = term if start == 0 else totals[x, y, d] + term
    for x, y in pairs:
        if (x, y, 0) not in totals:
            totals[x, y, 0] = totals[y, x, 0]
    return {key: jnp.sum(total, axis=0, keepdims=True) for key, total in totals.items()}


def put_sums(out_ref, sums, pairs, slot_of):
    for x, y in pairs:
        slot = slot_of(x, y)
        for half in range(2):
            columns = slice(half * (B // 2), (half + 1) * (B // 2))
            for d in range(REACH + 1):
                out_ref[2 * slot + half, d : d + 1, :] = sums[x, y, d][:, columns]


def lags(place, tables):
    odd = place % 2 == 1
    return odd | (place == 0), jnp.logical_not(odd | (place == tables - 2))


def held_bands_kernel(tables, keep_ref, send_ref, late_ref, out_ref):
    lag = lags(lax.axis_index("pair"), tables)
    out_ref[...] = jnp.zeros_like(out_ref)
    height = keep_ref.shape[0]
    for start in range(0, height, TILE):
        rows = slice(start, start + TILE)
        for n, ref in enumerate((keep_ref, send_ref)):
            value = ref[rows, :]
            late_ref[rows, n * B : (n + 1) * B] = jnp.where(lag[n], ahead(value, -LAG), value)

    def load(n, rows):
        return late_ref[rows, n * B : (n + 1) * B]

    pairs = [(x, y) for x in range(2) for y in range(2)]
    put_sums(out_ref, product_sums(load, height, pairs), pairs, lambda x, y: 2 * x + y)


def moved_bands_kernel(tables, late_ref, held_ref, come_ref, next_ref, lined_ref, out_ref):
    place = lax.axis_index("pair")
    odd = place % 2
    lower_sent = ring_before(place, tables) % 2
    own, other = 2 * odd, 2 - 2 * odd
    at = [own + 1 - odd, other + lower_sent, own + odd, other + 1 - lower_sent]
    lag = lags(place, tables)
    out_ref[...] = jnp.zeros_like(out_ref)
    height = come_ref.shape[0]
    columns = [pl.ds(pl.multiple_of(n * B, B), B) for n in at]
    for start in range(0, height, TILE):
        rows = slice(start, start + TILE)
        for n in range(2):
            lined_ref[rows, columns[n]] = late_ref[rows, n * B : (n + 1) * B]
        for n, ref in enumerate((come_ref, next_ref)):
            value = ref[rows, :]
            lined_ref[rows, columns[2 + n]] = jnp.where(lag[n], ahead(value, -LAG), value)

    def load(n, rows):
        return lined_ref[rows, columns[n]]

    def slot_of(x, y):
        return 4 * at[x] + at[y]

    pairs = [(x, y) for x, y in ALL_PAIRS if x > 1 or y > 1]
    put_sums(out_ref, product_sums(load, height, pairs), pairs, slot_of)
    for x in range(2):
        for y in range(2):
            for half in range(2):
                out_ref[2 * slot_of(x, y) + half] = held_ref[2 * (2 * x + y) + half]


def total_kernel(peers, parts_ref, out_ref):
    share = parts_ref.shape[0] // peers
    for part in range(share):
        total = parts_ref[part]
        for peer in range(1, peers):
            total = total + parts_ref[peer * share + part]
        for peer in range(peers):
            out_ref[peer * share + part] = total


def rotate_kernel(tables, sums_ref, lined_ref, keep_out, send_out):
    place = lax.axis_index("pair")
    left_lower, right_upper = sides(place, tables)

    def bands(x, y):
        slot = 4 * x + y
        return jnp.concatenate([sums_ref[2 * slot], sums_ref[2 * slot + 1]], axis=1)

    pairs = {
        (a, b): [bands(2 * a + x, 2 * b + y) for x in range(2) for y in range(2)]
        for a in range(2)
        for b in range(2)
    }
    (left_turns, right_turns), pairs = solve(pairs)
    uu, _, _, ll = pairs[0, 0]
    new_uu = jnp.where(left_lower, ll, uu)
    uu, _, _, ll = pairs[1, 1]
    new_ll = jnp.where(right_upper, uu, ll)
    uu, ul, lu, ll = pairs[0, 1]
    new_ul = jnp.where(
        left_lower, jnp.where(right_upper, lu, ll), jnp.where(right_upper, uu, ul)
    )
    uu, ul, lu, ll = pairs[1, 0]
    new_lu = jnp.where(
        left_lower, jnp.where(right_upper, ul, ll), jnp.where(right_upper, uu, lu)
    )
    (last_turns,), _ = solve({(0, 0): [new_uu, new_ul, new_lu, new_ll]})
    upper_sent = sends_upper(place ^ 1)
    height = keep_out.shape[0]
    groups = [
        [slice(r, r + TILE) for r in range(start, min(start + GROUP * TILE, height), TILE)]
        for start in range(0, height, GROUP * TILE)
    ]
    for n, out_ref, turns, lower_wanted in (
        (0, keep_out, left_turns, left_lower),
        (2, send_out, right_turns, jnp.logical_not(right_upper)),
    ):
        for group in groups:
            uppers = [lined_ref[rows, n * B : (n + 1) * B] for rows in group]
            lowers = [lined_ref[rows, (n + 1) * B : (n + 2) * B] for rows in group]
            for rows, value in zip(group, mix_tiles(uppers, lowers, turns, lower_wanted)):
                out_ref[rows, :] = value
    for group in groups:
        uppers = [keep_out[rows, :] for rows in group]
        lowers = [send_out[rows, :] for rows in group]
        uppers, lowers = turn_tiles(uppers, lowers, last_turns)
        for rows, upper, lower in zip(group, uppers, lowers):
            lower = ahead(lower, -LAG)
            keep_out[rows, :] = jnp.where(upper_sent, lower, upper)
            send_out[rows, :] = jnp.where(upper_sent, upper, lower)


def finish_kernel(keep_ref, come_ref, out_ref, sems):
    keep_at = jnp.where(lax.axis_index("pair") % 2 == 0, B, 0)
    copies = []
    for n, (block_ref, start) in enumerate(((keep_ref, keep_at), (come_ref, B - keep_at))):
        columns = pl.ds(pl.multiple_of(start, B), B)
        copies.append(pltpu.make_async_copy(block_ref, out_ref.at[:, columns], sems.at[n]))
    for copy in copies:
        copy.start()
    for copy in copies:
        copy.wait()


def line_seats(place, tables):
    odd = place % 2 == 1
    before = ring_before(place, tables)
    left, right = jnp.where(odd, before, place), jnp.where(odd, place, before)
    return 2 * left, 2 * left + 1, 2 * right, 2 * right + 1


def wanted_kernel(tables, seating_ref, out_ref):
    place = lax.axis_index("pair")
    lane = lax.broadcasted_iota(jnp.int32, out_ref.shape, 1)
    out = jnp.zeros(out_ref.shape, jnp.int32)
    for n, seat in enumerate(line_seats(place, tables) + line_seats(place ^ 1, tables)):
        out = jnp.where(lane == n, seating_ref[seat], out)
    out_ref[...] = out


def split_kernel(matrix_ref, top_ref, bottom_ref):
    half = top_ref.shape[0]
    top_ref[...] = matrix_ref[:half, :]
    bottom_ref[...] = matrix_ref[half:, :]


def chips_away(block, tables):
    chips = tables // 2
    return (block // 4 - lax.axis_index("pair") // 2 + chips) % chips


def block_columns(block):
    return pl.ds(pl.multiple_of((block % 2) * B, B), B)


def copy_block(tables, block, chosen, put, gathered):
    away = chips_away(block, tables)
    columns = block_columns(block)
    half = gathered[0].shape[0]
    for n in range(len(gathered) // 2):
        distance = (0, 1, 3, 2)[n]

        @pl.when(chosen & (away == distance))
        def _():
            for part in range(2):
                ref = gathered[2 * n + part]
                for start in range(0, half, TILE):
                    rows = slice(part * half + start, part * half + start + TILE)
                    put(rows, ref[start : start + TILE, columns])


def pick_near_kernel(tables, wanted_ref, *rest):
    gathered, out_ref = rest[:-1], rest[-1]
    wanted = wanted_ref[...]
    for n in range(4):

        def put(rows, value, n=n):
            out_ref[rows, n * B : (n + 1) * B] = value

        copy_block(tables, wanted[0, 4 + n], True, put, gathered)


def pick_far_kernel(tables, wanted_ref, near_ref, top_ref, bottom_ref, out_ref):
    wanted = wanted_ref[...]
    half = top_ref.shape[0]
    for n in range(4):
        block = wanted[0, 4 + n]
        far = chips_away(block, tables) == 2
        columns = block_columns(block)
        at = slice(n * B, (n + 1) * B)
        for part, ref in enumerate((top_ref, bottom_ref)):
            for start in range(0, half, TILE):
                rows = slice(part * half + start, part * half + start + TILE)
                value = ref[start : start + TILE, columns]
                out_ref[rows, at] = jnp.where(far, value, near_ref[rows, at])


def is_here(block):
    return (block // 2) % 2 == lax.axis_index("pair") % 2


def is_late(n, tables):
    left_lower, right_upper = sides(lax.axis_index("pair"), tables)
    return left_lower if n < 2 else jnp.logical_not(right_upper)


def here_kernel(tables, wanted_ref, *rest):
    gathered, out_ref = rest[:-1], rest[-1]
    wanted = wanted_ref[...]
    for n in range(4):
        late = is_late(n, tables)

        def put(rows, value, n=n, late=late):
            out_ref[rows, n * B : (n + 1) * B] = jnp.where(late, ahead(value, -LAG), value)

        copy_block(tables, wanted[0, n], is_here(wanted[0, n]), put, gathered)


def seated_bands_kernel(tables, wanted_ref, here_ref, swap_ref, lined_ref, out_ref):
    wanted = wanted_ref[...]
    height = here_ref.shape[0]
    for n in range(4):
        here, late = is_here(wanted[0, n]), is_late(n, tables)
        columns = slice(n * B, (n + 1) * B)
        for start in range(0, height, TILE):
            rows = slice(start, start + TILE)
            value = swap_ref[rows, columns]
            value = jnp.where(late, ahead(value, -LAG), value)
            lined_ref[rows, columns] = jnp.where(here, here_ref[rows, columns], value)

    def load(n, rows):
        return lined_ref[rows, n * B : (n + 1) * B]

    out_ref[...] = jnp.zeros_like(out_ref)
    sums = product_sums(load, height, ALL_PAIRS)
    put_sums(out_ref, sums, ALL_PAIRS, lambda x, y: 4 * x + y)


VMEM = pl.BlockSpec(memory_space=pltpu.VMEM)
PARAMS = pltpu.CompilerParams(vmem_limit_bytes=32 * 1024 * 1024)


def call(kernel, out_shape, *args):
    outs = [VMEM] * len(out_shape) if isinstance(out_shape, list) else VMEM
    return pl.pallas_call(
        kernel,
        out_shape=out_shape,
        in_specs=[VMEM] * len(args),
        out_specs=outs,
        compiler_params=PARAMS,
    )(*args)


def shape_of(*sizes):
    return jax.ShapeDtypeStruct(sizes, jnp.float32)


def bind(kernel, size):
    def bound(*refs):
        return kernel(size, *refs)

    return bound


def local(matrix, seating):
    height = matrix.shape[0]
    peers = lax.axis_size("row")
    tables = lax.axis_size("pair")
    ring = ring_of(tables)
    hosts = [table ^ 1 for table in ring]
    forward = list(zip(hosts, hosts[1:] + hosts[:1]))
    backward = [(b, a) for a, b in forward]
    up = [(j, (j + 2) % tables) for j in range(tables)]
    down = [(b, a) for a, b in up]
    across = [(j, j ^ 1) for j in range(tables)]
    wanted = pl.pallas_call(
        bind(wanted_kernel, tables),
        out_shape=jax.ShapeDtypeStruct((1, B // 2), jnp.int32),
        in_specs=[pl.BlockSpec(memory_space=pltpu.SMEM)],
        out_specs=VMEM,
        compiler_params=PARAMS,
    )(seating)
    top, bottom = call(split_kernel, [shape_of(height // 2, 2 * B)] * 2, matrix)
    left_top = lax.ppermute(top, "pair", up)
    right_bottom = lax.ppermute(bottom, "pair", down)
    later_top, later_bottom, wanted = lax.optimization_barrier((top, bottom, wanted))
    left_bottom = lax.ppermute(later_bottom, "pair", up)
    right_top = lax.ppermute(later_top, "pair", down)
    far_top = lax.ppermute(left_top, "pair", up)
    far_bottom = lax.ppermute(right_bottom, "pair", down)
    near = [wanted, top, bottom, right_top, right_bottom, left_top, left_bottom]
    far = [far_top, far_bottom]
    seated_shape = shape_of(height, 4 * B)
    swap = call(bind(pick_near_kernel, tables), seated_shape, *near)
    swap = call(bind(pick_far_kernel, tables), seated_shape, wanted, swap, *far)
    swap = lax.ppermute(swap, "pair", across)
    here = call(bind(here_kernel, tables), seated_shape, *near, *far)
    lined_shape = shape_of(height, 4 * B)
    spread_shape = shape_of(GROUPS, TILE, B // 2)
    block_shape = shape_of(height, B)
    for pair_of_steps in range(STEPS // 2):
        if pair_of_steps == 0:
            kernel = bind(seated_bands_kernel, tables)
            lined, sums = call(kernel, [lined_shape, spread_shape], wanted, here, swap)
        else:
            kernel = bind(moved_bands_kernel, tables)
            lined, sums = call(kernel, [lined_shape, spread_shape], *held)
        sums = lax.all_to_all(sums, "row", 0, 0, tiled=True)
        sums = call(bind(total_kernel, peers), spread_shape, sums)
        sums = lax.all_to_all(sums, "row", 0, 0, tiled=True)
        kernel = bind(rotate_kernel, tables)
        keep, send = call(kernel, [block_shape, block_shape], sums, lined)
        come = lax.ppermute(send, "pair", forward)
        if pair_of_steps < STEPS // 2 - 1:
            near = lax.ppermute(keep, "pair", backward)
            shapes = [shape_of(height, 2 * B), shape_of(TILE, TILE, B // 2)]
            late, local_sums = call(bind(held_bands_kernel, tables), shapes, keep, send)
            held = [late, local_sums, come, near]
    return pl.pallas_call(
        finish_kernel,
        out_shape=shape_of(height, 2 * B),
        in_specs=[VMEM] * 2,
        out_specs=pl.BlockSpec(memory_space=pl.ANY),
        scratch_shapes=[pltpu.SemaphoreType.DMA((2,))],
        compiler_params=PARAMS,
    )(keep, come)


def solution(mesh):
    in_specs = (P("row", "pair"), P())
    out_specs = P("row", "pair")
    return jax.shard_map(local, mesh=mesh, in_specs=in_specs, out_specs=out_specs, check_vma=False)
```

```python
import jax
import jax.numpy as jnp
from jax import lax
from jax.experimental import pallas as pl
from jax.experimental.pallas import tpu as pltpu
from jax.sharding import PartitionSpec as P

B = 256
STEPS = 4
INNER = 4
TILE = 8
REACH = 2 * (INNER - 1)
ALL_PAIRS = [(x, y) for x in range(4) for y in range(4)]
LAG = INNER - 1
GROUP = 24
GROUPS = 32


def ahead(block, distance):
    distance = distance % B
    return block if distance == 0 else pltpu.roll(block, B - distance, axis=1)


def ring_of(tables):
    return [0] + list(range(1, tables, 2)) + list(range(tables - 2, 0, -2))


def sends_upper(table):
    return (table == 0) | (table % 2 == 1)


def ring_before(place, tables):
    last = tables - 1
    odd = jnp.where(place == 1, 0, place - 2)
    even = jnp.where(place == last - 1, last, place + 2)
    return jnp.where(place % 2 == 1, odd, even)


def angle(upper_diag, lower_diag, coupling):
    differ = lower_diag - upper_diag
    signs = jnp.where(differ >= 0.0, 1.0, -1.0)
    whole = upper_diag + lower_diag
    denom = jnp.abs(differ) + jnp.sqrt(
        differ * differ + 4.0 * coupling * coupling + 1e-12 * (whole * whole)
    )
    tangent = 2.0 * signs * coupling / denom
    square = 1.0 + tangent * tangent
    guess = lax.rsqrt(square)
    cosines = guess * (1.5 - 0.5 * square * (guess * guess))
    return cosines, tangent * cosines


def turn_both(bands, left, right):
    (c, s), (cd, sd) = left, right
    uu, ul, lu, ll = bands
    top_u = c * uu - s * lu
    top_l = c * ul - s * ll
    low_u = s * uu + c * lu
    low_l = s * ul + c * ll
    return [
        cd * top_u - sd * top_l,
        sd * top_u + cd * top_l,
        cd * low_u - sd * low_l,
        sd * low_u + cd * low_l,
    ]


def spread(value):
    return jnp.broadcast_to(value[:1], (TILE, B))


def behind(value):
    return pltpu.roll(value, 0, axis=1, stride=1, stride_axis=0)


def next_heads(bands, c, s):
    uu, ul, lu, ll = bands
    uu_z, ul_z, lu_z, ll_z = (ahead(v, 1) for v in bands)
    uu_y, ul_y, lu_y, ll_y = (pltpu.roll(v, TILE - 1, axis=0) for v in (uu_z, ul_z, lu_z, ll_z))
    cz, sz = ahead(c, 1), ahead(s, 1)
    head_uu = c * (c * uu - s * lu) - s * (c * ul - s * ll)
    head_ul = c * (sz * uu_y + cz * lu_y) - s * (sz * ul_y + cz * ll_y)
    head_ll = sz * (sz * uu_z + cz * lu_z) + cz * (sz * ul_z + cz * ll_z)
    return head_uu, head_ul, head_ll


def solve(pairs):
    tables = sorted({a for a, _ in pairs})
    first_row = lax.broadcasted_iota(jnp.int32, (TILE, B), 0) == 0
    turns = [[] for _ in tables]
    heads = [(pairs[t, t][0], pairs[t, t][1], pairs[t, t][3]) for t in tables]
    for sweep in range(INNER):
        wide = []
        for t in tables:
            uu, ul, ll = heads[t]
            c, s = angle(uu, ll, ul)
            if sweep < INNER - 1:
                heads[t] = next_heads(pairs[t, t], c, s)
            c, s = spread(c), spread(s)
            turns[t].append((c, s))
            wide.append((behind(c), behind(s)))
        if sweep == INNER - 1 and len(tables) == 1:
            break
        pairs = {
            (a, b): turn_both(bands, turns[a][-1], wide[b]) for (a, b), bands in pairs.items()
        }
        if sweep == INNER - 1:
            break
        for key, (uu, ul, lu, ll) in pairs.items():
            ul = pltpu.roll(ul, 1, axis=0)
            lu = ahead(pltpu.roll(lu, TILE - 1, axis=0), 1)
            pairs[key] = [uu, ul, lu, ahead(ll, 1)]
        for a, b in pairs:
            pairs[a, b][1] = jnp.where(first_row, pairs[b, a][2], pairs[a, b][1])
    return turns, pairs


def turn_tiles(uppers, lowers, turns):
    for sweep, (c, s) in enumerate(turns):
        pairs = list(zip(uppers, lowers))
        uppers = [c * u - s * v for u, v in pairs]
        lowers = [s * u + c * v for u, v in pairs]
        if sweep < INNER - 1:
            lowers = [ahead(v, 1) for v in lowers]
    return uppers, lowers


def mix_tiles(uppers, lowers, turns, lower_wanted):
    uppers, lowers = turn_tiles(uppers, lowers, turns[:-1])
    c, s = turns[-1]
    from_u, from_l = jnp.where(lower_wanted, s, c), jnp.where(lower_wanted, c, -s)
    return [from_u * u + from_l * v for u, v in zip(uppers, lowers)]


def sides(place, tables):
    return place == 0, place == tables - 2


def product_sums(load, height, pairs):
    used = sorted({n for pair in pairs for n in pair})
    totals = {}
    for d in range(REACH + 1):
        kept = [(x, y) for x, y in pairs if d or x <= y or (y, x) not in pairs]
        for start in range(0, height, TILE):
            now = {n: load(n, slice(start, start + TILE)) for n in used}
            then = {n: ahead(v, -d) for n, v in now.items()}
            for x, y in kept:
                term = now[x] * then[y]
                totals[x, y, d] = term if start == 0 else totals[x, y, d] + term
    for x, y in pairs:
        if (x, y, 0) not in totals:
            totals[x, y, 0] = totals[y, x, 0]
    return {key: jnp.sum(total, axis=0, keepdims=True) for key, total in totals.items()}


def put_sums(out_ref, sums, pairs, slot_of):
    for x, y in pairs:
        slot = slot_of(x, y)
        for half in range(2):
            columns = slice(half * (B // 2), (half + 1) * (B // 2))
            for d in range(REACH + 1):
                out_ref[2 * slot + half, d : d + 1, :] = sums[x, y, d][:, columns]


def lags(place, tables):
    odd = place % 2 == 1
    return odd | (place == 0), jnp.logical_not(odd | (place == tables - 2))


def held_bands_kernel(tables, keep_ref, send_ref, late_ref, out_ref):
    lag = lags(lax.axis_index("pair"), tables)
    out_ref[...] = jnp.zeros_like(out_ref)
    height = keep_ref.shape[0]
    for start in range(0, height, TILE):
        rows = slice(start, start + TILE)
        for n, ref in enumerate((keep_ref, send_ref)):
            value = ref[rows, :]
            late_ref[rows, n * B : (n + 1) * B] = jnp.where(lag[n], ahead(value, -LAG), value)

    def load(n, rows):
        return late_ref[rows, n * B : (n + 1) * B]

    pairs = [(x, y) for x in range(2) for y in range(2)]
    put_sums(out_ref, product_sums(load, height, pairs), pairs, lambda x, y: 2 * x + y)


def moved_bands_kernel(tables, late_ref, held_ref, come_ref, next_ref, lined_ref, out_ref):
    place = lax.axis_index("pair")
    odd = place % 2
    lower_sent = ring_before(place, tables) % 2
    own, other = 2 * odd, 2 - 2 * odd
    at = [own + 1 - odd, other + lower_sent, own + odd, other + 1 - lower_sent]
    lag = lags(place, tables)
    out_ref[...] = jnp.zeros_like(out_ref)
    height = come_ref.shape[0]
    columns = [pl.ds(pl.multiple_of(n * B, B), B) for n in at]
    for start in range(0, height, TILE):
        rows = slice(start, start + TILE)
        for n in range(2):
            lined_ref[rows, columns[n]] = late_ref[rows, n * B : (n + 1) * B]
        for n, ref in enumerate((come_ref, next_ref)):
            value = ref[rows, :]
            lined_ref[rows, columns[2 + n]] = jnp.where(lag[n], ahead(value, -LAG), value)

    def load(n, rows):
        return lined_ref[rows, columns[n]]

    def slot_of(x, y):
        return 4 * at[x] + at[y]

    pairs = [(x, y) for x, y in ALL_PAIRS if x > 1 or y > 1]
    put_sums(out_ref, product_sums(load, height, pairs), pairs, slot_of)
    for x in range(2):
        for y in range(2):
            for half in range(2):
                out_ref[2 * slot_of(x, y) + half] = held_ref[2 * (2 * x + y) + half]


def total_kernel(peers, parts_ref, out_ref):
    share = parts_ref.shape[0] // peers
    for part in range(share):
        total = parts_ref[part]
        for peer in range(1, peers):
            total = total + parts_ref[peer * share + part]
        for peer in range(peers):
            out_ref[peer * share + part] = total


def rotate_kernel(tables, sums_ref, lined_ref, keep_out, send_out):
    place = lax.axis_index("pair")
    left_lower, right_upper = sides(place, tables)

    def bands(x, y):
        slot = 4 * x + y
        return jnp.concatenate([sums_ref[2 * slot], sums_ref[2 * slot + 1]], axis=1)

    pairs = {
        (a, b): [bands(2 * a + x, 2 * b + y) for x in range(2) for y in range(2)]
        for a in range(2)
        for b in range(2)
    }
    (left_turns, right_turns), pairs = solve(pairs)
    uu, _, _, ll = pairs[0, 0]
    new_uu = jnp.where(left_lower, ll, uu)
    uu, _, _, ll = pairs[1, 1]
    new_ll = jnp.where(right_upper, uu, ll)
    uu, ul, lu, ll = pairs[0, 1]
    new_ul = jnp.where(
        left_lower, jnp.where(right_upper, lu, ll), jnp.where(right_upper, uu, ul)
    )
    uu, ul, lu, ll = pairs[1, 0]
    new_lu = jnp.where(
        left_lower, jnp.where(right_upper, ul, ll), jnp.where(right_upper, uu, lu)
    )
    (last_turns,), _ = solve({(0, 0): [new_uu, new_ul, new_lu, new_ll]})
    upper_sent = sends_upper(place ^ 1)
    height = keep_out.shape[0]
    groups = [
        [slice(r, r + TILE) for r in range(start, min(start + GROUP * TILE, height), TILE)]
        for start in range(0, height, GROUP * TILE)
    ]
    for n, out_ref, turns, lower_wanted in (
        (0, keep_out, left_turns, left_lower),
        (2, send_out, right_turns, jnp.logical_not(right_upper)),
    ):
        for group in groups:
            uppers = [lined_ref[rows, n * B : (n + 1) * B] for rows in group]
            lowers = [lined_ref[rows, (n + 1) * B : (n + 2) * B] for rows in group]
            for rows, value in zip(group, mix_tiles(uppers, lowers, turns, lower_wanted)):
                out_ref[rows, :] = value
    for group in groups:
        uppers = [keep_out[rows, :] for rows in group]
        lowers = [send_out[rows, :] for rows in group]
        uppers, lowers = turn_tiles(uppers, lowers, last_turns)
        for rows, upper, lower in zip(group, uppers, lowers):
            lower = ahead(lower, -LAG)
            keep_out[rows, :] = jnp.where(upper_sent, lower, upper)
            send_out[rows, :] = jnp.where(upper_sent, upper, lower)


def finish_kernel(keep_ref, come_ref, out_ref, sems):
    keep_at = jnp.where(lax.axis_index("pair") % 2 == 0, B, 0)
    copies = []
    for n, (block_ref, start) in enumerate(((keep_ref, keep_at), (come_ref, B - keep_at))):
        columns = pl.ds(pl.multiple_of(start, B), B)
        copies.append(pltpu.make_async_copy(block_ref, out_ref.at[:, columns], sems.at[n]))
    for copy in copies:
        copy.start()
    for copy in copies:
        copy.wait()


def line_seats(place, tables):
    odd = place % 2 == 1
    before = ring_before(place, tables)
    left, right = jnp.where(odd, before, place), jnp.where(odd, place, before)
    return 2 * left, 2 * left + 1, 2 * right, 2 * right + 1


def wanted_kernel(tables, seating_ref, out_ref):
    place = lax.axis_index("pair")
    lane = lax.broadcasted_iota(jnp.int32, out_ref.shape, 1)
    out = jnp.zeros(out_ref.shape, jnp.int32)
    for n, seat in enumerate(line_seats(place, tables) + line_seats(place ^ 1, tables)):
        out = jnp.where(lane == n, seating_ref[seat], out)
    out_ref[...] = out


def split_kernel(matrix_ref, top_ref, bottom_ref):
    half = top_ref.shape[0]
    top_ref[...] = matrix_ref[:half, :]
    bottom_ref[...] = matrix_ref[half:, :]


def chips_away(block, tables):
    chips = tables // 2
    return (block // 4 - lax.axis_index("pair") // 2 + chips) % chips


def block_columns(block):
    return pl.ds(pl.multiple_of((block % 2) * B, B), B)


def copy_block(tables, block, chosen, put, gathered):
    away = chips_away(block, tables)
    columns = block_columns(block)
    half = gathered[0].shape[0]
    for n in range(len(gathered) // 2):
        distance = (0, 1, 3, 2)[n]

        @pl.when(chosen & (away == distance))
        def _():
            for part in range(2):
                ref = gathered[2 * n + part]
                for start in range(0, half, TILE):
                    rows = slice(part * half + start, part * half + start + TILE)
                    put(rows, ref[start : start + TILE, columns])


def pick_near_kernel(tables, wanted_ref, *rest):
    gathered, outs = rest[:-2], rest[-2:]
    wanted = wanted_ref[...]
    half = outs[0].shape[0]
    for n in range(4):

        def put(rows, value, n=n):
            part = rows.start // half
            rows = slice(rows.start - part * half, rows.stop - part * half)
            outs[part][rows, n * B : (n + 1) * B] = value

        copy_block(tables, wanted[0, 4 + n], True, put, gathered)


def pick_far_kernel(tables, wanted_ref, near_ref, far_ref, out_ref):
    wanted = wanted_ref[...]
    for n in range(4):
        block = wanted[0, 4 + n]
        far = chips_away(block, tables) == 2
        columns = block_columns(block)
        at = slice(n * B, (n + 1) * B)
        for start in range(0, far_ref.shape[0], TILE):
            rows = slice(start, start + TILE)
            out_ref[rows, at] = jnp.where(far, far_ref[rows, columns], near_ref[rows, at])


def is_here(block):
    return (block // 2) % 2 == lax.axis_index("pair") % 2


def is_late(n, tables):
    left_lower, right_upper = sides(lax.axis_index("pair"), tables)
    return left_lower if n < 2 else jnp.logical_not(right_upper)


def here_kernel(tables, wanted_ref, *rest):
    gathered, out_ref = rest[:-1], rest[-1]
    wanted = wanted_ref[...]
    for n in range(4):
        late = is_late(n, tables)

        def put(rows, value, n=n, late=late):
            out_ref[rows, n * B : (n + 1) * B] = jnp.where(late, ahead(value, -LAG), value)

        copy_block(tables, wanted[0, n], is_here(wanted[0, n]), put, gathered)


def seated_bands_kernel(tables, wanted_ref, here_ref, top_ref, bottom_ref, lined_ref, out_ref):
    wanted = wanted_ref[...]
    height = here_ref.shape[0]
    for n in range(4):
        here, late = is_here(wanted[0, n]), is_late(n, tables)
        columns = slice(n * B, (n + 1) * B)
        for part, ref in enumerate((top_ref, bottom_ref)):
            for start in range(0, ref.shape[0], TILE):
                rows = slice(part * ref.shape[0] + start, part * ref.shape[0] + start + TILE)
                value = ref[start : start + TILE, columns]
                value = jnp.where(late, ahead(value, -LAG), value)
                lined_ref[rows, columns] = jnp.where(here, here_ref[rows, columns], value)

    def load(n, rows):
        return lined_ref[rows, n * B : (n + 1) * B]

    out_ref[...] = jnp.zeros_like(out_ref)
    sums = product_sums(load, height, ALL_PAIRS)
    put_sums(out_ref, sums, ALL_PAIRS, lambda x, y: 4 * x + y)


VMEM = pl.BlockSpec(memory_space=pltpu.VMEM)
PARAMS = pltpu.CompilerParams(vmem_limit_bytes=32 * 1024 * 1024)


def call(kernel, out_shape, *args):
    outs = [VMEM] * len(out_shape) if isinstance(out_shape, list) else VMEM
    return pl.pallas_call(
        kernel,
        out_shape=out_shape,
        in_specs=[VMEM] * len(args),
        out_specs=outs,
        compiler_params=PARAMS,
    )(*args)


def shape_of(*sizes):
    return jax.ShapeDtypeStruct(sizes, jnp.float32)


def bind(kernel, size):
    def bound(*refs):
        return kernel(size, *refs)

    return bound


def local(matrix, seating):
    height = matrix.shape[0]
    peers = lax.axis_size("row")
    tables = lax.axis_size("pair")
    ring = ring_of(tables)
    hosts = [table ^ 1 for table in ring]
    forward = list(zip(hosts, hosts[1:] + hosts[:1]))
    backward = [(b, a) for a, b in forward]
    up = [(j, (j + 2) % tables) for j in range(tables)]
    down = [(b, a) for a, b in up]
    across = [(j, j ^ 1) for j in range(tables)]
    wanted = pl.pallas_call(
        bind(wanted_kernel, tables),
        out_shape=jax.ShapeDtypeStruct((1, B // 2), jnp.int32),
        in_specs=[pl.BlockSpec(memory_space=pltpu.SMEM)],
        out_specs=VMEM,
        compiler_params=PARAMS,
    )(seating)
    top, bottom = call(split_kernel, [shape_of(height // 2, 2 * B)] * 2, matrix)
    left_top = lax.ppermute(top, "pair", up)
    right_bottom = lax.ppermute(bottom, "pair", down)
    left_bottom = lax.ppermute(bottom, "pair", up)
    right_top = lax.ppermute(top, "pair", down)
    far_top = lax.ppermute(left_top, "pair", up)
    far_bottom = lax.ppermute(right_bottom, "pair", down)
    near = [wanted, top, bottom, right_top, right_bottom, left_top, left_bottom]
    far = [far_top, far_bottom]
    seated_shape = shape_of(height, 4 * B)
    half_shape = shape_of(height // 2, 4 * B)
    picked = call(bind(pick_near_kernel, tables), [half_shape] * 2, *near)
    swaps = []
    for near_half, far_half in zip(picked, far):
        swap = call(bind(pick_far_kernel, tables), half_shape, wanted, near_half, far_half)
        swaps.append(lax.ppermute(swap, "pair", across))
    here = call(bind(here_kernel, tables), seated_shape, *near, *far)
    lined_shape = shape_of(height, 4 * B)
    spread_shape = shape_of(GROUPS, TILE, B // 2)
    block_shape = shape_of(height, B)
    for pair_of_steps in range(STEPS // 2):
        if pair_of_steps == 0:
            kernel = bind(seated_bands_kernel, tables)
            lined, sums = call(kernel, [lined_shape, spread_shape], wanted, here, *swaps)
        else:
            kernel = bind(moved_bands_kernel, tables)
            lined, sums = call(kernel, [lined_shape, spread_shape], *held)
        sums = lax.all_to_all(sums, "row", 0, 0, tiled=True)
        sums = call(bind(total_kernel, peers), spread_shape, sums)
        sums = lax.all_to_all(sums, "row", 0, 0, tiled=True)
        kernel = bind(rotate_kernel, tables)
        keep, send = call(kernel, [block_shape, block_shape], sums, lined)
        come = lax.ppermute(send, "pair", forward)
        if pair_of_steps < STEPS // 2 - 1:
            near = lax.ppermute(keep, "pair", backward)
            shapes = [shape_of(height, 2 * B), shape_of(TILE, TILE, B // 2)]
            late, local_sums = call(bind(held_bands_kernel, tables), shapes, keep, send)
            held = [late, local_sums, come, near]
    return pl.pallas_call(
        finish_kernel,
        out_shape=shape_of(height, 2 * B),
        in_specs=[VMEM] * 2,
        out_specs=pl.BlockSpec(memory_space=pl.ANY),
        scratch_shapes=[pltpu.SemaphoreType.DMA((2,))],
        compiler_params=PARAMS,
    )(keep, come)


def solution(mesh):
    in_specs = (P("row", "pair"), P())
    out_specs = P("row", "pair")
    return jax.shard_map(local, mesh=mesh, in_specs=in_specs, out_specs=out_specs, check_vma=False)
```

```python
import jax
import jax.numpy as jnp
from jax import lax
from jax.experimental import pallas as pl
from jax.experimental.pallas import tpu as pltpu
from jax.sharding import PartitionSpec as P

B = 256
STEPS = 4
INNER = 4
TILE = 8
REACH = 2 * (INNER - 1)
ALL_PAIRS = [(x, y) for x in range(4) for y in range(4)]
LAG = INNER - 1
GROUP = 24
GROUPS = 32


def ahead(block, distance):
    distance = distance % B
    return block if distance == 0 else pltpu.roll(block, B - distance, axis=1)


def ring_of(tables):
    return [0] + list(range(1, tables, 2)) + list(range(tables - 2, 0, -2))


def sends_upper(table):
    return (table == 0) | (table % 2 == 1)


def ring_before(place, tables):
    last = tables - 1
    odd = jnp.where(place == 1, 0, place - 2)
    even = jnp.where(place == last - 1, last, place + 2)
    return jnp.where(place % 2 == 1, odd, even)


def angle(upper_diag, lower_diag, coupling):
    differ = lower_diag - upper_diag
    signs = jnp.where(differ >= 0.0, 1.0, -1.0)
    whole = upper_diag + lower_diag
    denom = jnp.abs(differ) + jnp.sqrt(
        differ * differ + 4.0 * coupling * coupling + 1e-12 * (whole * whole)
    )
    tangent = 2.0 * signs * coupling / denom
    square = 1.0 + tangent * tangent
    guess = lax.rsqrt(square)
    cosines = guess * (1.5 - 0.5 * square * (guess * guess))
    return cosines, tangent * cosines


def turn_both(bands, left, right):
    (c, s), (cd, sd) = left, right
    uu, ul, lu, ll = bands
    top_u = c * uu - s * lu
    top_l = c * ul - s * ll
    low_u = s * uu + c * lu
    low_l = s * ul + c * ll
    return [
        cd * top_u - sd * top_l,
        sd * top_u + cd * top_l,
        cd * low_u - sd * low_l,
        sd * low_u + cd * low_l,
    ]


def spread(value):
    return jnp.broadcast_to(value[:1], (TILE, B))


def behind(value):
    return pltpu.roll(value, 0, axis=1, stride=1, stride_axis=0)


def next_heads(bands, c, s):
    uu, ul, lu, ll = bands
    uu_z, ul_z, lu_z, ll_z = (ahead(v, 1) for v in bands)
    uu_y, ul_y, lu_y, ll_y = (pltpu.roll(v, TILE - 1, axis=0) for v in (uu_z, ul_z, lu_z, ll_z))
    cz, sz = ahead(c, 1), ahead(s, 1)
    head_uu = c * (c * uu - s * lu) - s * (c * ul - s * ll)
    head_ul = c * (sz * uu_y + cz * lu_y) - s * (sz * ul_y + cz * ll_y)
    head_ll = sz * (sz * uu_z + cz * lu_z) + cz * (sz * ul_z + cz * ll_z)
    return head_uu, head_ul, head_ll


def solve(pairs):
    tables = sorted({a for a, _ in pairs})
    first_row = lax.broadcasted_iota(jnp.int32, (TILE, B), 0) == 0
    turns = [[] for _ in tables]
    heads = [(pairs[t, t][0], pairs[t, t][1], pairs[t, t][3]) for t in tables]
    for sweep in range(INNER):
        wide = []
        for t in tables:
            uu, ul, ll = heads[t]
            c, s = angle(uu, ll, ul)
            if sweep < INNER - 1:
                heads[t] = next_heads(pairs[t, t], c, s)
            c, s = spread(c), spread(s)
            turns[t].append((c, s))
            wide.append((behind(c), behind(s)))
        if sweep == INNER - 1 and len(tables) == 1:
            break
        pairs = {
            (a, b): turn_both(bands, turns[a][-1], wide[b]) for (a, b), bands in pairs.items()
        }
        if sweep == INNER - 1:
            break
        for key, (uu, ul, lu, ll) in pairs.items():
            ul = pltpu.roll(ul, 1, axis=0)
            lu = ahead(pltpu.roll(lu, TILE - 1, axis=0), 1)
            pairs[key] = [uu, ul, lu, ahead(ll, 1)]
        for a, b in pairs:
            pairs[a, b][1] = jnp.where(first_row, pairs[b, a][2], pairs[a, b][1])
    return turns, pairs


def turn_tiles(uppers, lowers, turns):
    for sweep, (c, s) in enumerate(turns):
        pairs = list(zip(uppers, lowers))
        uppers = [c * u - s * v for u, v in pairs]
        lowers = [s * u + c * v for u, v in pairs]
        if sweep < INNER - 1:
            lowers = [ahead(v, 1) for v in lowers]
    return uppers, lowers


def mix_tiles(uppers, lowers, turns, lower_wanted):
    uppers, lowers = turn_tiles(uppers, lowers, turns[:-1])
    c, s = turns[-1]
    from_u, from_l = jnp.where(lower_wanted, s, c), jnp.where(lower_wanted, c, -s)
    return [from_u * u + from_l * v for u, v in zip(uppers, lowers)]


def sides(place, tables):
    return place == 0, place == tables - 2


def product_sums(load, height, pairs):
    used = sorted({n for pair in pairs for n in pair})
    totals = {}
    for d in range(REACH + 1):
        kept = [(x, y) for x, y in pairs if d or x <= y or (y, x) not in pairs]
        for start in range(0, height, TILE):
            now = {n: load(n, slice(start, start + TILE)) for n in used}
            then = {n: ahead(v, -d) for n, v in now.items()}
            for x, y in kept:
                term = now[x] * then[y]
                totals[x, y, d] = term if start == 0 else totals[x, y, d] + term
    for x, y in pairs:
        if (x, y, 0) not in totals:
            totals[x, y, 0] = totals[y, x, 0]
    return {key: jnp.sum(total, axis=0, keepdims=True) for key, total in totals.items()}


def put_sums(out_ref, sums, pairs, slot_of):
    for x, y in pairs:
        slot = slot_of(x, y)
        for half in range(2):
            columns = slice(half * (B // 2), (half + 1) * (B // 2))
            for d in range(REACH + 1):
                out_ref[2 * slot + half, d : d + 1, :] = sums[x, y, d][:, columns]


def lags(place, tables):
    odd = place % 2 == 1
    return odd | (place == 0), jnp.logical_not(odd | (place == tables - 2))


def held_bands_kernel(tables, keep_ref, send_ref, late_ref, out_ref):
    lag = lags(lax.axis_index("pair"), tables)
    out_ref[...] = jnp.zeros_like(out_ref)
    height = keep_ref.shape[0]
    for start in range(0, height, TILE):
        rows = slice(start, start + TILE)
        for n, ref in enumerate((keep_ref, send_ref)):
            value = ref[rows, :]
            late_ref[rows, n * B : (n + 1) * B] = jnp.where(lag[n], ahead(value, -LAG), value)

    def load(n, rows):
        return late_ref[rows, n * B : (n + 1) * B]

    pairs = [(x, y) for x in range(2) for y in range(2)]
    put_sums(out_ref, product_sums(load, height, pairs), pairs, lambda x, y: 2 * x + y)


def moved_bands_kernel(tables, late_ref, held_ref, come_ref, next_ref, lined_ref, out_ref):
    place = lax.axis_index("pair")
    odd = place % 2
    lower_sent = ring_before(place, tables) % 2
    own, other = 2 * odd, 2 - 2 * odd
    at = [own + 1 - odd, other + lower_sent, own + odd, other + 1 - lower_sent]
    lag = lags(place, tables)
    out_ref[...] = jnp.zeros_like(out_ref)
    height = come_ref.shape[0]
    columns = [pl.ds(pl.multiple_of(n * B, B), B) for n in at]
    for start in range(0, height, TILE):
        rows = slice(start, start + TILE)
        for n in range(2):
            lined_ref[rows, columns[n]] = late_ref[rows, n * B : (n + 1) * B]
        for n, ref in enumerate((come_ref, next_ref)):
            value = ref[rows, :]
            lined_ref[rows, columns[2 + n]] = jnp.where(lag[n], ahead(value, -LAG), value)

    def load(n, rows):
        return lined_ref[rows, columns[n]]

    def slot_of(x, y):
        return 4 * at[x] + at[y]

    pairs = [(x, y) for x, y in ALL_PAIRS if x > 1 or y > 1]
    put_sums(out_ref, product_sums(load, height, pairs), pairs, slot_of)
    for x in range(2):
        for y in range(2):
            for half in range(2):
                out_ref[2 * slot_of(x, y) + half] = held_ref[2 * (2 * x + y) + half]


def total_kernel(peers, parts_ref, out_ref):
    share = parts_ref.shape[0] // peers
    for part in range(share):
        total = parts_ref[part]
        for peer in range(1, peers):
            total = total + parts_ref[peer * share + part]
        for peer in range(peers):
            out_ref[peer * share + part] = total


def rotate_kernel(tables, sums_ref, lined_ref, keep_out, send_out):
    place = lax.axis_index("pair")
    left_lower, right_upper = sides(place, tables)

    def bands(x, y):
        slot = 4 * x + y
        return jnp.concatenate([sums_ref[2 * slot], sums_ref[2 * slot + 1]], axis=1)

    pairs = {
        (a, b): [bands(2 * a + x, 2 * b + y) for x in range(2) for y in range(2)]
        for a in range(2)
        for b in range(2)
    }
    (left_turns, right_turns), pairs = solve(pairs)
    uu, _, _, ll = pairs[0, 0]
    new_uu = jnp.where(left_lower, ll, uu)
    uu, _, _, ll = pairs[1, 1]
    new_ll = jnp.where(right_upper, uu, ll)
    uu, ul, lu, ll = pairs[0, 1]
    new_ul = jnp.where(
        left_lower, jnp.where(right_upper, lu, ll), jnp.where(right_upper, uu, ul)
    )
    uu, ul, lu, ll = pairs[1, 0]
    new_lu = jnp.where(
        left_lower, jnp.where(right_upper, ul, ll), jnp.where(right_upper, uu, lu)
    )
    (last_turns,), _ = solve({(0, 0): [new_uu, new_ul, new_lu, new_ll]})
    upper_sent = sends_upper(place ^ 1)
    height = keep_out.shape[0]
    groups = [
        [slice(r, r + TILE) for r in range(start, min(start + GROUP * TILE, height), TILE)]
        for start in range(0, height, GROUP * TILE)
    ]
    for n, out_ref, turns, lower_wanted in (
        (0, keep_out, left_turns, left_lower),
        (2, send_out, right_turns, jnp.logical_not(right_upper)),
    ):
        for group in groups:
            uppers = [lined_ref[rows, n * B : (n + 1) * B] for rows in group]
            lowers = [lined_ref[rows, (n + 1) * B : (n + 2) * B] for rows in group]
            for rows, value in zip(group, mix_tiles(uppers, lowers, turns, lower_wanted)):
                out_ref[rows, :] = value
    for group in groups:
        uppers = [keep_out[rows, :] for rows in group]
        lowers = [send_out[rows, :] for rows in group]
        uppers, lowers = turn_tiles(uppers, lowers, last_turns)
        for rows, upper, lower in zip(group, uppers, lowers):
            lower = ahead(lower, -LAG)
            keep_out[rows, :] = jnp.where(upper_sent, lower, upper)
            send_out[rows, :] = jnp.where(upper_sent, upper, lower)


def finish_kernel(keep_ref, come_ref, out_ref, sems):
    keep_at = jnp.where(lax.axis_index("pair") % 2 == 0, B, 0)
    copies = []
    for n, (block_ref, start) in enumerate(((keep_ref, keep_at), (come_ref, B - keep_at))):
        columns = pl.ds(pl.multiple_of(start, B), B)
        copies.append(pltpu.make_async_copy(block_ref, out_ref.at[:, columns], sems.at[n]))
    for copy in copies:
        copy.start()
    for copy in copies:
        copy.wait()


def line_seats(place, tables):
    odd = place % 2 == 1
    before = ring_before(place, tables)
    left, right = jnp.where(odd, before, place), jnp.where(odd, place, before)
    return 2 * left, 2 * left + 1, 2 * right, 2 * right + 1


def wanted_kernel(tables, seating_ref, out_ref):
    place = lax.axis_index("pair")
    lane = lax.broadcasted_iota(jnp.int32, out_ref.shape, 1)
    out = jnp.zeros(out_ref.shape, jnp.int32)
    for n, seat in enumerate(line_seats(place, tables) + line_seats(place ^ 1, tables)):
        out = jnp.where(lane == n, seating_ref[seat], out)
    out_ref[...] = out


def split_kernel(matrix_ref, top_ref, bottom_ref):
    half = top_ref.shape[0]
    top_ref[...] = matrix_ref[:half, :]
    bottom_ref[...] = matrix_ref[half:, :]


def chips_away(block, tables):
    chips = tables // 2
    return (block // 4 - lax.axis_index("pair") // 2 + chips) % chips


def block_columns(block):
    return pl.ds(pl.multiple_of((block % 2) * B, B), B)


def copy_block(tables, block, chosen, put, gathered):
    away = chips_away(block, tables)
    columns = block_columns(block)
    half = gathered[0].shape[0]
    for n in range(len(gathered) // 2):
        distance = (0, 1, 3, 2)[n]

        @pl.when(chosen & (away == distance))
        def _():
            for part in range(2):
                ref = gathered[2 * n + part]
                for start in range(0, half, TILE):
                    rows = slice(part * half + start, part * half + start + TILE)
                    put(rows, ref[start : start + TILE, columns])


def pick_near_kernel(tables, wanted_ref, *rest):
    gathered, out_ref = rest[:-1], rest[-1]
    wanted = wanted_ref[...]
    for n in range(4):
        late = is_late(n, tables, lax.axis_index("pair") ^ 1)

        def put(rows, value, n=n, late=late):
            out_ref[rows, n * B : (n + 1) * B] = jnp.where(late, ahead(value, -LAG), value)

        copy_block(tables, wanted[0, 4 + n], True, put, gathered)


def pick_far_kernel(tables, wanted_ref, near_ref, top_ref, bottom_ref, out_ref):
    wanted = wanted_ref[...]
    half = top_ref.shape[0]
    for n in range(4):
        block = wanted[0, 4 + n]
        far = chips_away(block, tables) == 2
        late = is_late(n, tables, lax.axis_index("pair") ^ 1)
        columns = block_columns(block)
        at = slice(n * B, (n + 1) * B)

        @pl.when(far)
        def _():
            for part, ref in enumerate((top_ref, bottom_ref)):
                for start in range(0, half, TILE):
                    rows = slice(part * half + start, part * half + start + TILE)
                    value = ref[start : start + TILE, columns]
                    out_ref[rows, at] = jnp.where(late, ahead(value, -LAG), value)

        @pl.when(jnp.logical_not(far))
        def _():
            out_ref[:, at] = near_ref[:, at]


def is_here(block):
    return (block // 2) % 2 == lax.axis_index("pair") % 2


def is_late(n, tables, place=None):
    left_lower, right_upper = sides(lax.axis_index("pair") if place is None else place, tables)
    return left_lower if n < 2 else jnp.logical_not(right_upper)


def here_kernel(tables, wanted_ref, *rest):
    gathered, out_ref = rest[:-1], rest[-1]
    wanted = wanted_ref[...]
    for n in range(4):
        late = is_late(n, tables)

        def put(rows, value, n=n, late=late):
            out_ref[rows, n * B : (n + 1) * B] = jnp.where(late, ahead(value, -LAG), value)

        copy_block(tables, wanted[0, n], is_here(wanted[0, n]), put, gathered)


def seated_bands_kernel(tables, wanted_ref, here_ref, swap_ref, lined_ref, out_ref):
    wanted = wanted_ref[...]
    height = here_ref.shape[0]
    for n in range(4):
        here = is_here(wanted[0, n])
        columns = slice(n * B, (n + 1) * B)
        for start in range(0, height, TILE):
            rows = slice(start, start + TILE)
            lined_ref[rows, columns] = jnp.where(
                here, here_ref[rows, columns], swap_ref[rows, columns]
            )

    def load(n, rows):
        return lined_ref[rows, n * B : (n + 1) * B]

    out_ref[...] = jnp.zeros_like(out_ref)
    sums = product_sums(load, height, ALL_PAIRS)
    put_sums(out_ref, sums, ALL_PAIRS, lambda x, y: 4 * x + y)


VMEM = pl.BlockSpec(memory_space=pltpu.VMEM)
PARAMS = pltpu.CompilerParams(vmem_limit_bytes=32 * 1024 * 1024)


def call(kernel, out_shape, *args):
    outs = [VMEM] * len(out_shape) if isinstance(out_shape, list) else VMEM
    return pl.pallas_call(
        kernel,
        out_shape=out_shape,
        in_specs=[VMEM] * len(args),
        out_specs=outs,
        compiler_params=PARAMS,
    )(*args)


def shape_of(*sizes):
    return jax.ShapeDtypeStruct(sizes, jnp.float32)


def bind(kernel, size):
    def bound(*refs):
        return kernel(size, *refs)

    return bound


def local(matrix, seating):
    height = matrix.shape[0]
    peers = lax.axis_size("row")
    tables = lax.axis_size("pair")
    ring = ring_of(tables)
    hosts = [table ^ 1 for table in ring]
    forward = list(zip(hosts, hosts[1:] + hosts[:1]))
    backward = [(b, a) for a, b in forward]
    up = [(j, (j + 2) % tables) for j in range(tables)]
    down = [(b, a) for a, b in up]
    across = [(j, j ^ 1) for j in range(tables)]
    wanted = pl.pallas_call(
        bind(wanted_kernel, tables),
        out_shape=jax.ShapeDtypeStruct((1, B // 2), jnp.int32),
        in_specs=[pl.BlockSpec(memory_space=pltpu.SMEM)],
        out_specs=VMEM,
        compiler_params=PARAMS,
    )(seating)
    top, bottom = call(split_kernel, [shape_of(height // 2, 2 * B)] * 2, matrix)
    left_top = lax.ppermute(top, "pair", up)
    right_bottom = lax.ppermute(bottom, "pair", down)
    left_bottom = lax.ppermute(bottom, "pair", up)
    right_top = lax.ppermute(top, "pair", down)
    far_top = lax.ppermute(left_top, "pair", up)
    far_bottom = lax.ppermute(right_bottom, "pair", down)
    near = [wanted, top, bottom, right_top, right_bottom, left_top, left_bottom]
    far = [far_top, far_bottom]
    seated_shape = shape_of(height, 4 * B)
    swap = call(bind(pick_near_kernel, tables), seated_shape, *near)
    swap = call(bind(pick_far_kernel, tables), seated_shape, wanted, swap, *far)
    swap = lax.ppermute(swap, "pair", across)
    here = call(bind(here_kernel, tables), seated_shape, *near, *far)
    lined_shape = shape_of(height, 4 * B)
    spread_shape = shape_of(GROUPS, TILE, B // 2)
    block_shape = shape_of(height, B)
    for pair_of_steps in range(STEPS // 2):
        if pair_of_steps == 0:
            kernel = bind(seated_bands_kernel, tables)
            lined, sums = call(kernel, [lined_shape, spread_shape], wanted, here, swap)
        else:
            kernel = bind(moved_bands_kernel, tables)
            lined, sums = call(kernel, [lined_shape, spread_shape], *held)
        sums = lax.all_to_all(sums, "row", 0, 0, tiled=True)
        sums = call(bind(total_kernel, peers), spread_shape, sums)
        sums = lax.all_to_all(sums, "row", 0, 0, tiled=True)
        kernel = bind(rotate_kernel, tables)
        keep, send = call(kernel, [block_shape, block_shape], sums, lined)
        come = lax.ppermute(send, "pair", forward)
        if pair_of_steps < STEPS // 2 - 1:
            near = lax.ppermute(keep, "pair", backward)
            shapes = [shape_of(height, 2 * B), shape_of(TILE, TILE, B // 2)]
            late, local_sums = call(bind(held_bands_kernel, tables), shapes, keep, send)
            held = [late, local_sums, come, near]
    return pl.pallas_call(
        finish_kernel,
        out_shape=shape_of(height, 2 * B),
        in_specs=[VMEM] * 2,
        out_specs=pl.BlockSpec(memory_space=pl.ANY),
        scratch_shapes=[pltpu.SemaphoreType.DMA((2,))],
        compiler_params=PARAMS,
    )(keep, come)


def solution(mesh):
    in_specs = (P("row", "pair"), P())
    out_specs = P("row", "pair")
    return jax.shard_map(local, mesh=mesh, in_specs=in_specs, out_specs=out_specs, check_vma=False)
```

```python
import jax
import jax.numpy as jnp
from jax import lax
from jax.experimental import pallas as pl
from jax.experimental.pallas import tpu as pltpu
from jax.sharding import PartitionSpec as P

B = 256
STEPS = 4
INNER = 4
TILE = 8
REACH = 2 * (INNER - 1)
ALL_PAIRS = [(x, y) for x in range(4) for y in range(4)]
LAG = INNER - 1
GROUP = 24
GROUPS = 32


def ahead(block, distance):
    distance = distance % B
    return block if distance == 0 else pltpu.roll(block, B - distance, axis=1)


def ring_of(tables):
    return [0] + list(range(1, tables, 2)) + list(range(tables - 2, 0, -2))


def sends_upper(table):
    return (table == 0) | (table % 2 == 1)


def ring_before(place, tables):
    last = tables - 1
    odd = jnp.where(place == 1, 0, place - 2)
    even = jnp.where(place == last - 1, last, place + 2)
    return jnp.where(place % 2 == 1, odd, even)


def angle(upper_diag, lower_diag, coupling):
    differ = lower_diag - upper_diag
    signs = jnp.where(differ >= 0.0, 1.0, -1.0)
    whole = upper_diag + lower_diag
    denom = jnp.abs(differ) + jnp.sqrt(
        differ * differ + 4.0 * coupling * coupling + 1e-12 * (whole * whole)
    )
    tangent = 2.0 * signs * coupling / denom
    square = 1.0 + tangent * tangent
    guess = lax.rsqrt(square)
    cosines = guess * (1.5 - 0.5 * square * (guess * guess))
    return cosines, tangent * cosines


def turn_both(bands, left, right):
    (c, s), (cd, sd) = left, right
    uu, ul, lu, ll = bands
    top_u = c * uu - s * lu
    top_l = c * ul - s * ll
    low_u = s * uu + c * lu
    low_l = s * ul + c * ll
    return [
        cd * top_u - sd * top_l,
        sd * top_u + cd * top_l,
        cd * low_u - sd * low_l,
        sd * low_u + cd * low_l,
    ]


def spread(value):
    return jnp.broadcast_to(value[:1], (TILE, B))


def behind(value):
    return pltpu.roll(value, 0, axis=1, stride=1, stride_axis=0)


def next_heads(bands, c, s):
    uu, ul, lu, ll = bands
    uu_z, ul_z, lu_z, ll_z = (ahead(v, 1) for v in bands)
    uu_y, ul_y, lu_y, ll_y = (pltpu.roll(v, TILE - 1, axis=0) for v in (uu_z, ul_z, lu_z, ll_z))
    cz, sz = ahead(c, 1), ahead(s, 1)
    head_uu = c * (c * uu - s * lu) - s * (c * ul - s * ll)
    head_ul = c * (sz * uu_y + cz * lu_y) - s * (sz * ul_y + cz * ll_y)
    head_ll = sz * (sz * uu_z + cz * lu_z) + cz * (sz * ul_z + cz * ll_z)
    return head_uu, head_ul, head_ll


def solve(pairs):
    tables = sorted({a for a, _ in pairs})
    first_row = lax.broadcasted_iota(jnp.int32, (TILE, B), 0) == 0
    turns = [[] for _ in tables]
    heads = [(pairs[t, t][0], pairs[t, t][1], pairs[t, t][3]) for t in tables]
    for sweep in range(INNER):
        wide = []
        for t in tables:
            uu, ul, ll = heads[t]
            c, s = angle(uu, ll, ul)
            if sweep < INNER - 1:
                heads[t] = next_heads(pairs[t, t], c, s)
            c, s = spread(c), spread(s)
            turns[t].append((c, s))
            wide.append((behind(c), behind(s)))
        if sweep == INNER - 1 and len(tables) == 1:
            break
        pairs = {
            (a, b): turn_both(bands, turns[a][-1], wide[b]) for (a, b), bands in pairs.items()
        }
        if sweep == INNER - 1:
            break
        for key, (uu, ul, lu, ll) in pairs.items():
            ul = pltpu.roll(ul, 1, axis=0)
            lu = ahead(pltpu.roll(lu, TILE - 1, axis=0), 1)
            pairs[key] = [uu, ul, lu, ahead(ll, 1)]
        for a, b in pairs:
            pairs[a, b][1] = jnp.where(first_row, pairs[b, a][2], pairs[a, b][1])
    return turns, pairs


def turn_tiles(uppers, lowers, turns):
    for sweep, (c, s) in enumerate(turns):
        pairs = list(zip(uppers, lowers))
        uppers = [c * u - s * v for u, v in pairs]
        lowers = [s * u + c * v for u, v in pairs]
        if sweep < INNER - 1:
            lowers = [ahead(v, 1) for v in lowers]
    return uppers, lowers


def mix_tiles(uppers, lowers, turns, lower_wanted):
    uppers, lowers = turn_tiles(uppers, lowers, turns[:-1])
    c, s = turns[-1]
    from_u, from_l = jnp.where(lower_wanted, s, c), jnp.where(lower_wanted, c, -s)
    return [from_u * u + from_l * v for u, v in zip(uppers, lowers)]


def sides(place, tables):
    return place == 0, place == tables - 2


def product_sums(load, height, pairs):
    used = sorted({n for pair in pairs for n in pair})
    totals = {}
    for d in range(REACH + 1):
        kept = [(x, y) for x, y in pairs if d or x <= y or (y, x) not in pairs]
        for start in range(0, height, TILE):
            now = {n: load(n, slice(start, start + TILE)) for n in used}
            then = {n: ahead(v, -d) for n, v in now.items()}
            for x, y in kept:
                term = now[x] * then[y]
                totals[x, y, d] = term if start == 0 else totals[x, y, d] + term
    for x, y in pairs:
        if (x, y, 0) not in totals:
            totals[x, y, 0] = totals[y, x, 0]
    return {key: jnp.sum(total, axis=0, keepdims=True) for key, total in totals.items()}


def put_sums(out_ref, sums, pairs, slot_of):
    for x, y in pairs:
        slot = slot_of(x, y)
        for half in range(2):
            columns = slice(half * (B // 2), (half + 1) * (B // 2))
            for d in range(REACH + 1):
                out_ref[2 * slot + half, d : d + 1, :] = sums[x, y, d][:, columns]


def lags(place, tables):
    odd = place % 2 == 1
    return odd | (place == 0), jnp.logical_not(odd | (place == tables - 2))


def held_bands_kernel(tables, keep_ref, send_ref, late_ref, out_ref):
    lag = lags(lax.axis_index("pair"), tables)
    out_ref[...] = jnp.zeros_like(out_ref)
    height = keep_ref.shape[0]
    for start in range(0, height, TILE):
        rows = slice(start, start + TILE)
        for n, ref in enumerate((keep_ref, send_ref)):
            value = ref[rows, :]
            late_ref[rows, n * B : (n + 1) * B] = jnp.where(lag[n], ahead(value, -LAG), value)

    def load(n, rows):
        return late_ref[rows, n * B : (n + 1) * B]

    pairs = [(x, y) for x in range(2) for y in range(2)]
    put_sums(out_ref, product_sums(load, height, pairs), pairs, lambda x, y: 2 * x + y)


def moved_bands_kernel(tables, late_ref, held_ref, come_ref, next_ref, lined_ref, out_ref):
    place = lax.axis_index("pair")
    odd = place % 2
    lower_sent = ring_before(place, tables) % 2
    own, other = 2 * odd, 2 - 2 * odd
    at = [own + 1 - odd, other + lower_sent, own + odd, other + 1 - lower_sent]
    lag = lags(place, tables)
    out_ref[...] = jnp.zeros_like(out_ref)
    height = come_ref.shape[0]
    columns = [pl.ds(pl.multiple_of(n * B, B), B) for n in at]
    for start in range(0, height, TILE):
        rows = slice(start, start + TILE)
        for n in range(2):
            lined_ref[rows, columns[n]] = late_ref[rows, n * B : (n + 1) * B]
        for n, ref in enumerate((come_ref, next_ref)):
            value = ref[rows, :]
            lined_ref[rows, columns[2 + n]] = jnp.where(lag[n], ahead(value, -LAG), value)

    def load(n, rows):
        return lined_ref[rows, columns[n]]

    def slot_of(x, y):
        return 4 * at[x] + at[y]

    pairs = [(x, y) for x, y in ALL_PAIRS if x > 1 or y > 1]
    put_sums(out_ref, product_sums(load, height, pairs), pairs, slot_of)
    for x in range(2):
        for y in range(2):
            for half in range(2):
                out_ref[2 * slot_of(x, y) + half] = held_ref[2 * (2 * x + y) + half]


def total_kernel(peers, parts_ref, out_ref):
    share = parts_ref.shape[0] // peers
    for part in range(share):
        total = parts_ref[part]
        for peer in range(1, peers):
            total = total + parts_ref[peer * share + part]
        for peer in range(peers):
            out_ref[peer * share + part] = total


def rotate_kernel(tables, sums_ref, lined_ref, keep_out, send_out):
    place = lax.axis_index("pair")
    left_lower, right_upper = sides(place, tables)

    def bands(x, y):
        slot = 4 * x + y
        return jnp.concatenate([sums_ref[2 * slot], sums_ref[2 * slot + 1]], axis=1)

    pairs = {
        (a, b): [bands(2 * a + x, 2 * b + y) for x in range(2) for y in range(2)]
        for a in range(2)
        for b in range(2)
    }
    (left_turns, right_turns), pairs = solve(pairs)
    uu, _, _, ll = pairs[0, 0]
    new_uu = jnp.where(left_lower, ll, uu)
    uu, _, _, ll = pairs[1, 1]
    new_ll = jnp.where(right_upper, uu, ll)
    uu, ul, lu, ll = pairs[0, 1]
    new_ul = jnp.where(
        left_lower, jnp.where(right_upper, lu, ll), jnp.where(right_upper, uu, ul)
    )
    uu, ul, lu, ll = pairs[1, 0]
    new_lu = jnp.where(
        left_lower, jnp.where(right_upper, ul, ll), jnp.where(right_upper, uu, lu)
    )
    (last_turns,), _ = solve({(0, 0): [new_uu, new_ul, new_lu, new_ll]})
    upper_sent = sends_upper(place ^ 1)
    height = keep_out.shape[0]
    groups = [
        [slice(r, r + TILE) for r in range(start, min(start + GROUP * TILE, height), TILE)]
        for start in range(0, height, GROUP * TILE)
    ]
    for n, out_ref, turns, lower_wanted in (
        (0, keep_out, left_turns, left_lower),
        (2, send_out, right_turns, jnp.logical_not(right_upper)),
    ):
        for group in groups:
            uppers = [lined_ref[rows, n * B : (n + 1) * B] for rows in group]
            lowers = [lined_ref[rows, (n + 1) * B : (n + 2) * B] for rows in group]
            for rows, value in zip(group, mix_tiles(uppers, lowers, turns, lower_wanted)):
                out_ref[rows, :] = value
    for group in groups:
        uppers = [keep_out[rows, :] for rows in group]
        lowers = [send_out[rows, :] for rows in group]
        uppers, lowers = turn_tiles(uppers, lowers, last_turns)
        for rows, upper, lower in zip(group, uppers, lowers):
            lower = ahead(lower, -LAG)
            keep_out[rows, :] = jnp.where(upper_sent, lower, upper)
            send_out[rows, :] = jnp.where(upper_sent, upper, lower)


def store_half(block_ref, out_ref, sem, upper):
    start = jnp.where(upper, 0, B)
    columns = pl.ds(pl.multiple_of(start, B), B)
    copy = pltpu.make_async_copy(block_ref, out_ref.at[:, columns], sem)
    copy.start()
    copy.wait()


def keep_kernel(keep_ref, out_ref, sem):
    store_half(keep_ref, out_ref, sem, lax.axis_index("pair") % 2 == 1)


def finish_kernel(half_ref, come_ref, out_ref, sem):
    store_half(come_ref, out_ref, sem, lax.axis_index("pair") % 2 == 0)


def line_seats(place, tables):
    odd = place % 2 == 1
    before = ring_before(place, tables)
    left, right = jnp.where(odd, before, place), jnp.where(odd, place, before)
    return 2 * left, 2 * left + 1, 2 * right, 2 * right + 1


def wanted_kernel(tables, seating_ref, out_ref):
    place = lax.axis_index("pair")
    lane = lax.broadcasted_iota(jnp.int32, out_ref.shape, 1)
    out = jnp.zeros(out_ref.shape, jnp.int32)
    for n, seat in enumerate(line_seats(place, tables) + line_seats(place ^ 1, tables)):
        out = jnp.where(lane == n, seating_ref[seat], out)
    out_ref[...] = out


def split_kernel(matrix_ref, top_ref, bottom_ref):
    half = top_ref.shape[0]
    top_ref[...] = matrix_ref[:half, :]
    bottom_ref[...] = matrix_ref[half:, :]


def chips_away(block, tables):
    chips = tables // 2
    return (block // 4 - lax.axis_index("pair") // 2 + chips) % chips


def block_columns(block):
    return pl.ds(pl.multiple_of((block % 2) * B, B), B)


def copy_block(tables, block, chosen, put, gathered):
    away = chips_away(block, tables)
    columns = block_columns(block)
    half = gathered[0].shape[0]
    for n in range(len(gathered) // 2):
        distance = (0, 1, 3, 2)[n]

        @pl.when(chosen & (away == distance))
        def _():
            for part in range(2):
                ref = gathered[2 * n + part]
                for start in range(0, half, TILE):
                    rows = slice(part * half + start, part * half + start + TILE)
                    put(rows, ref[start : start + TILE, columns])


def pick_near_kernel(tables, wanted_ref, *rest):
    gathered, out_ref = rest[:-1], rest[-1]
    wanted = wanted_ref[...]
    for n in range(4):

        def put(rows, value, n=n):
            out_ref[rows, n * B : (n + 1) * B] = value

        copy_block(tables, wanted[0, 4 + n], True, put, gathered)


def pick_far_kernel(tables, wanted_ref, near_ref, top_ref, bottom_ref, out_ref):
    wanted = wanted_ref[...]
    half = top_ref.shape[0]
    for n in range(4):
        block = wanted[0, 4 + n]
        far = chips_away(block, tables) == 2
        columns = block_columns(block)
        at = slice(n * B, (n + 1) * B)
        for part, ref in enumerate((top_ref, bottom_ref)):
            for start in range(0, half, TILE):
                rows = slice(part * half + start, part * half + start + TILE)
                value = ref[start : start + TILE, columns]
                out_ref[rows, at] = jnp.where(far, value, near_ref[rows, at])


def is_here(block):
    return (block // 2) % 2 == lax.axis_index("pair") % 2


def is_late(n, tables):
    left_lower, right_upper = sides(lax.axis_index("pair"), tables)
    return left_lower if n < 2 else jnp.logical_not(right_upper)


def here_kernel(tables, wanted_ref, *rest):
    gathered, out_ref = rest[:-1], rest[-1]
    wanted = wanted_ref[...]
    for n in range(4):
        late = is_late(n, tables)

        def put(rows, value, n=n, late=late):
            out_ref[rows, n * B : (n + 1) * B] = jnp.where(late, ahead(value, -LAG), value)

        copy_block(tables, wanted[0, n], is_here(wanted[0, n]), put, gathered)


def seated_bands_kernel(tables, wanted_ref, here_ref, swap_ref, lined_ref, out_ref):
    wanted = wanted_ref[...]
    height = here_ref.shape[0]
    for n in range(4):
        here, late = is_here(wanted[0, n]), is_late(n, tables)
        columns = slice(n * B, (n + 1) * B)
        for start in range(0, height, TILE):
            rows = slice(start, start + TILE)
            value = swap_ref[rows, columns]
            value = jnp.where(late, ahead(value, -LAG), value)
            lined_ref[rows, columns] = jnp.where(here, here_ref[rows, columns], value)

    def load(n, rows):
        return lined_ref[rows, n * B : (n + 1) * B]

    out_ref[...] = jnp.zeros_like(out_ref)
    sums = product_sums(load, height, ALL_PAIRS)
    put_sums(out_ref, sums, ALL_PAIRS, lambda x, y: 4 * x + y)


VMEM = pl.BlockSpec(memory_space=pltpu.VMEM)
PARAMS = pltpu.CompilerParams(vmem_limit_bytes=32 * 1024 * 1024)


def call(kernel, out_shape, *args):
    outs = [VMEM] * len(out_shape) if isinstance(out_shape, list) else VMEM
    return pl.pallas_call(
        kernel,
        out_shape=out_shape,
        in_specs=[VMEM] * len(args),
        out_specs=outs,
        compiler_params=PARAMS,
    )(*args)


def shape_of(*sizes):
    return jax.ShapeDtypeStruct(sizes, jnp.float32)


def bind(kernel, size):
    def bound(*refs):
        return kernel(size, *refs)

    return bound


def local(matrix, seating):
    height = matrix.shape[0]
    peers = lax.axis_size("row")
    tables = lax.axis_size("pair")
    ring = ring_of(tables)
    hosts = [table ^ 1 for table in ring]
    forward = list(zip(hosts, hosts[1:] + hosts[:1]))
    backward = [(b, a) for a, b in forward]
    up = [(j, (j + 2) % tables) for j in range(tables)]
    down = [(b, a) for a, b in up]
    across = [(j, j ^ 1) for j in range(tables)]
    wanted = pl.pallas_call(
        bind(wanted_kernel, tables),
        out_shape=jax.ShapeDtypeStruct((1, B // 2), jnp.int32),
        in_specs=[pl.BlockSpec(memory_space=pltpu.SMEM)],
        out_specs=VMEM,
        compiler_params=PARAMS,
    )(seating)
    top, bottom = call(split_kernel, [shape_of(height // 2, 2 * B)] * 2, matrix)
    left_top = lax.ppermute(top, "pair", up)
    right_bottom = lax.ppermute(bottom, "pair", down)
    left_bottom = lax.ppermute(bottom, "pair", up)
    right_top = lax.ppermute(top, "pair", down)
    far_top = lax.ppermute(left_top, "pair", up)
    far_bottom = lax.ppermute(right_bottom, "pair", down)
    near = [wanted, top, bottom, right_top, right_bottom, left_top, left_bottom]
    far = [far_top, far_bottom]
    seated_shape = shape_of(height, 4 * B)
    swap = call(bind(pick_near_kernel, tables), seated_shape, *near)
    swap = call(bind(pick_far_kernel, tables), seated_shape, wanted, swap, *far)
    swap = lax.ppermute(swap, "pair", across)
    here = call(bind(here_kernel, tables), seated_shape, *near, *far)
    lined_shape = shape_of(height, 4 * B)
    spread_shape = shape_of(GROUPS, TILE, B // 2)
    block_shape = shape_of(height, B)
    for pair_of_steps in range(STEPS // 2):
        if pair_of_steps == 0:
            kernel = bind(seated_bands_kernel, tables)
            lined, sums = call(kernel, [lined_shape, spread_shape], wanted, here, swap)
        else:
            kernel = bind(moved_bands_kernel, tables)
            lined, sums = call(kernel, [lined_shape, spread_shape], *held)
        sums = lax.all_to_all(sums, "row", 0, 0, tiled=True)
        sums = call(bind(total_kernel, peers), spread_shape, sums)
        sums = lax.all_to_all(sums, "row", 0, 0, tiled=True)
        kernel = bind(rotate_kernel, tables)
        keep, send = call(kernel, [block_shape, block_shape], sums, lined)
        come = lax.ppermute(send, "pair", forward)
        if pair_of_steps < STEPS // 2 - 1:
            near = lax.ppermute(keep, "pair", backward)
            shapes = [shape_of(height, 2 * B), shape_of(TILE, TILE, B // 2)]
            late, local_sums = call(bind(held_bands_kernel, tables), shapes, keep, send)
            held = [late, local_sums, come, near]
    options = dict(
        out_shape=shape_of(height, 2 * B),
        out_specs=pl.BlockSpec(memory_space=pl.ANY),
        scratch_shapes=[pltpu.SemaphoreType.DMA(())],
        compiler_params=PARAMS,
    )
    half = pl.pallas_call(keep_kernel, in_specs=[VMEM], **options)(keep)
    specs = [pl.BlockSpec(memory_space=pl.ANY), VMEM]
    finish = pl.pallas_call(finish_kernel, in_specs=specs, input_output_aliases={0: 0}, **options)
    return finish(half, come)


def solution(mesh):
    in_specs = (P("row", "pair"), P())
    out_specs = P("row", "pair")
    return jax.shard_map(local, mesh=mesh, in_specs=in_specs, out_specs=out_specs, check_vma=False)
```
